256 devices in a mesh: span: 32 (over z, y_lo, core), mp: 4 (over x), phase: 2 (over y_hi).
Axes of the slice: x: 4, y: 4 (y_hi: 2, y_lo: 2; y = y_hi * 2 + y_lo), z: 8, core: 2. Of those that a mesh axis runs over, the one named last changes fastest.
Arguments:
- latents: bfloat16 [32768, 2560], P(('span', 'phase')), may hold values from -6 to 6
- w_qkv: bfloat16 [2560, 3, 1536], P(None, None, 'mp'), may hold values from -0.125 to 0.125
- w_out: bfloat16 [1536, 2560], P('mp'), may hold values from -0.15625 to 0.15625
- decay: float32 [32, 2, 12], P('span', None, 'mp'), may hold values from 0.4 to 0.999, as said below
- frame_ids: int32 [32, 1024], P('span'), may hold values from 0 to 15, never falling along the last dimension, each value on 1 to 256 neighbouring positions
- memory_mask: int32 [32, 17], P('span'), may hold values 0 or 1
Outputs:
- refined: bfloat16 [32768, 2560], P(('span', 'phase'), 'mp')
The draws below stay inside these ranges and needn't reach their ends.
Inputs may be any that keep to these rules, and one draw needn't show every extreme that they name: `frame_ids`: along each span's 1024 tokens the frame numbers never fall, and every frame from 0 on holds 1 to 256 tokens. `decay`: every entry lies strictly between 0 and 1.
All inputs are finite; a program needn't handle non-finite values. No bound on the sum of `memory_mask` on one device may be relied on, other than what follows from the above.
Results may differ from the reference program's by a relative error of at most 0.004.
Values may be sent and summed in bfloat16 or wider, within the bound.
No kernel may reach another device: no remote copies, remote signals or barrier semaphores. Data moves between devices by JAX's collectives and lax.ppermute only.
A program may use at most 128 MiB of HBM per device.

```python
import math
import jax
import jax.numpy as jnp
import numpy as np
from jax import lax

D = 2560
ATTENTION_HEADS = 12
HD = 128
WIN = 64
MEM = 256
ROWS = 512
SPANS = 32
SPLIT = 2
SPAN_HALVES = 64
SPAN_LEN = 1024
TOKENS = 32768
CWIN = 17
FRAMES = 16
FRAME_MOST = 256
HC = 1536
N_MP = 4


def draw_latents(key, part):
    key_shared, key_own = jax.random.split(key)
    shared = jax.random.normal(key_shared, (SPAN_LEN, D), jnp.float32)
    own = jax.random.normal(key_own, (SPANS, SPAN_LEN, D), jnp.float32)
    mixed = 0.75 * shared[None, :, :] + 0.65 * own
    mixed = jnp.clip(mixed, -6.0, 6.0)
    return mixed.reshape(TOKENS, D).astype(jnp.bfloat16)


def draw_decay(key, part):
    key_pick, key_spread, key_location, key_length, key_fast = jax.random.split(key, 5)
    slow_share = 5
    slow = jax.random.randint(key_pick, (ATTENTION_HEADS,), 0, 10) < slow_share
    spread = jax.random.uniform(key_spread, (SPAN_HALVES, ATTENTION_HEADS), jnp.float32, 0.5, 1.0)
    gradual_decay_rate = jnp.exp(-math.log(10.0) / (3.0 * SPAN_HALVES) * spread)
    surge_location = jax.random.randint(key_location, (2,), 0, SPAN_HALVES)
    token_location = jnp.arange(SPAN_HALVES)
    removed_mask = jnp.any(token_location[:, None] == surge_location[None, :], axis=1)
    surge_length = jax.random.uniform(key_length, (SPAN_HALVES, ATTENTION_HEADS), jnp.float32, 0.5, 0.8)
    gradual_decay_rate = jnp.where(removed_mask[:, None], gradual_decay_rate * surge_length, gradual_decay_rate)
    fast_rate = jax.random.uniform(key_fast, (SPAN_HALVES, ATTENTION_HEADS), jnp.float32, 0.55, 0.85)
    rate = jnp.where(slow[None, :], gradual_decay_rate, fast_rate)
    return rate.reshape(SPANS, SPLIT, ATTENTION_HEADS).astype(jnp.float32)


def with_ends(values, key, low, largest):
    longest = values.shape.index(max(values.shape))
    spots = []
    for shift in (0, 1):
        where = [jax.random.randint(jax.random.fold_in(key, axis), (), 0, length) for axis, length in enumerate(values.shape)]
        where[longest] = (where[longest] + shift) % values.shape[longest]
        spots.append(tuple(where))
    return values.at[spots[0]].set(low).at[spots[1]].set(largest)


def levels(own_key, dims, pieces, least, largest):
    def one(position, blocks):
        heights = jax.random.uniform(jax.random.fold_in(jax.random.fold_in(own_key, 6), position), (blocks,), jnp.float32, least / len(pieces), largest / len(pieces))
        return jnp.repeat(jnp.exp(heights), dims[position] // blocks).reshape((-1,) + (1,) * (len(dims) - position - 1))

    factor_of = one(*pieces[0])
    for cut in pieces[1:]:
        factor_of = factor_of * one(*cut)
    return factor_of


def length_profile(amount, total, limit, slope):
    loads = [(1 << 20) // math.isqrt(rank ** slope) + 1 for rank in range(2, amount + 1)]
    rest, holding = total - limit - (amount - 1), [1] * (amount - 1)
    while rest > 0:
        movable = [i for i in range(amount - 1) if holding[i] < limit]
        mass, budget = sum([loads[i] for i in movable]), rest
        for i in movable:
            more = min(limit - holding[i], max(1, budget * loads[i] // mass), rest)
            holding[i] = holding[i] + more
            rest = rest - more
    return np.array([limit] + holding)


def ragged_sizes(stream_key, count, total, most, skew):
    if count == 2:
        one = jax.random.randint(stream_key, (), max(1, total - most), min(most, total - 1) + 1)
        return jnp.stack([one, total - one])
    lengths = jnp.asarray(length_profile(count, total, most, skew), jnp.int32)
    couples = (count - 1) // 2
    source_of, sink = lengths[1:1 + 2 * couples:2], lengths[2:2 + 2 * couples:2]
    room = jnp.minimum(source_of - 1, most - sink)
    passed = jax.random.randint(jax.random.fold_in(stream_key, 1), (couples,), 0, 1 << 20) % (room + 1)
    lengths = lengths.at[1:1 + 2 * couples:2].set(source_of - passed).at[2:2 + 2 * couples:2].set(sink + passed)
    return lengths[jax.random.permutation(jax.random.fold_in(stream_key, 2), count)]


def bell_draw(key, shape, scale, bound, pieces=(), kind=jnp.bfloat16):
    gain = levels(key, shape, pieces, -0.22, 0.18) if pieces else 1.0
    drawn = jax.random.normal(key, shape, jnp.float32) * scale * gain
    return jnp.minimum(jnp.maximum(drawn, -bound), bound).astype(kind)


def setup_inputs(seed: int = 0) -> dict:
    splits = jax.random.split(jax.random.key(seed), 7)
    return {
        "latents": draw_latents(jax.random.fold_in(splits[6], 71), 0),
        "w_qkv": bell_draw(splits[1], (D, 3, HC), D ** -0.5, 0.125, ((2, 4),)),
        "w_out": bell_draw(splits[2], (HC, D), HC ** -0.5, 0.15625, ((0, 4),)),
        "decay": draw_decay(jax.random.fold_in(splits[6], 71), 0),
        "frame_ids": jax.vmap(lambda own: jnp.searchsorted(jnp.cumsum(ragged_sizes(own, FRAMES, SPAN_LEN, FRAME_MOST, 1)), jnp.arange(SPAN_LEN), side="right"))(jax.random.split(splits[4], SPANS)).reshape((SPANS, SPAN_LEN)).astype(jnp.int32),
        "memory_mask": with_ends((jax.random.randint(splits[5], (SPANS, CWIN), 0, 4) < 3).astype(jnp.int32), jax.random.fold_in(splits[5], 1), 0, 1),
    }


outside_frame = 1048576
epsilon = 1e-06

def head_normed(raw):
    count = raw.shape[0]
    grouped = raw.reshape(count, -1, HD)
    scaled = grouped * lax.rsqrt(lax.optimization_barrier(jnp.mean(grouped * grouped, axis=-1, keepdims=True)) + epsilon)
    return scaled.reshape(count, -1).astype(jnp.bfloat16)

def project_span(rows_in, w_qkv):
    mixed = jnp.dot(rows_in, w_qkv.reshape(D, 3 * HC), preferred_element_type=jnp.float32)
    return (head_normed(mixed[:, :HC]), head_normed(mixed[:, HC:2 * HC]), mixed[:, 2 * HC:].astype(jnp.bfloat16))

def window_attend(queries_pad, keys_ext, values_ext, frames_ext, memory_keys, memory_values, memory_open):
    total_rows, width = queries_pad.shape
    heads = width // HD
    count = total_rows // WIN
    score_scale = HD ** (-0.5)
    window_query = queries_pad.astype(jnp.float32).reshape(count, WIN, heads, HD)
    key_win = keys_ext.astype(jnp.float32).reshape(count, WIN, heads, HD)
    value_win = values_ext.astype(jnp.float32).reshape(count, WIN, heads, HD)
    memory_key_rows = memory_keys.astype(jnp.float32).reshape(MEM, heads, HD)
    memory_value_rows = memory_values.astype(jnp.float32).reshape(MEM, heads, HD)
    score_win = jnp.einsum('wqhd,wkhd->whqk', window_query, key_win) * score_scale
    memory_score = jnp.einsum('bntu,atu->btna', window_query, memory_key_rows) * score_scale
    frame_win = frames_ext.reshape(count, WIN)
    allowed = frame_win[:, None, None, :] <= frame_win[:, None, :, None]
    exp_win = jnp.where(allowed, jnp.exp(score_win), 0.0)
    exp_mem = jnp.where((memory_open == 1)[:, None, None, None], jnp.exp(memory_score), 0.0)
    denom = lax.optimization_barrier(jnp.sum(exp_win, axis=-1, keepdims=True)) + lax.optimization_barrier(jnp.sum(exp_mem, axis=-1, keepdims=True))
    weight_win = lax.optimization_barrier((exp_win / denom).astype(jnp.bfloat16))
    memory_weight = lax.optimization_barrier((exp_mem / denom).astype(jnp.bfloat16))
    refined_output = jnp.einsum('whqk,wkhd->wqhd', weight_win.astype(jnp.float32), value_win)
    refined_output = refined_output + jnp.einsum('bykl,lyp->bkyp', memory_weight.astype(jnp.float32), memory_value_rows)
    return refined_output.reshape(total_rows, width).astype(jnp.bfloat16)

def reference(latents, w_qkv, w_out, decay, frame_ids, memory_mask):
    spanned = latents.reshape(SPANS, SPAN_LEN, D)
    queries_all, keys_all, values_all = lax.map(lambda block: project_span(block, w_qkv), spanned)
    rates = jnp.repeat(decay.reshape(SPAN_HALVES, ATTENTION_HEADS), HD, axis=1)
    last_keys = keys_all.reshape(SPAN_HALVES, ROWS, HC)[:, ROWS - MEM:]
    last_values = values_all.reshape(SPAN_HALVES, ROWS, HC)[:, ROWS - MEM:]

    def carry_step(state, inputs):
        rate, tail_keys, tail_values = inputs
        new_keys = rate * state[0] + (1.0 - rate) * tail_keys.astype(jnp.float32)
        new_values = rate * state[1] + jnp.sqrt(1.0 - rate * rate) * tail_values.astype(jnp.float32)
        return ((new_keys, new_values), state)
    start = (jnp.zeros((MEM, HC), jnp.float32), jnp.zeros((MEM, HC), jnp.float32))
    unused, memories = lax.scan(carry_step, start, (rates, last_keys, last_values))
    memory_keys_all = memories[0].reshape(SPANS, SPLIT, MEM, HC)
    memory_values_all = memories[1].reshape(SPANS, SPLIT, MEM, HC)
    half_win = WIN // 2
    group_cols = HC // N_MP

    def finish_span(items):
        block, queries, keys, values, frames, opened, mem_keys, mem_values = items
        keys_pad = jnp.pad(keys, ((half_win, half_win), (0, 0)))
        values_pad = jnp.pad(values, ((half_win, half_win), (0, 0)))
        frames_pad = jnp.pad(frames, (half_win, half_win), constant_values=outside_frame)
        outputs = []
        for half in range(SPLIT):
            offset = half * ROWS
            queries_pad = jnp.pad(queries[offset:offset + ROWS], ((half_win, half_win), (0, 0)))
            window_start = half * (ROWS // WIN)
            memory_keys_b = lax.optimization_barrier(mem_keys[half].astype(jnp.bfloat16))
            memory_values_b = lax.optimization_barrier(mem_values[half].astype(jnp.bfloat16))
            attended = window_attend(queries_pad, keys_pad[offset:offset + ROWS + WIN], values_pad[offset:offset + ROWS + WIN], frames_pad[offset:offset + ROWS + WIN], memory_keys_b, memory_values_b, opened[window_start:window_start + ROWS // WIN + 1])[half_win:half_win + ROWS]
            total = block[offset:offset + ROWS].astype(jnp.float32)
            for group in range(N_MP):
                lower = group * group_cols
                partial_sum = jnp.dot(attended[:, lower:lower + group_cols], w_out[lower:lower + group_cols], preferred_element_type=jnp.float32).astype(jnp.bfloat16)
                partial_sum = lax.optimization_barrier(partial_sum)
                total = total + partial_sum.astype(jnp.float32)
            outputs.append(total.astype(jnp.bfloat16))
        return jnp.concatenate(outputs, axis=0)
    refined = lax.map(finish_span, (spanned, queries_all, keys_all, values_all, frame_ids, memory_mask, memory_keys_all, memory_values_all))
    return refined.reshape(TOKENS, D)
```

```python
import functools

import jax
import jax.numpy as jnp
from jax import lax
from jax.experimental import pallas as pl
from jax.experimental.pallas import tpu as pltpu
from jax.sharding import Mesh
from jax.sharding import PartitionSpec as P

HD = 128
WIN = 64
HALF_WIN = 32
MEM = 256
ROWS = 512
EXT = ROWS + WIN
HEADS = 3
COLS = HEADS * HD
PARTS = 8
PART = MEM // PARTS
PAYLOAD = 2 * PART + 16
DEPTH = 512
BLOCK = 192
SPAN = ("z", "y", "core")
PLANE = ("y", "core", "phase")

outside_frame = 1048576
epsilon = 1e-06
F32 = jnp.float32
BF16 = jnp.bfloat16
SCALE2 = HD ** (-0.5) * 1.4426950408889634


def shape(dims, dtype):
    return jax.ShapeDtypeStruct(dims, dtype)


def normed(x):
    heads = []
    for h in range(HEADS):
        part = x[:, h * HD : (h + 1) * HD]
        square = jnp.mean(part * part, axis=-1, keepdims=True)
        heads.append(part * lax.rsqrt(square + epsilon))
    return jnp.concatenate(heads, axis=1).astype(BF16)


def pieces_of(row):
    full = jnp.broadcast_to(row, (16, COLS))
    high = full.astype(BF16).astype(F32)
    middle = (full - high).astype(BF16).astype(F32)
    low = full - high - middle
    at = lax.broadcasted_iota(jnp.int32, (16, COLS), 0)
    return jnp.where(at == 0, high, jnp.where(at == 1, middle, jnp.where(at == 2, low, 0.0))).astype(BF16)


def row_of(pieces):
    wide = pieces.astype(F32)
    return wide[0:1] + wide[1:2] + wide[2:3]


def tail_kernel(phase, decay, lat, wk, wv, out, acc):
    k = pl.program_id(0)

    @pl.when(k == 0)
    def _():
        acc[...] = jnp.zeros_like(acc)

    x = lat[...]
    acc[:, :COLS] += jnp.dot(x, wk[0], preferred_element_type=F32)
    acc[:, COLS:] += jnp.dot(x, wv[0], preferred_element_type=F32)

    @pl.when(k == pl.num_programs(0) - 1)
    def _():
        keys = normed(acc[:, :COLS])
        values = acc[:, COLS:].astype(BF16)
        first = phase[0] == 0
        rates = [jnp.where(first, decay[0, h], decay[1, h]) for h in range(HEADS)]
        lane = lax.broadcasted_iota(jnp.int32, (1, COLS), 1)
        row = jnp.where(lane < HD, rates[0], jnp.where(lane < 2 * HD, rates[1], rates[2]))
        tile = pieces_of(row)
        for d in range(PARTS):
            out[d, :PART] = keys[d * PART : (d + 1) * PART]
            out[d, PART : 2 * PART] = values[d * PART : (d + 1) * PART]
            out[d, 2 * PART :] = tile


def tails(phase, decay, latents, w3):
    depth = latents.shape[1]
    smem = pl.BlockSpec(memory_space=pltpu.SMEM)
    return pl.pallas_call(
        tail_kernel,
        grid=(depth // DEPTH,),
        out_shape=shape((PARTS, PAYLOAD, COLS), BF16),
        in_specs=[
            smem,
            smem,
            pl.BlockSpec((MEM, DEPTH), lambda k: (1, k)),
            pl.BlockSpec((1, DEPTH, COLS), lambda k: (1, k, 0)),
            pl.BlockSpec((1, DEPTH, COLS), lambda k: (2, k, 0)),
        ],
        out_specs=pl.BlockSpec((PARTS, PAYLOAD, COLS), lambda k: (0, 0, 0)),
        scratch_shapes=[pltpu.VMEM((MEM, 2 * COLS), F32)],
        cost_estimate=pl.CostEstimate(flops=2 * MEM * depth * 2 * COLS, bytes_accessed=5500000, transcendentals=0),
        name="tail_projection",
    )(phase, decay, latents, w3, w3)


def rest_kernel(phase, lat, wq, wk, wv, tail, q_out, kv_out, halo, accq, acc):
    k = pl.program_id(0)

    @pl.when(k == 0)
    def _():
        accq[...] = jnp.zeros_like(accq)
        acc[...] = jnp.zeros_like(acc)

    accq[...] += jnp.dot(lat[...], wq[0], preferred_element_type=F32)
    x = lat[:MEM]
    acc[:, :COLS] += jnp.dot(x, wk[0], preferred_element_type=F32)
    acc[:, COLS:] += jnp.dot(x, wv[0], preferred_element_type=F32)

    @pl.when(k == pl.num_programs(0) - 1)
    def _():
        q_out[...] = normed(accq[...])
        keys = normed(acc[:, :COLS])
        values = acc[:, COLS:].astype(BF16)
        kv_out[:, :COLS] = keys
        kv_out[:, COLS:] = values
        first = phase[0] == 0
        halo[:PART] = jnp.where(first, tail[0, :PART], keys[:PART])
        halo[PART:] = jnp.where(first, tail[0, PART : 2 * PART], values[:PART])


def rest(phase, latents, w3, payload):
    depth = latents.shape[1]
    smem = pl.BlockSpec(memory_space=pltpu.SMEM)
    weight = [pl.BlockSpec((1, DEPTH, COLS), lambda k, j=j: (j, k, 0)) for j in range(3)]
    return pl.pallas_call(
        rest_kernel,
        grid=(depth // DEPTH,),
        out_shape=(shape((ROWS, COLS), BF16), shape((MEM, 2 * COLS), BF16), shape((2 * PART, COLS), BF16)),
        in_specs=[
            smem,
            pl.BlockSpec((ROWS, DEPTH), lambda k: (0, k)),
            *weight,
            pl.BlockSpec((1, PAYLOAD, COLS), lambda k: (PARTS - 1, 0, 0)),
        ],
        out_specs=(
            pl.BlockSpec((ROWS, COLS), lambda k: (0, 0)),
            pl.BlockSpec((MEM, 2 * COLS), lambda k: (0, 0)),
            pl.BlockSpec((2 * PART, COLS), lambda k: (0, 0)),
        ),
        scratch_shapes=[pltpu.VMEM((ROWS, COLS), F32), pltpu.VMEM((MEM, 2 * COLS), F32)],
        cost_estimate=pl.CostEstimate(flops=4 * ROWS * depth * COLS, bytes_accessed=9000000, transcendentals=0),
        name="rest_projection",
    )(phase, latents, w3, w3, w3, payload)


def vmem_call(kernel, outs, name, flops, args, smem=0, scratch=()):
    specs = [pl.BlockSpec(memory_space=pltpu.SMEM)] * smem
    specs += [pl.BlockSpec(memory_space=pltpu.VMEM)] * (len(args) - smem)
    single = not isinstance(outs, tuple)
    out_spec = pl.BlockSpec(memory_space=pltpu.VMEM)
    nbytes = sum(a.size * a.dtype.itemsize for a in args)
    return pl.pallas_call(
        kernel,
        out_shape=outs,
        in_specs=specs,
        out_specs=out_spec if single else tuple(out_spec for _ in outs),
        scratch_shapes=list(scratch),
        cost_estimate=pl.CostEstimate(flops=flops, bytes_accessed=nbytes, transcendentals=0),
        compiler_params=pltpu.CompilerParams(vmem_limit_bytes=32 * 1024 * 1024),
        name=name,
    )(*args)


def window_kernel(q, head_rows, tail_rows, halo, frame_row, frame_column, top, bottom, qx, kx, vx):
    edge = jnp.zeros((HALF_WIN, COLS), BF16)
    qx[:HALF_WIN] = edge
    qx[HALF_WIN + ROWS :] = edge
    qx[HALF_WIN : HALF_WIN + ROWS] = q[...]
    for ext, columns, rows in ((kx, slice(0, COLS), slice(0, PART)), (vx, slice(COLS, 2 * COLS), slice(PART, 2 * PART))):
        ext[:HALF_WIN] = halo[rows]
        ext[HALF_WIN + ROWS :] = halo[rows]
        ext[HALF_WIN : HALF_WIN + MEM] = head_rows[:, columns]
        for d in range(PARTS):
            at = HALF_WIN + MEM + d * PART
            ext[at : at + PART] = tail_rows[d, rows]
    ones = jnp.ones((BLOCK, HD), BF16)
    window_a = lax.broadcasted_iota(jnp.int32, (BLOCK, BLOCK), 0) // WIN
    window_b = lax.broadcasted_iota(jnp.int32, (BLOCK, BLOCK), 1) // WIN
    for b in range(EXT // BLOCK):
        rows = slice(b * BLOCK, (b + 1) * BLOCK)
        allowed = (window_a == window_b) & (frame_row[b] <= frame_column[rows, :1])
        low, high = max(b * BLOCK, HALF_WIN), min((b + 1) * BLOCK, HALF_WIN + ROWS)
        for h in range(HEADS):
            c = slice(h * HD, (h + 1) * HD)
            score = lax.dot_general(qx[rows, c], kx[rows, c], (((1,), (1,)), ((), ())), preferred_element_type=F32)
            weight = jnp.where(allowed, jnp.exp2(score * SCALE2), 0.0).astype(BF16)
            both = jnp.concatenate([vx[rows, c], ones], axis=1)
            result = jnp.dot(weight, both, preferred_element_type=F32)
            cut = result[low - b * BLOCK : high - b * BLOCK]
            top[low - HALF_WIN : high - HALF_WIN, c] = cut[:, :HD]
            bottom[low - HALF_WIN : high - HALF_WIN, c] = cut[:, HD:]


def coefficients(rate):
    return 1.0 - rate, jnp.sqrt(1.0 - rate * rate)


def pack(out, state, row):
    out[: 2 * PART] = state.astype(BF16)
    out[2 * PART :] = pieces_of(row)


def keep(out, state, row):
    out[: 2 * PART] = state
    out[2 * PART :] = jnp.broadcast_to(row, (8, COLS))


def plane_step(keys, values, rate, tail_keys, tail_values):
    for_keys, for_values = coefficients(rate)
    return (
        rate * keys + for_keys * tail_keys.astype(F32),
        rate * values + for_values * tail_values.astype(F32),
    )


def plane_kernel(arrived, state, payload):
    keys = values = jnp.zeros((PART, COLS), F32)
    total = jnp.ones((1, COLS), F32)
    for i in range(PARTS):
        rate = row_of(arrived[i, 2 * PART :])
        keys, values = plane_step(keys, values, rate, arrived[i, :PART], arrived[i, PART : 2 * PART])
        total = total * rate
    both = jnp.concatenate([keys, values], axis=0)
    keep(state, both, total)
    pack(payload, both, total)


def first_kernel(own, got, before, payload):
    entering, rate = got[: 2 * PART].astype(F32), row_of(got[2 * PART :])
    keep(before, entering, rate)
    own_rate = own[2 * PART : 2 * PART + 1]
    pack(payload, own[: 2 * PART] + own_rate * entering, own_rate * rate)


def next_kernel(own, earlier, got, before, payload):
    rate = earlier[2 * PART : 2 * PART + 1]
    entering = earlier[: 2 * PART] + rate * got[: 2 * PART].astype(F32)
    rate = rate * row_of(got[2 * PART :])
    keep(before, entering, rate)
    own_rate = own[2 * PART : 2 * PART + 1]
    pack(payload, own[: 2 * PART] + own_rate * entering, own_rate * rate)


def memory_kernel(earlier, got, arrived, out):
    rate = earlier[2 * PART : 2 * PART + 1]
    entering = earlier[: 2 * PART] + rate * got[: 2 * PART].astype(F32)
    keys, values = entering[:PART], entering[PART:]
    for i in range(PARTS):
        out[i, :PART] = keys.astype(BF16)
        out[i, PART:] = values.astype(BF16)
        if i < PARTS - 1:
            rate = row_of(arrived[i, 2 * PART :])
            keys, values = plane_step(keys, values, rate, arrived[i, :PART], arrived[i, PART : 2 * PART])


def attend_kernel(phase, opened, q, memory, top, bottom, out):
    start = phase[0] * (ROWS // WIN)
    row = lax.broadcasted_iota(jnp.int32, (ROWS, HD), 0)
    window = (row + HALF_WIN) // WIN
    is_open = jnp.zeros((ROWS, HD), F32)
    for w in range(ROWS // WIN + 1):
        flag = jnp.where(opened[0, start + w] == 1, 1.0, 0.0)
        is_open = jnp.where(window == w, flag, is_open)
    ones = jnp.ones((MEM, HD), BF16)
    for h in range(HEADS):
        c = slice(h * HD, (h + 1) * HD)
        keys = memory[:, :PART, c].reshape(MEM, HD)
        values = memory[:, PART:, c].reshape(MEM, HD)
        score = lax.dot_general(q[:, c], keys, (((1,), (1,)), ((), ())), preferred_element_type=F32)
        weight = jnp.exp2(score * SCALE2).astype(BF16)
        result = jnp.dot(weight, jnp.concatenate([values, ones], axis=1), preferred_element_type=F32)
        above = top[:, c] + is_open * result[:, :HD]
        below = bottom[:, c] + is_open * result[:, HD:]
        out[:, c] = (above / below).astype(BF16)


def final_kernel(column, lat, *refs):
    out = refs[-1]
    attended, weights = refs[:4], refs[4:8]
    total = lat[...].astype(F32)
    for a, w in zip(attended, weights):
        total = total + jnp.dot(a[...], w[...], preferred_element_type=F32).astype(BF16).astype(F32)
    out[...] = total.astype(BF16)


def final(column, latents, attended, weights):
    share = weights[0].shape[1]
    rows = 256
    whole = pl.BlockSpec((COLS, share), lambda i, col: (0, 0))
    return pl.pallas_call(
        final_kernel,
        grid_spec=pltpu.PrefetchScalarGridSpec(
            num_scalar_prefetch=1,
            grid=(ROWS // rows,),
            in_specs=[pl.BlockSpec((rows, share), lambda i, col: (i, col[0]))]
            + [pl.BlockSpec((rows, COLS), lambda i, col: (i, 0))] * 4
            + [whole] * 4,
            out_specs=pl.BlockSpec((rows, share), lambda i, col: (i, 0)),
        ),
        out_shape=shape((ROWS, share), BF16),
        cost_estimate=pl.CostEstimate(flops=2 * ROWS * 4 * COLS * share, bytes_accessed=4000000, transcendentals=0),
        name="output_projection",
    )(column, latents, *attended, *weights)


def moved(x, axis, by, wrap=True):
    size = lax.axis_size(axis)
    pairs = [(i, (i + by) % size) for i in range(size) if wrap or 0 <= i + by < size]
    return lax.ppermute(x, axis, pairs)


def local(latents, w_qkv, w_out, decay, frame_ids, memory_mask):
    phase = lax.axis_index("phase")
    mp = lax.axis_index("mp")
    phase_ref = phase.reshape(1).astype(jnp.int32)
    w3 = jnp.transpose(w_qkv, (1, 0, 2))

    payload = tails(phase_ref, decay[0], latents, w3)
    arrived = lax.all_to_all(payload, PLANE, 0, 0, tiled=True)

    queries, head_rows, halo = rest(phase_ref, latents, w3, payload)
    halo = lax.ppermute(halo, "phase", [(0, 1), (1, 0)])

    share = w_out.shape[1] // 4
    offsets = (0, 1, -1, 2)
    weights = []
    for by in offsets:
        piece = lax.dynamic_slice_in_dim(w_out, (mp + by) % 4 * share, share, 1)
        weights.append(moved(piece, "mp", by) if by else piece)

    frames_pad = jnp.pad(frame_ids[0], (HALF_WIN, HALF_WIN), constant_values=outside_frame)
    frames = lax.dynamic_slice_in_dim(frames_pad, phase * ROWS, EXT)
    frame_row = frames.reshape(EXT // BLOCK, 1, BLOCK)
    frame_column = jnp.broadcast_to(frames[:, None], (EXT, HD))
    top, bottom = vmem_call(
        window_kernel,
        (shape((ROWS, COLS), F32), shape((ROWS, COLS), F32)),
        "window_attention",
        4 * EXT * BLOCK * COLS * 2,
        (queries, head_rows, payload, halo, frame_row, frame_column),
        scratch=[pltpu.VMEM((EXT, COLS), BF16)] * 3,
    )

    wide = shape((2 * PART + 8, COLS), F32)
    packed = shape((PAYLOAD, COLS), BF16)
    own, sent = vmem_call(plane_kernel, (wide, packed), "plane_total", 1000000, (arrived,))
    got = moved(sent, "z", 1, wrap=False)
    before, sent = vmem_call(first_kernel, (wide, packed), "before_1", 100000, (own, got))
    got = moved(sent, "z", 2, wrap=False)
    before, sent = vmem_call(next_kernel, (wide, packed), "before_3", 100000, (own, before, got))
    got = moved(sent, "z", 4, wrap=False)
    memory = vmem_call(
        memory_kernel, shape((PARTS, 2 * PART, COLS), BF16), "section_memory", 1000000, (before, got, arrived)
    )
    memory = lax.all_to_all(memory, PLANE, 0, 0, tiled=True)

    attended = vmem_call(
        attend_kernel,
        shape((ROWS, COLS), BF16),
        "memory_attention",
        4 * ROWS * MEM * COLS * 2,
        (phase_ref, memory_mask, queries, memory, top, bottom),
        smem=2,
    )
    gathered = [moved(attended, "mp", by) if by else attended for by in offsets]
    return final(mp.reshape(1).astype(jnp.int32), latents, gathered, weights)


def solution(mesh):
    finer = Mesh(
        mesh.devices.reshape(8, 2, 2, mesh.shape["mp"], mesh.shape["phase"]),
        ("z", "y", "core", "mp", "phase"),
    )
    placed = (
        P((*SPAN, "phase"), None),
        P(None, None, "mp"),
        P("mp", None),
        P(SPAN, None, "mp"),
        P(SPAN, None),
        P(SPAN, None),
    )
    return jax.shard_map(
        local, mesh=finer, in_specs=placed, out_specs=P((*SPAN, "phase"), "mp"), check_vma=False
    )
```

```python
import functools

import jax
import jax.numpy as jnp
from jax import lax
from jax.experimental import pallas as pl
from jax.experimental.pallas import tpu as pltpu
from jax.sharding import Mesh
from jax.sharding import PartitionSpec as P

HD = 128
WIN = 64
HALF_WIN = 32
MEM = 256
ROWS = 512
EXT = ROWS + WIN
HEADS = 3
COLS = HEADS * HD
PARTS = 8
PART = MEM // PARTS
PAYLOAD = 2 * PART + 16
CHUNKS = 5
TAIL_LIMIT = 60 * 1024 * 1024
REST_LIMIT = 60 * 1024 * 1024
LIMIT = 32 * 1024 * 1024
BLOCK = 192
SPAN = ("z", "y", "core")
PLANE = ("y", "core", "phase")

outside_frame = 1048576
epsilon = 1e-06
F32 = jnp.float32
BF16 = jnp.bfloat16
SCALE2 = HD ** (-0.5) * 1.4426950408889634


def shape(dims, dtype):
    return jax.ShapeDtypeStruct(dims, dtype)


def normed(x):
    heads = []
    for h in range(HEADS):
        part = x[:, h * HD : (h + 1) * HD]
        square = jnp.mean(part * part, axis=-1, keepdims=True)
        heads.append(part * lax.rsqrt(square + epsilon))
    return jnp.concatenate(heads, axis=1).astype(BF16)


def pieces_of(row):
    full = jnp.broadcast_to(row, (16, COLS))
    high = full.astype(BF16).astype(F32)
    middle = (full - high).astype(BF16).astype(F32)
    low = full - high - middle
    at = lax.broadcasted_iota(jnp.int32, (16, COLS), 0)
    return jnp.where(at == 0, high, jnp.where(at == 1, middle, jnp.where(at == 2, low, 0.0))).astype(BF16)


def row_of(pieces):
    wide = pieces.astype(F32)
    return wide[0:1] + wide[1:2] + wide[2:3]


def tail_kernel(phase, decay, lat, w, out, tail, wkv, acc, sems):
    depth = lat.shape[1]
    step = depth // CHUNKS
    copies = []
    for k in range(CHUNKS):
        at = pl.ds(k * step, step)
        group = [
            pltpu.make_async_copy(lat.at[pl.ds(MEM, MEM), at], tail.at[:, at], sems.at[3 * k]),
            pltpu.make_async_copy(w.at[1, at], wkv.at[at, pl.ds(0, COLS)], sems.at[3 * k + 1]),
            pltpu.make_async_copy(w.at[2, at], wkv.at[at, pl.ds(COLS, COLS)], sems.at[3 * k + 2]),
        ]
        for copy in group:
            copy.start()
        copies.append(group)
    for k, group in enumerate(copies):
        for copy in group:
            copy.wait()
        at = slice(k * step, (k + 1) * step)
        part = jnp.dot(tail[:, at], wkv[at], preferred_element_type=F32)
        if k == 0:
            acc[...] = part
        else:
            acc[...] += part
    keys = normed(acc[:, :COLS])
    values = acc[:, COLS:].astype(BF16)
    first = phase[0] == 0
    rates = [jnp.where(first, decay[0, h], decay[1, h]) for h in range(HEADS)]
    lane = lax.broadcasted_iota(jnp.int32, (1, COLS), 1)
    row = jnp.where(lane < HD, rates[0], jnp.where(lane < 2 * HD, rates[1], rates[2]))
    tile = pieces_of(row)
    for d in range(PARTS):
        out[d, :PART] = keys[d * PART : (d + 1) * PART]
        out[d, PART : 2 * PART] = values[d * PART : (d + 1) * PART]
        out[d, 2 * PART :] = tile


def tails(phase, decay, latents, w3):
    depth = latents.shape[1]
    smem = pl.BlockSpec(memory_space=pltpu.SMEM)
    vmem = pl.BlockSpec(memory_space=pltpu.VMEM)
    hbm = pl.BlockSpec(memory_space=pl.ANY)
    return pl.pallas_call(
        tail_kernel,
        out_shape=shape((PARTS, PAYLOAD, COLS), BF16),
        in_specs=[smem, smem, hbm, hbm],
        out_specs=vmem,
        scratch_shapes=[
            pltpu.VMEM((MEM, depth), BF16),
            pltpu.VMEM((depth, 2 * COLS), BF16),
            pltpu.VMEM((MEM, 2 * COLS), F32),
            pltpu.SemaphoreType.DMA((3 * CHUNKS,)),
        ],
        cost_estimate=pl.CostEstimate(flops=2 * MEM * depth * 2 * COLS, bytes_accessed=5500000, transcendentals=0),
        compiler_params=pltpu.CompilerParams(vmem_limit_bytes=TAIL_LIMIT),
        name="tail_projection",
    )(phase, decay, latents, w3)


def rest_kernel(phase, lat, w, payload, q_out, kv_out, halo, rows, wkv, wq, sems):
    copies = [
        pltpu.make_async_copy(lat.at[pl.ds(0, MEM)], rows.at[pl.ds(0, MEM)], sems.at[0]),
        pltpu.make_async_copy(w.at[1], wkv.at[:, pl.ds(0, COLS)], sems.at[1]),
        pltpu.make_async_copy(w.at[2], wkv.at[:, pl.ds(COLS, COLS)], sems.at[2]),
        pltpu.make_async_copy(lat.at[pl.ds(MEM, MEM)], rows.at[pl.ds(MEM, MEM)], sems.at[3]),
        pltpu.make_async_copy(w.at[0], wq, sems.at[4]),
    ]
    for copy in copies:
        copy.start()
    copies[0].wait()
    copies[1].wait()
    keys = normed(jnp.dot(rows[:MEM], wkv[:, :COLS], preferred_element_type=F32))
    copies[2].wait()
    values = jnp.dot(rows[:MEM], wkv[:, COLS:], preferred_element_type=F32).astype(BF16)
    kv_out[:, :COLS] = keys
    kv_out[:, COLS:] = values
    first = phase[0] == 0
    halo[:PART] = jnp.where(first, payload[PARTS - 1, :PART], keys[:PART])
    halo[PART:] = jnp.where(first, payload[PARTS - 1, PART : 2 * PART], values[:PART])
    copies[3].wait()
    copies[4].wait()
    q_out[...] = normed(jnp.dot(rows[...], wq[...], preferred_element_type=F32))


def rest(phase, latents, w3, payload):
    depth = latents.shape[1]
    smem = pl.BlockSpec(memory_space=pltpu.SMEM)
    vmem = pl.BlockSpec(memory_space=pltpu.VMEM)
    hbm = pl.BlockSpec(memory_space=pl.ANY)
    return pl.pallas_call(
        rest_kernel,
        out_shape=(shape((ROWS, COLS), BF16), shape((MEM, 2 * COLS), BF16), shape((2 * PART, COLS), BF16)),
        in_specs=[smem, hbm, hbm, vmem],
        out_specs=(vmem, vmem, vmem),
        scratch_shapes=[
            pltpu.VMEM((ROWS, depth), BF16),
            pltpu.VMEM((depth, 2 * COLS), BF16),
            pltpu.VMEM((depth, COLS), BF16),
            pltpu.SemaphoreType.DMA((5,)),
        ],
        cost_estimate=pl.CostEstimate(flops=4 * ROWS * depth * COLS, bytes_accessed=9000000, transcendentals=0),
        compiler_params=pltpu.CompilerParams(vmem_limit_bytes=REST_LIMIT),
        name="rest_projection",
    )(phase, latents, w3, payload)


def vmem_call(kernel, outs, name, flops, args, smem=0, scratch=()):
    specs = [pl.BlockSpec(memory_space=pltpu.SMEM)] * smem
    specs += [pl.BlockSpec(memory_space=pltpu.VMEM)] * (len(args) - smem)
    single = not isinstance(outs, tuple)
    out_spec = pl.BlockSpec(memory_space=pltpu.VMEM)
    nbytes = sum(a.size * a.dtype.itemsize for a in args)
    return pl.pallas_call(
        kernel,
        out_shape=outs,
        in_specs=specs,
        out_specs=out_spec if single else tuple(out_spec for _ in outs),
        scratch_shapes=list(scratch),
        cost_estimate=pl.CostEstimate(flops=flops, bytes_accessed=nbytes, transcendentals=0),
        compiler_params=pltpu.CompilerParams(vmem_limit_bytes=LIMIT),
        name=name,
    )(*args)


def window_kernel(q, head_rows, tail_rows, halo, frame_row, frame_column, top, bottom, qx, kx, vx):
    edge = jnp.zeros((HALF_WIN, COLS), BF16)
    qx[:HALF_WIN] = edge
    qx[HALF_WIN + ROWS :] = edge
    qx[HALF_WIN : HALF_WIN + ROWS] = q[...]
    for ext, columns, rows in ((kx, slice(0, COLS), slice(0, PART)), (vx, slice(COLS, 2 * COLS), slice(PART, 2 * PART))):
        ext[:HALF_WIN] = halo[rows]
        ext[HALF_WIN + ROWS :] = halo[rows]
        ext[HALF_WIN : HALF_WIN + MEM] = head_rows[:, columns]
        for d in range(PARTS):
            at = HALF_WIN + MEM + d * PART
            ext[at : at + PART] = tail_rows[d, rows]
    ones = jnp.ones((BLOCK, HD), BF16)
    window_a = lax.broadcasted_iota(jnp.int32, (BLOCK, BLOCK), 0) // WIN
    window_b = lax.broadcasted_iota(jnp.int32, (BLOCK, BLOCK), 1) // WIN
    for b in range(EXT // BLOCK):
        rows = slice(b * BLOCK, (b + 1) * BLOCK)
        allowed = (window_a == window_b) & (frame_row[b] <= frame_column[rows, :1])
        low, high = max(b * BLOCK, HALF_WIN), min((b + 1) * BLOCK, HALF_WIN + ROWS)
        for h in range(HEADS):
            c = slice(h * HD, (h + 1) * HD)
            score = lax.dot_general(qx[rows, c], kx[rows, c], (((1,), (1,)), ((), ())), preferred_element_type=F32)
            weight = jnp.where(allowed, jnp.exp2(score * SCALE2), 0.0).astype(BF16)
            both = jnp.concatenate([vx[rows, c], ones], axis=1)
            result = jnp.dot(weight, both, preferred_element_type=F32)
            cut = result[low - b * BLOCK : high - b * BLOCK]
            top[low - HALF_WIN : high - HALF_WIN, c] = cut[:, :HD]
            bottom[low - HALF_WIN : high - HALF_WIN, c] = cut[:, HD:]


def coefficients(rate):
    return 1.0 - rate, jnp.sqrt(1.0 - rate * rate)


def pack(out, state, row):
    out[: 2 * PART] = state.astype(BF16)
    out[2 * PART :] = pieces_of(row)


def keep(out, state, row):
    out[: 2 * PART] = state
    out[2 * PART :] = jnp.broadcast_to(row, (8, COLS))


def plane_step(keys, values, rate, tail_keys, tail_values):
    for_keys, for_values = coefficients(rate)
    return (
        rate * keys + for_keys * tail_keys.astype(F32),
        rate * values + for_values * tail_values.astype(F32),
    )


def plane_kernel(arrived, state, payload):
    keys = values = jnp.zeros((PART, COLS), F32)
    total = jnp.ones((1, COLS), F32)
    for i in range(PARTS):
        rate = row_of(arrived[i, 2 * PART :])
        keys, values = plane_step(keys, values, rate, arrived[i, :PART], arrived[i, PART : 2 * PART])
        total = total * rate
    both = jnp.concatenate([keys, values], axis=0)
    keep(state, both, total)
    pack(payload, both, total)


def first_kernel(own, got, payload):
    entering, rate = got[: 2 * PART].astype(F32), row_of(got[2 * PART :])
    own_rate = own[2 * PART : 2 * PART + 1]
    pack(payload, own[: 2 * PART] + own_rate * entering, own_rate * rate)


def next_kernel(own, got_1, got_2, payload):
    rate = row_of(got_1[2 * PART :])
    entering = got_1[: 2 * PART].astype(F32) + rate * got_2[: 2 * PART].astype(F32)
    own_rate = own[2 * PART : 2 * PART + 1]
    payload[...] = (own[: 2 * PART] + own_rate * entering).astype(BF16)


def memory_kernel(got_1, got_2, got_4, arrived, out):
    near, middle = row_of(got_1[2 * PART :]), row_of(got_2[2 * PART :])
    far = got_2[: 2 * PART].astype(F32) + middle * got_4[...].astype(F32)
    entering = got_1[: 2 * PART].astype(F32) + near * far
    keys, values = entering[:PART], entering[PART:]
    for i in range(PARTS):
        out[i, :PART] = keys.astype(BF16)
        out[i, PART:] = values.astype(BF16)
        if i < PARTS - 1:
            rate = row_of(arrived[i, 2 * PART :])
            keys, values = plane_step(keys, values, rate, arrived[i, :PART], arrived[i, PART : 2 * PART])


def attend_kernel(base, phase, opened, q, memory, top, bottom, out):
    rows = out.shape[0]
    start = phase[0] * (ROWS // WIN)
    row = lax.broadcasted_iota(jnp.int32, (rows, HD), 0) + base
    window = (row + HALF_WIN) // WIN
    is_open = jnp.zeros((rows, HD), F32)
    for w in range((base + HALF_WIN) // WIN, (base + rows - 1 + HALF_WIN) // WIN + 1):
        flag = jnp.where(opened[0, start + w] == 1, 1.0, 0.0)
        is_open = jnp.where(window == w, flag, is_open)
    ones = jnp.ones((MEM, HD), BF16)
    at = slice(base, base + rows)
    for h in range(HEADS):
        c = slice(h * HD, (h + 1) * HD)
        keys = memory[:, :PART, c].reshape(MEM, HD)
        values = memory[:, PART:, c].reshape(MEM, HD)
        score = lax.dot_general(q[at, c], keys, (((1,), (1,)), ((), ())), preferred_element_type=F32)
        weight = jnp.exp2(score * SCALE2).astype(BF16)
        result = jnp.dot(weight, jnp.concatenate([values, ones], axis=1), preferred_element_type=F32)
        above = top[at, c] + is_open * result[:, :HD]
        below = bottom[at, c] + is_open * result[:, HD:]
        out[:, c] = (above / below).astype(BF16)


def final_kernel(column, lat, *refs):
    out = refs[-1]
    attended, weights = refs[:5], refs[5:9]
    total = lat[...].astype(F32)
    for a, w in zip(attended[:3], weights[:3]):
        total = total + jnp.dot(a[...], w[...], preferred_element_type=F32)
    far = jnp.concatenate([attended[3][...], attended[4][...]], axis=0)
    total = total + jnp.dot(far, weights[3][...], preferred_element_type=F32)
    out[...] = total.astype(BF16)


def final(r, column, latents, attended, weights, earlier=None):
    share = weights[0].shape[1]
    rows = attended[0].shape[0]
    vmem = pl.BlockSpec(memory_space=pltpu.VMEM)
    specs = [pl.BlockSpec((rows, share), lambda i, col: (r, col[0]))] + [vmem] * 9
    operands = [column, latents, *attended, *weights]
    aliases = {}
    if earlier is not None:
        specs.append(pl.BlockSpec(memory_space=pl.ANY))
        aliases = {len(operands): 0}
        operands.append(earlier)
    return pl.pallas_call(
        final_kernel,
        grid_spec=pltpu.PrefetchScalarGridSpec(
            num_scalar_prefetch=1,
            grid=(1,),
            in_specs=specs,
            out_specs=pl.BlockSpec((rows, share), lambda i, col: (r, 0)),
        ),
        out_shape=shape((ROWS, share), BF16),
        input_output_aliases=aliases,
        cost_estimate=pl.CostEstimate(flops=2 * rows * 4 * COLS * share, bytes_accessed=2000000, transcendentals=0),
        compiler_params=pltpu.CompilerParams(vmem_limit_bytes=LIMIT),
        name=f"output_projection_{r}",
    )(*operands)


def moved(x, axis, by, wrap=True):
    size = lax.axis_size(axis)
    pairs = [(i, (i + by) % size) for i in range(size) if wrap or 0 <= i + by < size]
    return lax.ppermute(x, axis, pairs)


def local(latents, w_qkv, w_out, decay, frame_ids, memory_mask):
    phase = lax.axis_index("phase")
    mp = lax.axis_index("mp")
    phase_ref = phase.reshape(1).astype(jnp.int32)
    w3 = jnp.transpose(w_qkv, (1, 0, 2))

    payload = tails(phase_ref, decay[0], latents, w3)
    arrived = lax.all_to_all(payload, PLANE, 0, 0, tiled=True)
    queries, head_rows, halo = rest(phase_ref, latents, w3, payload)
    arrived, queries = lax.optimization_barrier((arrived, queries))
    halo = lax.ppermute(halo, "phase", [(0, 1), (1, 0)])

    w_out, head_rows, frame_ids = lax.optimization_barrier((w_out, head_rows, frame_ids))
    share = w_out.shape[1] // 4
    offsets = (0, 1, -1, 2)
    weights = []
    for by in offsets:
        piece = lax.dynamic_slice_in_dim(w_out, ((mp + by) & 3) * share, share, 1)
        weights.append(moved(piece, "mp", by) if by else piece)

    frames_pad = jnp.pad(frame_ids[0], (HALF_WIN, HALF_WIN), constant_values=outside_frame)
    frames = lax.dynamic_slice_in_dim(frames_pad, phase * ROWS, EXT)
    frame_row = frames.reshape(EXT // BLOCK, 1, BLOCK)
    frame_column = jnp.broadcast_to(frames[:, None], (EXT, HD))
    top, bottom = vmem_call(
        window_kernel,
        (shape((ROWS, COLS), F32), shape((ROWS, COLS), F32)),
        "window_attention",
        4 * EXT * BLOCK * COLS * 2,
        (queries, head_rows, payload, halo, frame_row, frame_column),
        scratch=[pltpu.VMEM((EXT, COLS), BF16)] * 3,
    )

    wide = shape((2 * PART + 8, COLS), F32)
    packed = shape((PAYLOAD, COLS), BF16)
    plain = shape((2 * PART, COLS), BF16)
    plain_all = shape((PARTS, 2 * PART, COLS), BF16)
    own, sent = vmem_call(plane_kernel, (wide, packed), "plane_total", 1000000, (arrived,))
    got_1 = moved(sent, "z", 1, wrap=False)
    sent = vmem_call(first_kernel, packed, "through_1", 100000, (own, got_1))
    got_2 = moved(sent, "z", 2, wrap=False)
    sent = vmem_call(next_kernel, plain, "through_3", 100000, (own, got_1, got_2))
    got_4 = moved(sent, "z", 4, wrap=False)
    got_4, top, bottom, weights = lax.optimization_barrier((got_4, top, bottom, weights))
    memory = vmem_call(
        memory_kernel, plain_all, "section_memory", 1000000, (got_1, got_2, got_4, arrived)
    )
    memory = lax.all_to_all(memory, PLANE, 0, 0, tiled=True)

    pieces = []
    rows = ROWS // 2
    for r in range(2):
        pieces.append(
            vmem_call(
                functools.partial(attend_kernel, r * rows),
                shape((rows, COLS), BF16),
                f"memory_attention_{r}",
                4 * rows * MEM * COLS * 2,
                (phase_ref, memory_mask, queries, memory, top, bottom),
                smem=2,
            )
        )
    column = mp.reshape(1).astype(jnp.int32)
    near = [(moved(piece, "mp", 1), moved(piece, "mp", -1)) for piece in pieces]
    refined = None
    for r, (piece, (right, left)) in enumerate(zip(pieces, near)):
        far = (moved(right[: rows // 2], "mp", 1), moved(left[rows // 2 :], "mp", -1))
        refined = final(r, column, latents, (piece, right, left, *far), weights, refined)
    return refined


def solution(mesh):
    finer = Mesh(
        mesh.devices.reshape(8, 2, 2, mesh.shape["mp"], mesh.shape["phase"]),
        ("z", "y", "core", "mp", "phase"),
    )
    placed = (
        P((*SPAN, "phase"), None),
        P(None, None, "mp"),
        P("mp", None),
        P(SPAN, None, "mp"),
        P(SPAN, None),
        P(SPAN, None),
    )
    return jax.shard_map(
        local, mesh=finer, in_specs=placed, out_specs=P((*SPAN, "phase"), "mp"), check_vma=False
    )
```

```python
import functools

import jax
import jax.numpy as jnp
from jax import lax
from jax.experimental import pallas as pl
from jax.experimental.pallas import tpu as pltpu
from jax.sharding import Mesh
from jax.sharding import PartitionSpec as P

HD = 128
WIN = 64
HALF_WIN = 32
MEM = 256
ROWS = 512
EXT = ROWS + WIN
HEADS = 3
COLS = HEADS * HD
PARTS = 8
PART = MEM // PARTS
PAYLOAD = 2 * PART + 8
CHUNKS = 5
TAIL_LIMIT = 60 * 1024 * 1024
REST_LIMIT = 60 * 1024 * 1024
LIMIT = 32 * 1024 * 1024
BLOCK = 192
SPAN = ("z", "y", "core")
PLANE = ("y", "core", "phase")

outside_frame = 1048576
epsilon = 1e-06
F32 = jnp.float32
BF16 = jnp.bfloat16
SCALE2 = HD ** (-0.5) * 1.4426950408889634


def shape(dims, dtype):
    return jax.ShapeDtypeStruct(dims, dtype)


def normed(x):
    heads = []
    for h in range(HEADS):
        part = x[:, h * HD : (h + 1) * HD]
        square = jnp.mean(part * part, axis=-1, keepdims=True)
        heads.append(part * lax.rsqrt(square + epsilon))
    return jnp.concatenate(heads, axis=1).astype(BF16)


def pieces_of(row):
    full = jnp.broadcast_to(row, (8, COLS))
    high = full.astype(BF16).astype(F32)
    middle = (full - high).astype(BF16).astype(F32)
    low = full - high - middle
    at = lax.broadcasted_iota(jnp.int32, (8, COLS), 0)
    return jnp.where(at == 0, high, jnp.where(at == 1, middle, jnp.where(at == 2, low, 0.0))).astype(BF16)


def row_of(pieces):
    wide = pieces.astype(F32)
    return wide[0:1] + wide[1:2] + wide[2:3]


def tail_kernel(phase, decay, lat, w, out, tail, wkv, acc, sems):
    depth = lat.shape[1]
    step = depth // CHUNKS
    copies = []
    for k in range(CHUNKS):
        at = pl.ds(k * step, step)
        group = [
            pltpu.make_async_copy(lat.at[pl.ds(MEM, MEM), at], tail.at[:, at], sems.at[3 * k]),
            pltpu.make_async_copy(w.at[1, at], wkv.at[at, pl.ds(0, COLS)], sems.at[3 * k + 1]),
            pltpu.make_async_copy(w.at[2, at], wkv.at[at, pl.ds(COLS, COLS)], sems.at[3 * k + 2]),
        ]
        for copy in group:
            copy.start()
        copies.append(group)
    for k, group in enumerate(copies):
        for copy in group:
            copy.wait()
        at = slice(k * step, (k + 1) * step)
        part = jnp.dot(tail[:, at], wkv[at], preferred_element_type=F32)
        if k == 0:
            acc[...] = part
        else:
            acc[...] += part
    keys = normed(acc[:, :COLS])
    values = acc[:, COLS:].astype(BF16)
    first = phase[0] == 0
    rates = [jnp.where(first, decay[0, h], decay[1, h]) for h in range(HEADS)]
    lane = lax.broadcasted_iota(jnp.int32, (1, COLS), 1)
    row = jnp.where(lane < HD, rates[0], jnp.where(lane < 2 * HD, rates[1], rates[2]))
    tile = pieces_of(row)
    for d in range(PARTS):
        out[d, :PART] = keys[d * PART : (d + 1) * PART]
        out[d, PART : 2 * PART] = values[d * PART : (d + 1) * PART]
        out[d, 2 * PART :] = tile


def tails(phase, decay, latents, w3):
    depth = latents.shape[1]
    smem = pl.BlockSpec(memory_space=pltpu.SMEM)
    vmem = pl.BlockSpec(memory_space=pltpu.VMEM)
    hbm = pl.BlockSpec(memory_space=pl.ANY)
    return pl.pallas_call(
        tail_kernel,
        out_shape=shape((PARTS, PAYLOAD, COLS), BF16),
        in_specs=[smem, smem, hbm, hbm],
        out_specs=vmem,
        scratch_shapes=[
            pltpu.VMEM((MEM, depth), BF16),
            pltpu.VMEM((depth, 2 * COLS), BF16),
            pltpu.VMEM((MEM, 2 * COLS), F32),
            pltpu.SemaphoreType.DMA((3 * CHUNKS,)),
        ],
        cost_estimate=pl.CostEstimate(flops=2 * MEM * depth * 2 * COLS, bytes_accessed=5500000, transcendentals=0),
        compiler_params=pltpu.CompilerParams(vmem_limit_bytes=TAIL_LIMIT),
        name="tail_projection",
    )(phase, decay, latents, w3)


def call_on_hbm(kernel, outs, name, flops, nbytes, args, scratch):
    vmem = pl.BlockSpec(memory_space=pltpu.VMEM)
    hbm = pl.BlockSpec(memory_space=pl.ANY)
    single = not isinstance(outs, tuple)
    return pl.pallas_call(
        kernel,
        out_shape=outs,
        in_specs=[pl.BlockSpec(memory_space=pltpu.SMEM), hbm, hbm] + [vmem] * (len(args) - 3),
        out_specs=vmem if single else tuple(vmem for _ in outs),
        scratch_shapes=scratch,
        cost_estimate=pl.CostEstimate(flops=flops, bytes_accessed=nbytes, transcendentals=0),
        compiler_params=pltpu.CompilerParams(vmem_limit_bytes=REST_LIMIT),
        name=name,
    )(*args)


def head_kernel(which, after, lat, w, out, rows, part, sems):
    copies = [
        pltpu.make_async_copy(w.at[which], part, sems.at[0]),
        pltpu.make_async_copy(lat.at[pl.ds(0, MEM)], rows, sems.at[1]),
    ]
    for copy in copies:
        copy.start()
    for copy in copies:
        copy.wait()
    mixed = jnp.dot(rows[...], part[...], preferred_element_type=F32)
    out[...] = normed(mixed) if which == 1 else mixed.astype(BF16)


def heads(which, after, latents, w3):
    depth = latents.shape[1]
    return call_on_hbm(
        functools.partial(head_kernel, which),
        shape((MEM, COLS), BF16),
        f"head_projection_{which}",
        2 * MEM * depth * COLS,
        3300000,
        (after, latents, w3),
        [pltpu.VMEM((MEM, depth), BF16), pltpu.VMEM((depth, COLS), BF16), pltpu.SemaphoreType.DMA((2,))],
    )


def query_kernel(after, lat, w, out, rows, part, sems):
    copies = [
        pltpu.make_async_copy(w.at[0], part, sems.at[0]),
        pltpu.make_async_copy(lat.at[pl.ds(0, MEM)], rows.at[pl.ds(0, MEM)], sems.at[1]),
        pltpu.make_async_copy(lat.at[pl.ds(MEM, MEM)], rows.at[pl.ds(MEM, MEM)], sems.at[2]),
    ]
    for copy in copies:
        copy.start()
    copies[0].wait()
    for r in range(2):
        copies[1 + r].wait()
        at = slice(r * MEM, (r + 1) * MEM)
        out[at] = normed(jnp.dot(rows[at], part[...], preferred_element_type=F32))


def query(after, latents, w3):
    depth = latents.shape[1]
    return call_on_hbm(
        query_kernel,
        shape((ROWS, COLS), BF16),
        "query_projection",
        2 * ROWS * depth * COLS,
        4600000,
        (after, latents, w3),
        [pltpu.VMEM((ROWS, depth), BF16), pltpu.VMEM((depth, COLS), BF16), pltpu.SemaphoreType.DMA((3,))],
    )


def vmem_call(kernel, outs, name, flops, args, smem=0, scratch=()):
    specs = [pl.BlockSpec(memory_space=pltpu.SMEM)] * smem
    specs += [pl.BlockSpec(memory_space=pltpu.VMEM)] * (len(args) - smem)
    single = not isinstance(outs, tuple)
    out_spec = pl.BlockSpec(memory_space=pltpu.VMEM)
    nbytes = sum(a.size * a.dtype.itemsize for a in args)
    return pl.pallas_call(
        kernel,
        out_shape=outs,
        in_specs=specs,
        out_specs=out_spec if single else tuple(out_spec for _ in outs),
        scratch_shapes=list(scratch),
        cost_estimate=pl.CostEstimate(flops=flops, bytes_accessed=nbytes, transcendentals=0),
        compiler_params=pltpu.CompilerParams(vmem_limit_bytes=LIMIT),
        name=name,
    )(*args)


def window_kernel(q, head_keys, head_values, tail_rows, halo, frame_row, frame_column, top, bottom, qx, kx, vx):
    edge = jnp.zeros((HALF_WIN, COLS), BF16)
    qx[:HALF_WIN] = edge
    qx[HALF_WIN + ROWS :] = edge
    qx[HALF_WIN : HALF_WIN + ROWS] = q[...]
    for ext, head, rows in ((kx, head_keys, slice(0, PART)), (vx, head_values, slice(PART, 2 * PART))):
        ext[:HALF_WIN] = halo[rows]
        ext[HALF_WIN + ROWS :] = halo[rows]
        ext[HALF_WIN : HALF_WIN + MEM] = head[...]
        for d in range(PARTS):
            at = HALF_WIN + MEM + d * PART
            ext[at : at + PART] = tail_rows[d, rows]
    ones = jnp.ones((BLOCK, HD), BF16)
    window_a = lax.broadcasted_iota(jnp.int32, (BLOCK, BLOCK), 0) // WIN
    window_b = lax.broadcasted_iota(jnp.int32, (BLOCK, BLOCK), 1) // WIN
    for b in range(EXT // BLOCK):
        rows = slice(b * BLOCK, (b + 1) * BLOCK)
        allowed = (window_a == window_b) & (frame_row[b] <= frame_column[rows, :1])
        low, high = max(b * BLOCK, HALF_WIN), min((b + 1) * BLOCK, HALF_WIN + ROWS)
        for h in range(HEADS):
            c = slice(h * HD, (h + 1) * HD)
            score = lax.dot_general(qx[rows, c], kx[rows, c], (((1,), (1,)), ((), ())), preferred_element_type=F32)
            weight = jnp.where(allowed, jnp.exp2(score * SCALE2), 0.0).astype(BF16)
            both = jnp.concatenate([vx[rows, c], ones], axis=1)
            result = jnp.dot(weight, both, preferred_element_type=F32)
            cut = result[low - b * BLOCK : high - b * BLOCK]
            top[low - HALF_WIN : high - HALF_WIN, c] = cut[:, :HD]
            bottom[low - HALF_WIN : high - HALF_WIN, c] = cut[:, HD:]


def coefficients(rate):
    return 1.0 - rate, jnp.sqrt(1.0 - rate * rate)


def pack(out, state, row):
    out[: 2 * PART] = state.astype(BF16)
    out[2 * PART :] = pieces_of(row)


def keep(out, state, row):
    out[: 2 * PART] = state
    out[2 * PART :] = jnp.broadcast_to(row, (8, COLS))


def plane_step(keys, values, rate, tail_keys, tail_values):
    for_keys, for_values = coefficients(rate)
    return (
        rate * keys + for_keys * tail_keys.astype(F32),
        rate * values + for_values * tail_values.astype(F32),
    )


def plane_kernel(arrived, state, payload):
    keys = values = jnp.zeros((PART, COLS), F32)
    total = jnp.ones((1, COLS), F32)
    for i in range(PARTS):
        rate = row_of(arrived[i, 2 * PART :])
        keys, values = plane_step(keys, values, rate, arrived[i, :PART], arrived[i, PART : 2 * PART])
        total = total * rate
    both = jnp.concatenate([keys, values], axis=0)
    keep(state, both, total)
    pack(payload, both, total)


def joined(upper, mine, rate, got):
    other, other_rate = got[: 2 * PART].astype(F32), row_of(got[2 * PART :])
    return jnp.where(upper, mine + rate * other, other + other_rate * mine), rate * other_rate


def first_kernel(z, own, got_1, payload):
    total, rate = joined((z[0] & 1) == 1, own[: 2 * PART], own[2 * PART : 2 * PART + 1], got_1)
    pack(payload, total, rate)


def next_kernel(z, own, got_1, got_2, payload):
    total, rate = joined((z[0] & 1) == 1, own[: 2 * PART], own[2 * PART : 2 * PART + 1], got_1)
    total, rate = joined((z[0] & 2) == 2, total, rate, got_2)
    payload[...] = total.astype(BF16)


def memory_kernel(z, got_1, got_2, got_4, arrived, out):
    at_1, at_2, at_4 = (z[0] & 1) == 1, (z[0] & 2) == 2, (z[0] & 4) == 4
    entering = jnp.where(at_1, got_1[: 2 * PART].astype(F32), 0.0)
    rate = jnp.where(at_1, row_of(got_1[2 * PART :]), 1.0)
    entering = jnp.where(at_2, entering + rate * got_2[: 2 * PART].astype(F32), entering)
    rate = jnp.where(at_2, rate * row_of(got_2[2 * PART :]), rate)
    entering = jnp.where(at_4, entering + rate * got_4[...].astype(F32), entering)
    keys, values = entering[:PART], entering[PART:]
    for i in range(PARTS):
        out[i, :PART] = keys.astype(BF16)
        out[i, PART:] = values.astype(BF16)
        if i < PARTS - 1:
            rate = row_of(arrived[i, 2 * PART :])
            keys, values = plane_step(keys, values, rate, arrived[i, :PART], arrived[i, PART : 2 * PART])


def attend_kernel(base, phase, opened, q, memory, top, bottom, out):
    rows = out.shape[0]
    start = phase[0] * (ROWS // WIN)
    row = lax.broadcasted_iota(jnp.int32, (rows, HD), 0) + base
    window = (row + HALF_WIN) // WIN
    is_open = jnp.zeros((rows, HD), F32)
    for w in range((base + HALF_WIN) // WIN, (base + rows - 1 + HALF_WIN) // WIN + 1):
        flag = jnp.where(opened[0, start + w] == 1, 1.0, 0.0)
        is_open = jnp.where(window == w, flag, is_open)
    ones = jnp.ones((MEM, HD), BF16)
    at = slice(base, base + rows)
    for h in range(HEADS):
        c = slice(h * HD, (h + 1) * HD)
        keys = memory[:, :PART, c].reshape(MEM, HD)
        values = memory[:, PART:, c].reshape(MEM, HD)
        score = lax.dot_general(q[at, c], keys, (((1,), (1,)), ((), ())), preferred_element_type=F32)
        weight = jnp.exp2(score * SCALE2).astype(BF16)
        result = jnp.dot(weight, jnp.concatenate([values, ones], axis=1), preferred_element_type=F32)
        above = top[at, c] + is_open * result[:, :HD]
        below = bottom[at, c] + is_open * result[:, HD:]
        out[:, c] = (above / below).astype(BF16)


def final_kernel(column, lat, *refs):
    out = refs[-1]
    attended, weights = refs[:5], refs[5:9]
    total = lat[...].astype(F32)
    for a, w in zip(attended[:3], weights[:3]):
        total = total + jnp.dot(a[...], w[...], preferred_element_type=F32)
    far = jnp.concatenate([attended[3][...], attended[4][...]], axis=0)
    total = total + jnp.dot(far, weights[3][...], preferred_element_type=F32)
    out[...] = total.astype(BF16)


def final(r, column, latents, attended, weights, earlier=None):
    share = weights[0].shape[1]
    rows = attended[0].shape[0]
    vmem = pl.BlockSpec(memory_space=pltpu.VMEM)
    specs = [pl.BlockSpec((rows, share), lambda i, col: (r, col[0]))] + [vmem] * 9
    operands = [column, latents, *attended, *weights]
    aliases = {}
    if earlier is not None:
        specs.append(pl.BlockSpec(memory_space=pl.ANY))
        aliases = {len(operands): 0}
        operands.append(earlier)
    return pl.pallas_call(
        final_kernel,
        grid_spec=pltpu.PrefetchScalarGridSpec(
            num_scalar_prefetch=1,
            grid=(1,),
            in_specs=specs,
            out_specs=pl.BlockSpec((rows, share), lambda i, col: (r, 0)),
        ),
        out_shape=shape((ROWS, share), BF16),
        input_output_aliases=aliases,
        cost_estimate=pl.CostEstimate(flops=2 * rows * 4 * COLS * share, bytes_accessed=2000000, transcendentals=0),
        compiler_params=pltpu.CompilerParams(vmem_limit_bytes=LIMIT),
        name=f"output_projection_{r}",
    )(*operands)


def moved(x, axis, by):
    size = lax.axis_size(axis)
    return lax.ppermute(x, axis, [(i, (i + by) % size) for i in range(size)])


def swapped(x, axis, bit):
    return lax.ppermute(x, axis, [(i, i ^ bit) for i in range(lax.axis_size(axis))])


def local(latents, w_qkv, w_out, decay, frame_ids, memory_mask):
    phase = lax.axis_index("phase")
    mp = lax.axis_index("mp")
    phase_ref = phase.reshape(1).astype(jnp.int32)
    w3 = jnp.transpose(w_qkv, (1, 0, 2))

    z_ref = lax.axis_index("z").reshape(1).astype(jnp.int32)
    payload = tails(phase_ref, decay[0], latents, w3)
    arrived = lax.all_to_all(payload, PLANE, 0, 0, tiled=True)

    w_out, payload = lax.optimization_barrier((w_out, payload))
    share = w_out.shape[1] // 4
    offsets = (0, 1, -1, 2)
    sends = [lax.dynamic_slice_in_dim(w_out, ((mp + by) & 3) * share, share, 1) for by in offsets]
    weights = [moved(piece, "mp", by) if by else piece for by, piece in zip(offsets, sends)]
    arrived, _ = lax.optimization_barrier((arrived, sends))

    wide = shape((2 * PART + 8, COLS), F32)
    packed = shape((PAYLOAD, COLS), BF16)
    plain = shape((2 * PART, COLS), BF16)
    plain_all = shape((PARTS, 2 * PART, COLS), BF16)
    own, sent = vmem_call(plane_kernel, (wide, packed), "plane_total", 1000000, (arrived,))
    after, sent = lax.optimization_barrier((z_ref, sent))
    got_1 = swapped(sent, "z", 1)
    head_keys = heads(1, after, latents, w3)
    got_1, head_keys = lax.optimization_barrier((got_1, head_keys))

    sent = vmem_call(first_kernel, packed, "through_1", 100000, (z_ref, own, got_1), smem=1)
    after, sent = lax.optimization_barrier((z_ref, sent))
    got_2 = swapped(sent, "z", 2)
    head_values = heads(2, after, latents, w3)
    got_2, head_values = lax.optimization_barrier((got_2, head_values))

    sent = vmem_call(next_kernel, plain, "through_3", 100000, (z_ref, own, got_1, got_2), smem=1)
    got_4 = swapped(sent, "z", 4)
    got_4, weights = lax.optimization_barrier((got_4, weights))
    memory = vmem_call(
        memory_kernel, plain_all, "section_memory", 1000000, (z_ref, got_1, got_2, got_4, arrived), smem=1
    )
    after, memory, head_keys, head_values, frame_ids = lax.optimization_barrier(
        (z_ref, memory, head_keys, head_values, frame_ids)
    )
    memory = lax.all_to_all(memory, PLANE, 0, 0, tiled=True)
    edge = jnp.where(
        phase == 0,
        payload[PARTS - 1, : 2 * PART],
        jnp.concatenate([head_keys[:PART], head_values[:PART]], axis=0),
    )
    halo = swapped(edge, "phase", 1)
    frames_pad = jnp.pad(frame_ids[0], (HALF_WIN, HALF_WIN), constant_values=outside_frame)
    frames = lax.dynamic_slice_in_dim(frames_pad, phase * ROWS, EXT)
    frame_row = frames.reshape(EXT // BLOCK, 1, BLOCK)
    frame_column = jnp.broadcast_to(frames[:, None], (EXT, HD))
    queries = query(after, latents, w3)
    top, bottom = vmem_call(
        window_kernel,
        (shape((ROWS, COLS), F32), shape((ROWS, COLS), F32)),
        "window_attention",
        4 * EXT * BLOCK * COLS * 2,
        (queries, head_keys, head_values, payload, halo, frame_row, frame_column),
        scratch=[pltpu.VMEM((EXT, COLS), BF16)] * 3,
    )
    memory, top, bottom = lax.optimization_barrier((memory, top, bottom))

    pieces = []
    rows = ROWS // 2
    for r in range(2):
        pieces.append(
            vmem_call(
                functools.partial(attend_kernel, r * rows),
                shape((rows, COLS), BF16),
                f"memory_attention_{r}",
                4 * rows * MEM * COLS * 2,
                (phase_ref, memory_mask, queries, memory, top, bottom),
                smem=2,
            )
        )
    column = mp.reshape(1).astype(jnp.int32)
    near = [(moved(piece, "mp", 1), moved(piece, "mp", -1)) for piece in pieces]
    refined = None
    for r, (piece, (right, left)) in enumerate(zip(pieces, near)):
        far = (moved(right[: rows // 2], "mp", 1), moved(left[rows // 2 :], "mp", -1))
        refined = final(r, column, latents, (piece, right, left, *far), weights, refined)
    return refined


def solution(mesh):
    finer = Mesh(
        mesh.devices.reshape(8, 2, 2, mesh.shape["mp"], mesh.shape["phase"]),
        ("z", "y", "core", "mp", "phase"),
    )
    placed = (
        P((*SPAN, "phase"), None),
        P(None, None, "mp"),
        P("mp", None),
        P(SPAN, None, "mp"),
        P(SPAN, None),
        P(SPAN, None),
    )
    return jax.shard_map(
        local, mesh=finer, in_specs=placed, out_specs=P((*SPAN, "phase"), "mp"), check_vma=False
    )
```

```python
import functools

import jax
import jax.numpy as jnp
from jax import lax
from jax.experimental import pallas as pl
from jax.experimental.pallas import tpu as pltpu
from jax.sharding import Mesh
from jax.sharding import PartitionSpec as P

HD = 128
WIN = 64
HALF_WIN = 32
MEM = 256
ROWS = 512
EXT = ROWS + WIN
HEADS = 3
COLS = HEADS * HD
PARTS = 8
PART = MEM // PARTS
PAYLOAD = 2 * PART + 8
CHUNKS = 5
TAIL_LIMIT = 60 * 1024 * 1024
REST_LIMIT = 60 * 1024 * 1024
ATTEND_LIMIT = 53 * 1024 * 1024
LIMIT = 32 * 1024 * 1024
BLOCK = 192
SPAN = ("z", "y", "core")
PLANE = ("y", "core", "phase")

outside_frame = 1048576
epsilon = 1e-06
F32 = jnp.float32
BF16 = jnp.bfloat16
SCALE2 = HD ** (-0.5) * 1.4426950408889634


def shape(dims, dtype):
    return jax.ShapeDtypeStruct(dims, dtype)


def normed(x):
    heads = []
    for h in range(HEADS):
        part = x[:, h * HD : (h + 1) * HD]
        square = jnp.mean(part * part, axis=-1, keepdims=True)
        heads.append(part * lax.rsqrt(square + epsilon))
    return jnp.concatenate(heads, axis=1).astype(BF16)


def pieces_of(row):
    full = jnp.broadcast_to(row, (8, COLS))
    high = full.astype(BF16).astype(F32)
    middle = (full - high).astype(BF16).astype(F32)
    low = full - high - middle
    at = lax.broadcasted_iota(jnp.int32, (8, COLS), 0)
    return jnp.where(at == 0, high, jnp.where(at == 1, middle, jnp.where(at == 2, low, 0.0))).astype(BF16)


def row_of(pieces):
    wide = pieces.astype(F32)
    return wide[0:1] + wide[1:2] + wide[2:3]


def tail_kernel(phase, decay, lat, w, out, tail, wkv, acc, sems):
    depth = lat.shape[1]
    step = depth // CHUNKS
    copies = []
    for k in range(CHUNKS):
        at = pl.ds(k * step, step)
        group = [
            pltpu.make_async_copy(lat.at[pl.ds(MEM, MEM), at], tail.at[:, at], sems.at[3 * k]),
            pltpu.make_async_copy(w.at[1, at], wkv.at[at, pl.ds(0, COLS)], sems.at[3 * k + 1]),
            pltpu.make_async_copy(w.at[2, at], wkv.at[at, pl.ds(COLS, COLS)], sems.at[3 * k + 2]),
        ]
        for copy in group:
            copy.start()
        copies.append(group)
    for k, group in enumerate(copies):
        for copy in group:
            copy.wait()
        at = slice(k * step, (k + 1) * step)
        part = jnp.dot(tail[:, at], wkv[at], preferred_element_type=F32)
        if k == 0:
            acc[...] = part
        else:
            acc[...] += part
    keys = normed(acc[:, :COLS])
    values = acc[:, COLS:].astype(BF16)
    first = phase[0] == 0
    rates = [jnp.where(first, decay[0, h], decay[1, h]) for h in range(HEADS)]
    lane = lax.broadcasted_iota(jnp.int32, (1, COLS), 1)
    row = jnp.where(lane < HD, rates[0], jnp.where(lane < 2 * HD, rates[1], rates[2]))
    tile = pieces_of(row)
    for d in range(PARTS):
        out[d, :PART] = keys[d * PART : (d + 1) * PART]
        out[d, PART : 2 * PART] = values[d * PART : (d + 1) * PART]
        out[d, 2 * PART :] = tile


def tails(phase, decay, latents, w3):
    depth = latents.shape[1]
    smem = pl.BlockSpec(memory_space=pltpu.SMEM)
    vmem = pl.BlockSpec(memory_space=pltpu.VMEM)
    hbm = pl.BlockSpec(memory_space=pl.ANY)
    return pl.pallas_call(
        tail_kernel,
        out_shape=shape((PARTS, PAYLOAD, COLS), BF16),
        in_specs=[smem, smem, hbm, hbm],
        out_specs=vmem,
        scratch_shapes=[
            pltpu.VMEM((MEM, depth), BF16),
            pltpu.VMEM((depth, 2 * COLS), BF16),
            pltpu.VMEM((MEM, 2 * COLS), F32),
            pltpu.SemaphoreType.DMA((3 * CHUNKS,)),
        ],
        cost_estimate=pl.CostEstimate(flops=2 * MEM * depth * 2 * COLS, bytes_accessed=5500000, transcendentals=0),
        compiler_params=pltpu.CompilerParams(vmem_limit_bytes=TAIL_LIMIT),
        name="tail_projection",
    )(phase, decay, latents, w3)


def call_on_hbm(kernel, outs, name, flops, nbytes, args, scratch):
    vmem = pl.BlockSpec(memory_space=pltpu.VMEM)
    hbm = pl.BlockSpec(memory_space=pl.ANY)
    single = not isinstance(outs, tuple)
    return pl.pallas_call(
        kernel,
        out_shape=outs,
        in_specs=[pl.BlockSpec(memory_space=pltpu.SMEM), hbm, hbm] + [vmem] * (len(args) - 3),
        out_specs=vmem if single else tuple(vmem for _ in outs),
        scratch_shapes=scratch,
        cost_estimate=pl.CostEstimate(flops=flops, bytes_accessed=nbytes, transcendentals=0),
        compiler_params=pltpu.CompilerParams(vmem_limit_bytes=REST_LIMIT),
        name=name,
    )(*args)


def head_project(which, lat, w, rows, part, sems):
    copies = [
        pltpu.make_async_copy(w.at[which], part, sems.at[0]),
        pltpu.make_async_copy(lat.at[pl.ds(0, MEM)], rows, sems.at[1]),
    ]
    for copy in copies:
        copy.start()
    for copy in copies:
        copy.wait()
    return jnp.dot(rows[...], part[...], preferred_element_type=F32)


def head_values_kernel(after, lat, w, out, rows, part, sems):
    out[...] = head_project(2, lat, w, rows, part, sems).astype(BF16)


def head_keys_kernel(phase, lat, w, values, payload, out, edge, rows, part, sems):
    keys = normed(head_project(1, lat, w, rows, part, sems))
    out[...] = keys
    first = phase[0] == 0
    edge[:PART] = jnp.where(first, payload[PARTS - 1, :PART], keys[:PART])
    edge[PART:] = jnp.where(first, payload[PARTS - 1, PART : 2 * PART], values[:PART])


def heads(kernel, outs, name, after, latents, w3, *more):
    depth = latents.shape[1]
    return call_on_hbm(
        kernel,
        outs,
        name,
        2 * MEM * depth * COLS,
        3300000,
        (after, latents, w3, *more),
        [pltpu.VMEM((MEM, depth), BF16), pltpu.VMEM((depth, COLS), BF16), pltpu.SemaphoreType.DMA((2,))],
    )


def query_kernel(after, lat, w, out, rows, part, sems):
    copies = [
        pltpu.make_async_copy(w.at[0], part, sems.at[0]),
        pltpu.make_async_copy(lat.at[pl.ds(0, MEM)], rows.at[pl.ds(0, MEM)], sems.at[1]),
        pltpu.make_async_copy(lat.at[pl.ds(MEM, MEM)], rows.at[pl.ds(MEM, MEM)], sems.at[2]),
    ]
    for copy in copies:
        copy.start()
    copies[0].wait()
    for r in range(2):
        copies[1 + r].wait()
        at = slice(r * MEM, (r + 1) * MEM)
        out[at] = normed(jnp.dot(rows[at], part[...], preferred_element_type=F32))


def query(after, latents, w3):
    depth = latents.shape[1]
    return call_on_hbm(
        query_kernel,
        shape((ROWS, COLS), BF16),
        "query_projection",
        2 * ROWS * depth * COLS,
        4600000,
        (after, latents, w3),
        [pltpu.VMEM((ROWS, depth), BF16), pltpu.VMEM((depth, COLS), BF16), pltpu.SemaphoreType.DMA((3,))],
    )


def vmem_call(kernel, outs, name, flops, args, smem=0, scratch=()):
    specs = [pl.BlockSpec(memory_space=pltpu.SMEM)] * smem
    specs += [pl.BlockSpec(memory_space=pltpu.VMEM)] * (len(args) - smem)
    single = not isinstance(outs, tuple)
    out_spec = pl.BlockSpec(memory_space=pltpu.VMEM)
    nbytes = sum(a.size * a.dtype.itemsize for a in args)
    return pl.pallas_call(
        kernel,
        out_shape=outs,
        in_specs=specs,
        out_specs=out_spec if single else tuple(out_spec for _ in outs),
        scratch_shapes=list(scratch),
        cost_estimate=pl.CostEstimate(flops=flops, bytes_accessed=nbytes, transcendentals=0),
        compiler_params=pltpu.CompilerParams(vmem_limit_bytes=LIMIT),
        name=name,
    )(*args)


def window_part(frame_row, frame_column, top, bottom, qx, kx, vx):
    ones = jnp.ones((BLOCK, HD), BF16)
    window_a = lax.broadcasted_iota(jnp.int32, (BLOCK, BLOCK), 0) // WIN
    window_b = lax.broadcasted_iota(jnp.int32, (BLOCK, BLOCK), 1) // WIN
    for b in range(EXT // BLOCK):
        rows = slice(b * BLOCK, (b + 1) * BLOCK)
        allowed = (window_a == window_b) & (frame_row[b] <= frame_column[rows, :1])
        low, high = max(b * BLOCK, HALF_WIN), min((b + 1) * BLOCK, HALF_WIN + ROWS)
        for h in range(HEADS):
            c = slice(h * HD, (h + 1) * HD)
            score = lax.dot_general(qx[rows, c], kx[rows, c], (((1,), (1,)), ((), ())), preferred_element_type=F32)
            weight = jnp.where(allowed, jnp.exp2(score * SCALE2), 0.0).astype(BF16)
            both = jnp.concatenate([vx[rows, c], ones], axis=1)
            result = jnp.dot(weight, both, preferred_element_type=F32)
            cut = result[low - b * BLOCK : high - b * BLOCK]
            top[low - HALF_WIN : high - HALF_WIN, c] = cut[:, :HD]
            bottom[low - HALF_WIN : high - HALF_WIN, c] = cut[:, HD:]


def coefficients(rate):
    return 1.0 - rate, jnp.sqrt(1.0 - rate * rate)


def pack(out, state, row):
    out[: 2 * PART] = state.astype(BF16)
    out[2 * PART :] = pieces_of(row)


def keep(out, state, row):
    out[: 2 * PART] = state
    out[2 * PART :] = jnp.broadcast_to(row, (8, COLS))


def plane_step(keys, values, rate, tail_keys, tail_values):
    for_keys, for_values = coefficients(rate)
    return (
        rate * keys + for_keys * tail_keys.astype(F32),
        rate * values + for_values * tail_values.astype(F32),
    )


def plane_kernel(arrived, state, payload):
    keys = values = jnp.zeros((PART, COLS), F32)
    total = jnp.ones((1, COLS), F32)
    for i in range(PARTS):
        rate = row_of(arrived[i, 2 * PART :])
        keys, values = plane_step(keys, values, rate, arrived[i, :PART], arrived[i, PART : 2 * PART])
        total = total * rate
    both = jnp.concatenate([keys, values], axis=0)
    keep(state, both, total)
    pack(payload, both, total)


def joined(upper, mine, rate, got):
    other, other_rate = got[: 2 * PART].astype(F32), row_of(got[2 * PART :])
    return jnp.where(upper, mine + rate * other, other + other_rate * mine), rate * other_rate


def first_kernel(z, own, got_1, payload):
    total, rate = joined((z[0] & 1) == 1, own[: 2 * PART], own[2 * PART : 2 * PART + 1], got_1)
    pack(payload, total, rate)


def next_kernel(z, own, got_1, got_2, payload):
    total, rate = joined((z[0] & 1) == 1, own[: 2 * PART], own[2 * PART : 2 * PART + 1], got_1)
    total, rate = joined((z[0] & 2) == 2, total, rate, got_2)
    payload[...] = total.astype(BF16)


def memory_kernel(z, got_1, got_2, got_4, arrived, out):
    at_1, at_2, at_4 = (z[0] & 1) == 1, (z[0] & 2) == 2, (z[0] & 4) == 4
    entering = jnp.where(at_1, got_1[: 2 * PART].astype(F32), 0.0)
    rate = jnp.where(at_1, row_of(got_1[2 * PART :]), 1.0)
    entering = jnp.where(at_2, entering + rate * got_2[: 2 * PART].astype(F32), entering)
    rate = jnp.where(at_2, rate * row_of(got_2[2 * PART :]), rate)
    entering = jnp.where(at_4, entering + rate * got_4[...].astype(F32), entering)
    keys, values = entering[:PART], entering[PART:]
    for i in range(PARTS):
        out[i, :PART] = keys.astype(BF16)
        out[i, PART:] = values.astype(BF16)
        if i < PARTS - 1:
            rate = row_of(arrived[i, 2 * PART :])
            keys, values = plane_step(keys, values, rate, arrived[i, :PART], arrived[i, PART : 2 * PART])


def attend_kernel(
    phase, opened, q, head_keys, head_values, tail_rows, halo, rows_in, columns_in, memory_in,
    out, top, bottom, qx, kx, vx, tail, frame_row, frame_column, memory, sems,
):
    own, upper = pl.ds(HALF_WIN, ROWS), pl.ds(HALF_WIN + ROWS, HALF_WIN)
    lower, head = pl.ds(0, HALF_WIN), pl.ds(HALF_WIN, MEM)
    first, second = pl.ds(0, PART), pl.ds(PART, PART)
    pairs = [
        (tail_rows, tail),
        (q, qx.at[own]),
        (head_keys, kx.at[head]),
        (head_values, vx.at[head]),
        (halo.at[first], kx.at[lower]),
        (halo.at[first], kx.at[upper]),
        (halo.at[second], vx.at[lower]),
        (halo.at[second], vx.at[upper]),
        (rows_in, frame_row),
        (columns_in, frame_column),
        (memory_in, memory),
    ]
    copies = [pltpu.make_async_copy(a, b, sems.at[i]) for i, (a, b) in enumerate(pairs)]
    for copy in copies:
        copy.start()
    edge = jnp.zeros((HALF_WIN, COLS), BF16)
    qx[:HALF_WIN] = edge
    qx[HALF_WIN + ROWS :] = edge
    copies[0].wait()
    for d in range(PARTS):
        at = HALF_WIN + MEM + d * PART
        kx[at : at + PART] = tail[d, :PART]
        vx[at : at + PART] = tail[d, PART : 2 * PART]
    for copy in copies[1:-1]:
        copy.wait()
    window_part(frame_row, frame_column, top, bottom, qx, kx, vx)
    start = phase[0] * (ROWS // WIN)
    window = (lax.broadcasted_iota(jnp.int32, (ROWS, HD), 0) + HALF_WIN) // WIN
    is_open = jnp.zeros((ROWS, HD), F32)
    for w in range(ROWS // WIN + 1):
        flag = jnp.where(opened[0, start + w] == 1, 1.0, 0.0)
        is_open = jnp.where(window == w, flag, is_open)
    ones = jnp.ones((MEM, HD), BF16)
    copies[-1].wait()
    for h in range(HEADS):
        c = slice(h * HD, (h + 1) * HD)
        keys = memory[:, :PART, c].reshape(MEM, HD)
        values = memory[:, PART:, c].reshape(MEM, HD)
        score = lax.dot_general(
            qx[HALF_WIN : HALF_WIN + ROWS, c], keys, (((1,), (1,)), ((), ())), preferred_element_type=F32
        )
        weight = jnp.exp2(score * SCALE2).astype(BF16)
        result = jnp.dot(weight, jnp.concatenate([values, ones], axis=1), preferred_element_type=F32)
        above = top[:, c] + is_open * result[:, :HD]
        below = bottom[:, c] + is_open * result[:, HD:]
        out[:, c] = (above / below).astype(BF16)


def attention(phase, opened, *operands):
    smem = pl.BlockSpec(memory_space=pltpu.SMEM)
    hbm = pl.BlockSpec(memory_space=pl.ANY)
    extended = pltpu.VMEM((EXT, COLS), BF16)
    return pl.pallas_call(
        attend_kernel,
        out_shape=shape((ROWS, COLS), BF16),
        in_specs=[smem, smem] + [hbm] * len(operands),
        out_specs=pl.BlockSpec(memory_space=pltpu.VMEM),
        scratch_shapes=[
            pltpu.VMEM((ROWS, COLS), F32),
            pltpu.VMEM((ROWS, COLS), F32),
            extended,
            extended,
            extended,
            pltpu.VMEM((PARTS, PAYLOAD, COLS), BF16),
            pltpu.VMEM((EXT // BLOCK, 1, BLOCK), jnp.int32),
            pltpu.VMEM((EXT, HD), jnp.int32),
            pltpu.VMEM((PARTS, 2 * PART, COLS), BF16),
            pltpu.SemaphoreType.DMA((11,)),
        ],
        cost_estimate=pl.CostEstimate(
            flops=4 * ROWS * (MEM + BLOCK) * COLS * 2, bytes_accessed=3000000, transcendentals=0
        ),
        compiler_params=pltpu.CompilerParams(vmem_limit_bytes=ATTEND_LIMIT),
        name="attention",
    )(phase, opened, *operands)


def near_kernel(lat, own, right, left, w_own, w_right, w_left, total):
    sums = lat[...].astype(F32)
    for a, w in ((own, w_own), (right, w_right), (left, w_left)):
        sums = sums + jnp.dot(a[...], w[...], preferred_element_type=F32)
    total[...] = sums


def far_kernel(total, first, second, w, out):
    half = ROWS // 2
    for r, part in enumerate((first, second)):
        at = slice(r * half, (r + 1) * half)
        out[at] = (total[at] + jnp.dot(part[...], w[...], preferred_element_type=F32)).astype(BF16)


def moved(x, axis, by):
    size = lax.axis_size(axis)
    return lax.ppermute(x, axis, [(i, (i + by) % size) for i in range(size)])


def swapped(x, axis, bit):
    return lax.ppermute(x, axis, [(i, i ^ bit) for i in range(lax.axis_size(axis))])


def local(latents, w_qkv, w_out, decay, frame_ids, memory_mask):
    phase = lax.axis_index("phase")
    mp = lax.axis_index("mp")
    phase_ref = phase.reshape(1).astype(jnp.int32)
    w3 = jnp.transpose(w_qkv, (1, 0, 2))

    z_ref = lax.axis_index("z").reshape(1).astype(jnp.int32)
    payload = tails(phase_ref, decay[0], latents, w3)
    arrived = lax.all_to_all(payload, PLANE, 0, 0, tiled=True)

    w_out, payload = lax.optimization_barrier((w_out, payload))
    share = w_out.shape[1] // 4
    offsets = (0, 1, -1, 2)
    sends = [lax.dynamic_slice_in_dim(w_out, ((mp + by) & 3) * share, share, 1) for by in offsets]
    weights = [moved(piece, "mp", by) if by else piece for by, piece in zip(offsets, sends)]
    half_keys = shape((MEM, COLS), BF16)
    after, payload = lax.optimization_barrier((z_ref, payload))
    head_values = heads(head_values_kernel, half_keys, "head_values", after, latents, w3)
    arrived, _, head_values = lax.optimization_barrier((arrived, sends, head_values))

    wide = shape((2 * PART + 8, COLS), F32)
    packed = shape((PAYLOAD, COLS), BF16)
    plain = shape((2 * PART, COLS), BF16)
    plain_all = shape((PARTS, 2 * PART, COLS), BF16)
    own, sent = vmem_call(plane_kernel, (wide, packed), "plane_total", 1000000, (arrived,))
    got_1 = swapped(sent, "z", 1)
    sent = vmem_call(first_kernel, packed, "through_1", 100000, (z_ref, own, got_1), smem=1)
    latents, sent = lax.optimization_barrier((latents, sent))
    got_2 = swapped(sent, "z", 2)
    own_columns = lax.dynamic_slice_in_dim(latents, mp * share, share, 1)
    got_2, own_columns = lax.optimization_barrier((got_2, own_columns))

    sent = vmem_call(next_kernel, plain, "through_3", 100000, (z_ref, own, got_1, got_2), smem=1)
    after, sent = lax.optimization_barrier((phase_ref, sent))
    got_4 = swapped(sent, "z", 4)
    head_keys, edge = heads(
        head_keys_kernel, (half_keys, plain), "head_keys", after, latents, w3, head_values, payload
    )
    got_4, head_keys = lax.optimization_barrier((got_4, head_keys))
    memory = vmem_call(
        memory_kernel, plain_all, "section_memory", 1000000, (z_ref, got_1, got_2, got_4, arrived), smem=1
    )
    after, memory, edge, frame_ids = lax.optimization_barrier((z_ref, memory, edge, frame_ids))
    memory = lax.all_to_all(memory, PLANE, 0, 0, tiled=True)
    halo = swapped(edge, "phase", 1)
    frames_pad = jnp.pad(frame_ids[0], (HALF_WIN, HALF_WIN), constant_values=outside_frame)
    frames = lax.dynamic_slice_in_dim(frames_pad, phase * ROWS, EXT)
    frame_row = frames.reshape(EXT // BLOCK, 1, BLOCK)
    frame_column = jnp.broadcast_to(frames[:, None], (EXT, HD))
    queries = query(after, latents, w3)
    memory, weights = lax.optimization_barrier((memory, weights))
    attended = attention(
        phase_ref, memory_mask, queries, head_keys, head_values, payload, halo, frame_row, frame_column, memory
    )
    right, left = moved(attended, "mp", 1), moved(attended, "mp", -1)
    far_1, far_2 = moved(right[: ROWS // 2], "mp", 1), moved(left[ROWS // 2 :], "mp", -1)
    total = vmem_call(
        near_kernel,
        shape((ROWS, share), F32),
        "near_projection",
        6 * ROWS * COLS * share,
        (own_columns, attended, right, left, *weights[:3]),
    )
    return vmem_call(
        far_kernel,
        shape((ROWS, share), BF16),
        "far_projection",
        2 * ROWS * COLS * share,
        (total, far_1, far_2, weights[3]),
    )


def solution(mesh):
    finer = Mesh(
        mesh.devices.reshape(8, 2, 2, mesh.shape["mp"], mesh.shape["phase"]),
        ("z", "y", "core", "mp", "phase"),
    )
    placed = (
        P((*SPAN, "phase"), None),
        P(None, None, "mp"),
        P("mp", None),
        P(SPAN, None, "mp"),
        P(SPAN, None),
        P(SPAN, None),
    )
    return jax.shard_map(
        local, mesh=finer, in_specs=placed, out_specs=P((*SPAN, "phase"), "mp"), check_vma=False
    )
```

```python
import functools

import jax
import jax.numpy as jnp
from jax import lax
from jax.experimental import pallas as pl
from jax.experimental.pallas import tpu as pltpu
from jax.sharding import Mesh
from jax.sharding import PartitionSpec as P

HD = 128
WIN = 64
HALF_WIN = 32
MEM = 256
ROWS = 512
EXT = ROWS + WIN
HEADS = 3
COLS = HEADS * HD
PARTS = 8
PART = MEM // PARTS
PAYLOAD = 2 * PART + 8
CHUNKS = 5
TAIL_LIMIT = 60 * 1024 * 1024
REST_LIMIT = 60 * 1024 * 1024
ATTEND_LIMIT = 53 * 1024 * 1024
LIMIT = 32 * 1024 * 1024
SPAN = ("z", "y", "core")
PLANE = ("y", "core", "phase")

outside_frame = 1048576
epsilon = 1e-06
F32 = jnp.float32
BF16 = jnp.bfloat16
SCALE2 = HD ** (-0.5) * 1.4426950408889634


def shape(dims, dtype):
    return jax.ShapeDtypeStruct(dims, dtype)


def normed(x):
    heads = []
    for h in range(HEADS):
        part = x[:, h * HD : (h + 1) * HD]
        square = jnp.mean(part * part, axis=-1, keepdims=True)
        heads.append(part * lax.rsqrt(square + epsilon))
    return jnp.concatenate(heads, axis=1).astype(BF16)


def pieces_of(row):
    full = jnp.broadcast_to(row, (8, COLS))
    high = full.astype(BF16).astype(F32)
    middle = (full - high).astype(BF16).astype(F32)
    low = full - high - middle
    at = lax.broadcasted_iota(jnp.int32, (8, COLS), 0)
    return jnp.where(at == 0, high, jnp.where(at == 1, middle, jnp.where(at == 2, low, 0.0))).astype(BF16)


def row_of(pieces):
    wide = pieces.astype(F32)
    return wide[0:1] + wide[1:2] + wide[2:3]


def tail_kernel(phase, decay, lat, w, out, tail, wkv, acc, sems):
    depth = lat.shape[1]
    step = depth // CHUNKS
    copies = []
    for k in range(CHUNKS):
        at = pl.ds(k * step, step)
        group = [
            pltpu.make_async_copy(lat.at[pl.ds(MEM, MEM), at], tail.at[:, at], sems.at[3 * k]),
            pltpu.make_async_copy(w.at[1, at], wkv.at[at, pl.ds(0, COLS)], sems.at[3 * k + 1]),
            pltpu.make_async_copy(w.at[2, at], wkv.at[at, pl.ds(COLS, COLS)], sems.at[3 * k + 2]),
        ]
        for copy in group:
            copy.start()
        copies.append(group)
    for k, group in enumerate(copies):
        for copy in group:
            copy.wait()
        at = slice(k * step, (k + 1) * step)
        part = jnp.dot(tail[:, at], wkv[at], preferred_element_type=F32)
        if k == 0:
            acc[...] = part
        else:
            acc[...] += part
    keys = normed(acc[:, :COLS])
    values = acc[:, COLS:].astype(BF16)
    first = phase[0] == 0
    rates = [jnp.where(first, decay[0, h], decay[1, h]) for h in range(HEADS)]
    lane = lax.broadcasted_iota(jnp.int32, (1, COLS), 1)
    row = jnp.where(lane < HD, rates[0], jnp.where(lane < 2 * HD, rates[1], rates[2]))
    tile = pieces_of(row)
    for d in range(PARTS):
        out[d, :PART] = keys[d * PART : (d + 1) * PART]
        out[d, PART : 2 * PART] = values[d * PART : (d + 1) * PART]
        out[d, 2 * PART :] = tile


def tails(phase, decay, latents, w3):
    depth = latents.shape[1]
    smem = pl.BlockSpec(memory_space=pltpu.SMEM)
    vmem = pl.BlockSpec(memory_space=pltpu.VMEM)
    hbm = pl.BlockSpec(memory_space=pl.ANY)
    return pl.pallas_call(
        tail_kernel,
        out_shape=shape((PARTS, PAYLOAD, COLS), BF16),
        in_specs=[smem, smem, hbm, hbm],
        out_specs=vmem,
        scratch_shapes=[
            pltpu.VMEM((MEM, depth), BF16),
            pltpu.VMEM((depth, 2 * COLS), BF16),
            pltpu.VMEM((MEM, 2 * COLS), F32),
            pltpu.SemaphoreType.DMA((3 * CHUNKS,)),
        ],
        cost_estimate=pl.CostEstimate(flops=2 * MEM * depth * 2 * COLS, bytes_accessed=5500000, transcendentals=0),
        compiler_params=pltpu.CompilerParams(vmem_limit_bytes=TAIL_LIMIT),
        name="tail_projection",
    )(phase, decay, latents, w3)


def call_on_hbm(kernel, outs, name, flops, nbytes, args, scratch):
    vmem = pl.BlockSpec(memory_space=pltpu.VMEM)
    hbm = pl.BlockSpec(memory_space=pl.ANY)
    single = not isinstance(outs, tuple)
    return pl.pallas_call(
        kernel,
        out_shape=outs,
        in_specs=[pl.BlockSpec(memory_space=pltpu.SMEM)] + [hbm] * (len(args) - 1),
        out_specs=vmem if single else tuple(vmem for _ in outs),
        scratch_shapes=scratch,
        cost_estimate=pl.CostEstimate(flops=flops, bytes_accessed=nbytes, transcendentals=0),
        compiler_params=pltpu.CompilerParams(vmem_limit_bytes=REST_LIMIT),
        name=name,
    )(*args)


def head_project(which, lat, w, rows, part, sems):
    copies = [
        pltpu.make_async_copy(w.at[which], part, sems.at[0]),
        pltpu.make_async_copy(lat.at[pl.ds(0, MEM)], rows, sems.at[1]),
    ]
    for copy in copies:
        copy.start()
    for copy in copies:
        copy.wait()
    return jnp.dot(rows[...], part[...], preferred_element_type=F32)


def head_values_kernel(after, lat, w, out, rows, part, sems):
    out[...] = head_project(2, lat, w, rows, part, sems).astype(BF16)


def head_keys_kernel(phase, lat, w, values, payload, out, edge, rows, part, first_values, last, sems):
    copies = [
        pltpu.make_async_copy(values.at[pl.ds(0, PART)], first_values, sems.at[2]),
        pltpu.make_async_copy(payload.at[PARTS - 1, pl.ds(0, 2 * PART)], last, sems.at[3]),
    ]
    for copy in copies:
        copy.start()
    keys = normed(head_project(1, lat, w, rows, part, sems))
    out[...] = keys
    for copy in copies:
        copy.wait()
    first = phase[0] == 0
    edge[:PART] = jnp.where(first, last[:PART], keys[:PART])
    edge[PART:] = jnp.where(first, last[PART:], first_values[...])


def heads(kernel, outs, name, after, latents, w3, *more):
    depth = latents.shape[1]
    scratch = [pltpu.VMEM((MEM, depth), BF16), pltpu.VMEM((depth, COLS), BF16)]
    if more:
        scratch += [pltpu.VMEM((PART, COLS), BF16), pltpu.VMEM((2 * PART, COLS), BF16)]
    return call_on_hbm(
        kernel,
        outs,
        name,
        2 * MEM * depth * COLS,
        3300000,
        (after, latents, w3, *more),
        scratch + [pltpu.SemaphoreType.DMA((4,))],
    )


def query_kernel(after, lat, w, out, rows, part, sems):
    copies = [
        pltpu.make_async_copy(w.at[0], part, sems.at[0]),
        pltpu.make_async_copy(lat.at[pl.ds(0, MEM)], rows.at[pl.ds(0, MEM)], sems.at[1]),
        pltpu.make_async_copy(lat.at[pl.ds(MEM, MEM)], rows.at[pl.ds(MEM, MEM)], sems.at[2]),
    ]
    for copy in copies:
        copy.start()
    copies[0].wait()
    for r in range(2):
        copies[1 + r].wait()
        at = slice(r * MEM, (r + 1) * MEM)
        out[at] = normed(jnp.dot(rows[at], part[...], preferred_element_type=F32))


def query(after, latents, w3):
    depth = latents.shape[1]
    return call_on_hbm(
        query_kernel,
        shape((ROWS, COLS), BF16),
        "query_projection",
        2 * ROWS * depth * COLS,
        4600000,
        (after, latents, w3),
        [pltpu.VMEM((ROWS, depth), BF16), pltpu.VMEM((depth, COLS), BF16), pltpu.SemaphoreType.DMA((3,))],
    )


def vmem_call(kernel, outs, name, flops, args, smem=0, scratch=()):
    specs = [pl.BlockSpec(memory_space=pltpu.SMEM)] * smem
    specs += [pl.BlockSpec(memory_space=pltpu.VMEM)] * (len(args) - smem)
    single = not isinstance(outs, tuple)
    out_spec = pl.BlockSpec(memory_space=pltpu.VMEM)
    nbytes = sum(a.size * a.dtype.itemsize for a in args)
    return pl.pallas_call(
        kernel,
        out_shape=outs,
        in_specs=specs,
        out_specs=out_spec if single else tuple(out_spec for _ in outs),
        scratch_shapes=list(scratch),
        cost_estimate=pl.CostEstimate(flops=flops, bytes_accessed=nbytes, transcendentals=0),
        compiler_params=pltpu.CompilerParams(vmem_limit_bytes=LIMIT),
        name=name,
    )(*args)


def coefficients(rate):
    return 1.0 - rate, jnp.sqrt(1.0 - rate * rate)


def pack(out, state, row):
    out[: 2 * PART] = state.astype(BF16)
    out[2 * PART :] = pieces_of(row)


def keep(out, state, row):
    out[: 2 * PART] = state
    out[2 * PART :] = jnp.broadcast_to(row, (8, COLS))


def plane_step(keys, values, rate, tail_keys, tail_values):
    for_keys, for_values = coefficients(rate)
    return (
        rate * keys + for_keys * tail_keys.astype(F32),
        rate * values + for_values * tail_values.astype(F32),
    )


def plane_kernel(arrived, state, payload):
    keys = values = jnp.zeros((PART, COLS), F32)
    total = jnp.ones((1, COLS), F32)
    for i in range(PARTS):
        rate = row_of(arrived[i, 2 * PART :])
        keys, values = plane_step(keys, values, rate, arrived[i, :PART], arrived[i, PART : 2 * PART])
        total = total * rate
    both = jnp.concatenate([keys, values], axis=0)
    keep(state, both, total)
    pack(payload, both, total)


def joined(upper, mine, rate, got):
    other, other_rate = got[: 2 * PART].astype(F32), row_of(got[2 * PART :])
    return jnp.where(upper, mine + rate * other, other + other_rate * mine), rate * other_rate


def first_kernel(z, own, got_1, payload):
    total, rate = joined((z[0] & 1) == 1, own[: 2 * PART], own[2 * PART : 2 * PART + 1], got_1)
    pack(payload, total, rate)


def next_kernel(z, own, got_1, got_2, payload):
    total, rate = joined((z[0] & 1) == 1, own[: 2 * PART], own[2 * PART : 2 * PART + 1], got_1)
    total, rate = joined((z[0] & 2) == 2, total, rate, got_2)
    payload[...] = total.astype(BF16)


def memory_kernel(z, got_1, got_2, got_4, arrived, out):
    at_1, at_2, at_4 = (z[0] & 1) == 1, (z[0] & 2) == 2, (z[0] & 4) == 4
    entering = jnp.where(at_1, got_1[: 2 * PART].astype(F32), 0.0)
    rate = jnp.where(at_1, row_of(got_1[2 * PART :]), 1.0)
    entering = jnp.where(at_2, entering + rate * got_2[: 2 * PART].astype(F32), entering)
    rate = jnp.where(at_2, rate * row_of(got_2[2 * PART :]), rate)
    entering = jnp.where(at_4, entering + rate * got_4[...].astype(F32), entering)
    keys, values = entering[:PART], entering[PART:]
    for i in range(PARTS):
        out[i, :PART] = keys.astype(BF16)
        out[i, PART:] = values.astype(BF16)
        if i < PARTS - 1:
            rate = row_of(arrived[i, 2 * PART :])
            keys, values = plane_step(keys, values, rate, arrived[i, :PART], arrived[i, PART : 2 * PART])


def attend_kernel(
    r, phase, opened, q, head_keys, head_values, tail_rows, halo, rows_in, columns_in, memory_in,
    out, top, bottom, qx, kx, vx, tail, frame_row, frame_column, memory, sems,
):
    half = ROWS // 2
    base = r * half
    low, high = base, base + half + WIN
    first, second = pl.ds(0, PART), pl.ds(PART, PART)
    seen = pl.ds(low, high - low)
    used = 1 if r == 0 else PARTS
    pairs = [
        (q.at[pl.ds(base, half)], qx.at[pl.ds(HALF_WIN + base, half)]),
        (memory_in, memory),
        (tail_rows.at[pl.ds(0, used)], tail.at[pl.ds(0, used)]),
        (rows_in, frame_row),
        (columns_in.at[seen], frame_column.at[seen]),
    ]
    if r == 0:
        edge, head, source = pl.ds(0, HALF_WIN), pl.ds(HALF_WIN, MEM), pl.ds(0, MEM)
    else:
        edge, head, source = pl.ds(HALF_WIN + ROWS, HALF_WIN), pl.ds(low, HALF_WIN), pl.ds(MEM - HALF_WIN, HALF_WIN)
    pairs += [
        (head_keys.at[source], kx.at[head]),
        (head_values.at[source], vx.at[head]),
        (halo.at[first], kx.at[edge]),
        (halo.at[second], vx.at[edge]),
    ]
    copies = [pltpu.make_async_copy(a, b, sems.at[i]) for i, (a, b) in enumerate(pairs)]
    for copy in copies:
        copy.start()
    blank = jnp.zeros((HALF_WIN, COLS), BF16)
    qx[low : low + HALF_WIN] = blank
    qx[high - HALF_WIN : high] = blank
    start = phase[0] * (ROWS // WIN)
    window = (lax.broadcasted_iota(jnp.int32, (half, HD), 0) + base + HALF_WIN) // WIN
    is_open = jnp.zeros((half, HD), F32)
    for w in range(low // WIN, high // WIN):
        flag = jnp.where(opened[0, start + w] == 1, 1.0, 0.0)
        is_open = jnp.where(window == w, flag, is_open)
    ones = jnp.ones((MEM, HD), BF16)
    copies[0].wait()
    copies[1].wait()
    for h in range(HEADS):
        c = slice(h * HD, (h + 1) * HD)
        keys = memory[:, :PART, c].reshape(MEM, HD)
        values = memory[:, PART:, c].reshape(MEM, HD)
        own = qx[HALF_WIN + base : HALF_WIN + base + half, c]
        score = lax.dot_general(own, keys, (((1,), (1,)), ((), ())), preferred_element_type=F32)
        weight = jnp.exp2(score * SCALE2).astype(BF16)
        result = jnp.dot(weight, jnp.concatenate([values, ones], axis=1), preferred_element_type=F32)
        top[:, c] = is_open * result[:, :HD]
        bottom[:, c] = is_open * result[:, HD:]
    for copy in copies[2:]:
        copy.wait()
    for d in range(used):
        at = HALF_WIN + MEM + d * PART
        kx[at : at + PART] = tail[d, :PART]
        vx[at : at + PART] = tail[d, PART : 2 * PART]
    for begin, size in ((low, half), (low + half, WIN)):
        rows = slice(begin, begin + size)
        window_a = lax.broadcasted_iota(jnp.int32, (size, size), 0) // WIN
        window_b = lax.broadcasted_iota(jnp.int32, (size, size), 1) // WIN
        allowed = (window_a == window_b) & (frame_row[:, rows] <= frame_column[rows, :1])
        begin_own, end_own = max(begin, low + HALF_WIN), min(begin + size, high - HALF_WIN)
        to = slice(begin_own - HALF_WIN - base, end_own - HALF_WIN - base)
        for h in range(HEADS):
            c = slice(h * HD, (h + 1) * HD)
            score = lax.dot_general(qx[rows, c], kx[rows, c], (((1,), (1,)), ((), ())), preferred_element_type=F32)
            weight = jnp.where(allowed, jnp.exp2(score * SCALE2), 0.0).astype(BF16)
            both = jnp.concatenate([vx[rows, c], jnp.ones((size, HD), BF16)], axis=1)
            cut = jnp.dot(weight, both, preferred_element_type=F32)[begin_own - begin : end_own - begin]
            above, below = top[to, c] + cut[:, :HD], bottom[to, c] + cut[:, HD:]
            out[to, c] = (above / below).astype(BF16)


def attention(r, phase, opened, *operands):
    smem = pl.BlockSpec(memory_space=pltpu.SMEM)
    hbm = pl.BlockSpec(memory_space=pl.ANY)
    half = ROWS // 2
    extended = pltpu.VMEM((EXT, COLS), BF16)
    return pl.pallas_call(
        functools.partial(attend_kernel, r),
        out_shape=shape((half, COLS), BF16),
        in_specs=[smem, smem] + [hbm] * len(operands),
        out_specs=pl.BlockSpec(memory_space=pltpu.VMEM),
        scratch_shapes=[
            pltpu.VMEM((half, COLS), F32),
            pltpu.VMEM((half, COLS), F32),
            extended,
            extended,
            extended,
            pltpu.VMEM((PARTS, PAYLOAD, COLS), BF16),
            pltpu.VMEM((1, EXT), jnp.int32),
            pltpu.VMEM((EXT, HD), jnp.int32),
            pltpu.VMEM((PARTS, 2 * PART, COLS), BF16),
            pltpu.SemaphoreType.DMA((9,)),
        ],
        cost_estimate=pl.CostEstimate(
            flops=2 * ROWS * (MEM + half) * COLS * 2, bytes_accessed=1500000, transcendentals=0
        ),
        compiler_params=pltpu.CompilerParams(vmem_limit_bytes=ATTEND_LIMIT),
        name=f"attention_{r}",
    )(phase, opened, *operands)


def near_kernel(lat, own_0, own_1, right_0, right_1, left_0, left_1, w_own, w_right, w_left, total):
    half = ROWS // 2
    for r, parts in enumerate(((own_0, right_0, left_0), (own_1, right_1, left_1))):
        at = slice(r * half, (r + 1) * half)
        sums = lat[at].astype(F32)
        for a, w in zip(parts, (w_own, w_right, w_left)):
            sums = sums + jnp.dot(a[...], w[...], preferred_element_type=F32)
        total[at] = sums


def far_kernel(total, first, second, w, out):
    half = ROWS // 2
    for r, part in enumerate((first, second)):
        at = slice(r * half, (r + 1) * half)
        out[at] = (total[at] + jnp.dot(part[...], w[...], preferred_element_type=F32)).astype(BF16)


def moved(x, axis, by):
    size = lax.axis_size(axis)
    return lax.ppermute(x, axis, [(i, (i + by) % size) for i in range(size)])


def swapped(x, axis, bit):
    return lax.ppermute(x, axis, [(i, i ^ bit) for i in range(lax.axis_size(axis))])


def local(latents, w_qkv, w_out, decay, frame_ids, memory_mask):
    phase = lax.axis_index("phase")
    mp = lax.axis_index("mp")
    phase_ref = phase.reshape(1).astype(jnp.int32)
    w3 = jnp.transpose(w_qkv, (1, 0, 2))

    z_ref = lax.axis_index("z").reshape(1).astype(jnp.int32)
    payload = tails(phase_ref, decay[0], latents, w3)
    arrived = lax.all_to_all(payload, PLANE, 0, 0, tiled=True)

    w_out, payload = lax.optimization_barrier((w_out, payload))
    share = w_out.shape[1] // 4
    offsets = (0, 1, -1, 2)
    sends = [lax.dynamic_slice_in_dim(w_out, ((mp + by) & 3) * share, share, 1) for by in offsets]
    weights = [moved(piece, "mp", by) if by else piece for by, piece in zip(offsets, sends)]
    arrived, _ = lax.optimization_barrier((arrived, sends))
    half_keys = shape((MEM, COLS), BF16)

    wide = shape((2 * PART + 8, COLS), F32)
    packed = shape((PAYLOAD, COLS), BF16)
    plain = shape((2 * PART, COLS), BF16)
    plain_all = shape((PARTS, 2 * PART, COLS), BF16)
    own, sent = vmem_call(plane_kernel, (wide, packed), "plane_total", 1000000, (arrived,))
    latents, sent = lax.optimization_barrier((latents, sent))
    got_1 = swapped(sent, "z", 1)
    own_columns = lax.dynamic_slice_in_dim(latents, mp * share, share, 1)
    got_1, own_columns = lax.optimization_barrier((got_1, own_columns))
    sent = vmem_call(first_kernel, packed, "through_1", 100000, (z_ref, own, got_1), smem=1)
    after, sent = lax.optimization_barrier((z_ref, sent))
    got_2 = swapped(sent, "z", 2)
    head_values = heads(head_values_kernel, half_keys, "head_values", after, latents, w3)
    got_2, head_values = lax.optimization_barrier((got_2, head_values))

    sent = vmem_call(next_kernel, plain, "through_3", 100000, (z_ref, own, got_1, got_2), smem=1)
    after, sent = lax.optimization_barrier((phase_ref, sent))
    got_4 = swapped(sent, "z", 7)
    head_keys, edge = heads(
        head_keys_kernel, (half_keys, plain), "head_keys", after, latents, w3, head_values, payload
    )
    got_4, head_keys = lax.optimization_barrier((got_4, head_keys))
    memory = vmem_call(
        memory_kernel, plain_all, "section_memory", 1000000, (z_ref, got_1, got_2, got_4, arrived), smem=1
    )
    after, memory, edge, frame_ids = lax.optimization_barrier((z_ref, memory, edge, frame_ids))
    memory = lax.all_to_all(memory, PLANE, 0, 0, tiled=True)
    halo = swapped(edge, "phase", 1)
    frames_pad = jnp.pad(frame_ids[0], (HALF_WIN, HALF_WIN), constant_values=outside_frame)
    frames = lax.dynamic_slice_in_dim(frames_pad, phase * ROWS, EXT)
    frame_row = frames.reshape(1, EXT)
    frame_column = jnp.broadcast_to(frames[:, None], (EXT, HD))
    queries = query(after, latents, w3)
    memory, weights = lax.optimization_barrier((memory, weights))
    halves = [
        attention(
            r, phase_ref, memory_mask, queries, head_keys, head_values, payload, halo, frame_row, frame_column, memory
        )
        for r in range(2)
    ]
    right = [moved(piece, "mp", 1) for piece in halves]
    left = [moved(piece, "mp", -1) for piece in halves]
    right[1], left[1] = lax.optimization_barrier((right[1], left[1]))
    far_1, far_2 = moved(right[0], "mp", 1), moved(left[1], "mp", -1)
    total = vmem_call(
        near_kernel,
        shape((ROWS, share), F32),
        "near_projection",
        6 * ROWS * COLS * share,
        (own_columns, *halves, *right, *left, *weights[:3]),
    )
    return vmem_call(
        far_kernel,
        shape((ROWS, share), BF16),
        "far_projection",
        2 * ROWS * COLS * share,
        (total, far_1, far_2, weights[3]),
    )


def solution(mesh):
    finer = Mesh(
        mesh.devices.reshape(8, 2, 2, mesh.shape["mp"], mesh.shape["phase"]),
        ("z", "y", "core", "mp", "phase"),
    )
    placed = (
        P((*SPAN, "phase"), None),
        P(None, None, "mp"),
        P("mp", None),
        P(SPAN, None, "mp"),
        P(SPAN, None),
        P(SPAN, None),
    )
    return jax.shard_map(
        local, mesh=finer, in_specs=placed, out_specs=P((*SPAN, "phase"), "mp"), check_vma=False
    )
```

```python
import functools

import jax
import jax.numpy as jnp
from jax import lax
from jax.experimental import pallas as pl
from jax.experimental.pallas import tpu as pltpu
from jax.sharding import Mesh
from jax.sharding import PartitionSpec as P

HD = 128
WIN = 64
HALF_WIN = 32
MEM = 256
ROWS = 512
EXT = ROWS + WIN
HEADS = 3
COLS = HEADS * HD
PARTS = 8
PART = MEM // PARTS
PAYLOAD = 2 * PART + 8
CHUNKS = 5
TAIL_LIMIT = 60 * 1024 * 1024
REST_LIMIT = 60 * 1024 * 1024
ATTEND_LIMIT = 53 * 1024 * 1024
QUERY_LIMIT = 60 * 1024 * 1024
LIMIT = 32 * 1024 * 1024
SPAN = ("z", "y", "core")
PLANE = ("y", "core", "phase")

outside_frame = 1048576
epsilon = 1e-06
F32 = jnp.float32
BF16 = jnp.bfloat16
SCALE2 = HD ** (-0.5) * 1.4426950408889634


def shape(dims, dtype):
    return jax.ShapeDtypeStruct(dims, dtype)


def normed(x):
    heads = []
    for h in range(HEADS):
        part = x[:, h * HD : (h + 1) * HD]
        square = jnp.mean(part * part, axis=-1, keepdims=True)
        heads.append(part * lax.rsqrt(square + epsilon))
    return jnp.concatenate(heads, axis=1).astype(BF16)


def pieces_of(row):
    full = jnp.broadcast_to(row, (8, COLS))
    high = full.astype(BF16).astype(F32)
    middle = (full - high).astype(BF16).astype(F32)
    low = full - high - middle
    at = lax.broadcasted_iota(jnp.int32, (8, COLS), 0)
    return jnp.where(at == 0, high, jnp.where(at == 1, middle, jnp.where(at == 2, low, 0.0))).astype(BF16)


def row_of(pieces):
    wide = pieces.astype(F32)
    return wide[0:1] + wide[1:2] + wide[2:3]


def tail_kernel(phase, decay, lat, w, out, tail, wkv, acc, sems):
    depth = lat.shape[1]
    step = depth // CHUNKS
    copies = []
    for k in range(CHUNKS):
        at = pl.ds(k * step, step)
        group = [
            pltpu.make_async_copy(lat.at[pl.ds(MEM, MEM), at], tail.at[:, at], sems.at[3 * k]),
            pltpu.make_async_copy(w.at[1, at], wkv.at[at, pl.ds(0, COLS)], sems.at[3 * k + 1]),
            pltpu.make_async_copy(w.at[2, at], wkv.at[at, pl.ds(COLS, COLS)], sems.at[3 * k + 2]),
        ]
        for copy in group:
            copy.start()
        copies.append(group)
    for k, group in enumerate(copies):
        for copy in group:
            copy.wait()
        at = slice(k * step, (k + 1) * step)
        part = jnp.dot(tail[:, at], wkv[at], preferred_element_type=F32)
        if k == 0:
            acc[...] = part
        else:
            acc[...] += part
    keys = normed(acc[:, :COLS])
    values = acc[:, COLS:].astype(BF16)
    first = phase[0] == 0
    rates = [jnp.where(first, decay[0, h], decay[1, h]) for h in range(HEADS)]
    lane = lax.broadcasted_iota(jnp.int32, (1, COLS), 1)
    row = jnp.where(lane < HD, rates[0], jnp.where(lane < 2 * HD, rates[1], rates[2]))
    tile = pieces_of(row)
    for d in range(PARTS):
        out[d, :PART] = keys[d * PART : (d + 1) * PART]
        out[d, PART : 2 * PART] = values[d * PART : (d + 1) * PART]
        out[d, 2 * PART :] = tile


def tails(phase, decay, latents, w3):
    depth = latents.shape[1]
    smem = pl.BlockSpec(memory_space=pltpu.SMEM)
    vmem = pl.BlockSpec(memory_space=pltpu.VMEM)
    hbm = pl.BlockSpec(memory_space=pl.ANY)
    return pl.pallas_call(
        tail_kernel,
        out_shape=shape((PARTS, PAYLOAD, COLS), BF16),
        in_specs=[smem, smem, hbm, hbm],
        out_specs=vmem,
        scratch_shapes=[
            pltpu.VMEM((MEM, depth), BF16),
            pltpu.VMEM((depth, 2 * COLS), BF16),
            pltpu.VMEM((MEM, 2 * COLS), F32),
            pltpu.SemaphoreType.DMA((3 * CHUNKS,)),
        ],
        cost_estimate=pl.CostEstimate(flops=2 * MEM * depth * 2 * COLS, bytes_accessed=5500000, transcendentals=0),
        compiler_params=pltpu.CompilerParams(vmem_limit_bytes=TAIL_LIMIT),
        name="tail_projection",
    )(phase, decay, latents, w3)


def call_on_hbm(kernel, outs, name, flops, nbytes, args, scratch, limit=REST_LIMIT):
    vmem = pl.BlockSpec(memory_space=pltpu.VMEM)
    hbm = pl.BlockSpec(memory_space=pl.ANY)
    single = not isinstance(outs, tuple)
    return pl.pallas_call(
        kernel,
        out_shape=outs,
        in_specs=[pl.BlockSpec(memory_space=pltpu.SMEM)] + [hbm] * (len(args) - 1),
        out_specs=vmem if single else tuple(vmem for _ in outs),
        scratch_shapes=scratch,
        cost_estimate=pl.CostEstimate(flops=flops, bytes_accessed=nbytes, transcendentals=0),
        compiler_params=pltpu.CompilerParams(vmem_limit_bytes=limit),
        name=name,
    )(*args)


def head_project(which, lat, w, rows, part, sems):
    copies = [
        pltpu.make_async_copy(w.at[which], part, sems.at[0]),
        pltpu.make_async_copy(lat.at[pl.ds(0, MEM)], rows, sems.at[1]),
    ]
    for copy in copies:
        copy.start()
    for copy in copies:
        copy.wait()
    return jnp.dot(rows[...], part[...], preferred_element_type=F32)


def head_values_kernel(after, lat, w, out, rows, part, sems):
    out[...] = head_project(2, lat, w, rows, part, sems).astype(BF16)


def head_keys_kernel(phase, lat, w, values, payload, out, edge, rows, part, first_values, last, sems):
    copies = [
        pltpu.make_async_copy(values.at[pl.ds(0, PART)], first_values, sems.at[2]),
        pltpu.make_async_copy(payload.at[PARTS - 1, pl.ds(0, 2 * PART)], last, sems.at[3]),
    ]
    for copy in copies:
        copy.start()
    keys = normed(head_project(1, lat, w, rows, part, sems))
    out[...] = keys
    for copy in copies:
        copy.wait()
    first = phase[0] == 0
    edge[:PART] = jnp.where(first, last[:PART], keys[:PART])
    edge[PART:] = jnp.where(first, last[PART:], first_values[...])


def heads(kernel, outs, name, after, latents, w3, *more):
    depth = latents.shape[1]
    scratch = [pltpu.VMEM((MEM, depth), BF16), pltpu.VMEM((depth, COLS), BF16)]
    if more:
        scratch += [pltpu.VMEM((PART, COLS), BF16), pltpu.VMEM((2 * PART, COLS), BF16)]
    return call_on_hbm(
        kernel,
        outs,
        name,
        2 * MEM * depth * COLS,
        3300000,
        (after, latents, w3, *more),
        scratch + [pltpu.SemaphoreType.DMA((4,))],
    )


def query_kernel(after, lat, w, out, rows, part, sems):
    copies = [
        pltpu.make_async_copy(w.at[0], part, sems.at[0]),
        pltpu.make_async_copy(lat.at[pl.ds(0, MEM)], rows.at[pl.ds(0, MEM)], sems.at[1]),
        pltpu.make_async_copy(lat.at[pl.ds(MEM, MEM)], rows.at[pl.ds(MEM, MEM)], sems.at[2]),
    ]
    for copy in copies:
        copy.start()
    copies[0].wait()
    for r in range(2):
        copies[1 + r].wait()
        at = slice(r * MEM, (r + 1) * MEM)
        out[at] = normed(jnp.dot(rows[at], part[...], preferred_element_type=F32))


def query(after, latents, w3):
    depth = latents.shape[1]
    return call_on_hbm(
        query_kernel,
        shape((ROWS, COLS), BF16),
        "query_projection",
        2 * ROWS * depth * COLS,
        4600000,
        (after, latents, w3),
        [pltpu.VMEM((ROWS, depth), BF16), pltpu.VMEM((depth, COLS), BF16), pltpu.SemaphoreType.DMA((3,))],
        QUERY_LIMIT,
    )


def vmem_call(kernel, outs, name, flops, args, smem=0, scratch=()):
    specs = [pl.BlockSpec(memory_space=pltpu.SMEM)] * smem
    specs += [pl.BlockSpec(memory_space=pltpu.VMEM)] * (len(args) - smem)
    single = not isinstance(outs, tuple)
    out_spec = pl.BlockSpec(memory_space=pltpu.VMEM)
    nbytes = sum(a.size * a.dtype.itemsize for a in args)
    return pl.pallas_call(
        kernel,
        out_shape=outs,
        in_specs=specs,
        out_specs=out_spec if single else tuple(out_spec for _ in outs),
        scratch_shapes=list(scratch),
        cost_estimate=pl.CostEstimate(flops=flops, bytes_accessed=nbytes, transcendentals=0),
        compiler_params=pltpu.CompilerParams(vmem_limit_bytes=LIMIT),
        name=name,
    )(*args)


def coefficients(rate):
    return 1.0 - rate, jnp.sqrt(1.0 - rate * rate)


def pack(out, state, row):
    out[: 2 * PART] = state.astype(BF16)
    out[2 * PART :] = pieces_of(row)


def keep(out, state, row):
    out[: 2 * PART] = state
    out[2 * PART :] = jnp.broadcast_to(row, (8, COLS))


def plane_step(keys, values, rate, tail_keys, tail_values):
    for_keys, for_values = coefficients(rate)
    return (
        rate * keys + for_keys * tail_keys.astype(F32),
        rate * values + for_values * tail_values.astype(F32),
    )


def plane_kernel(arrived, state, payload):
    keys = values = jnp.zeros((PART, COLS), F32)
    total = jnp.ones((1, COLS), F32)
    for i in range(PARTS):
        rate = row_of(arrived[i, 2 * PART :])
        keys, values = plane_step(keys, values, rate, arrived[i, :PART], arrived[i, PART : 2 * PART])
        total = total * rate
    both = jnp.concatenate([keys, values], axis=0)
    keep(state, both, total)
    pack(payload, both, total)


def joined(upper, mine, rate, got):
    other, other_rate = got[: 2 * PART].astype(F32), row_of(got[2 * PART :])
    return jnp.where(upper, mine + rate * other, other + other_rate * mine), rate * other_rate


def first_kernel(z, own, got_1, payload):
    total, rate = joined((z[0] & 1) == 1, own[: 2 * PART], own[2 * PART : 2 * PART + 1], got_1)
    pack(payload, total, rate)


def next_kernel(z, own, got_1, got_2, payload):
    total, rate = joined((z[0] & 1) == 1, own[: 2 * PART], own[2 * PART : 2 * PART + 1], got_1)
    total, rate = joined((z[0] & 2) == 2, total, rate, got_2)
    payload[...] = total.astype(BF16)


def memory_kernel(z, got_1, got_2, got_4, arrived, out):
    at_1, at_2, at_4 = (z[0] & 1) == 1, (z[0] & 2) == 2, (z[0] & 4) == 4
    entering = jnp.where(at_1, got_1[: 2 * PART].astype(F32), 0.0)
    rate = jnp.where(at_1, row_of(got_1[2 * PART :]), 1.0)
    entering = jnp.where(at_2, entering + rate * got_2[: 2 * PART].astype(F32), entering)
    rate = jnp.where(at_2, rate * row_of(got_2[2 * PART :]), rate)
    entering = jnp.where(at_4, entering + rate * got_4[...].astype(F32), entering)
    keys, values = entering[:PART], entering[PART:]
    for i in range(PARTS):
        out[i, :PART] = keys.astype(BF16)
        out[i, PART:] = values.astype(BF16)
        if i < PARTS - 1:
            rate = row_of(arrived[i, 2 * PART :])
            keys, values = plane_step(keys, values, rate, arrived[i, :PART], arrived[i, PART : 2 * PART])


def attend_kernel(
    r, phase, opened, q, head_keys, head_values, tail_rows, halo, rows_in, columns_in, memory_in,
    out, top, bottom, qx, kx, vx, tail, frame_row, frame_column, memory, sems,
):
    half = ROWS // 2
    base = r * half
    low, high = base, base + half + WIN
    first, second = pl.ds(0, PART), pl.ds(PART, PART)
    seen = pl.ds(low, high - low)
    used = 1 if r == 0 else PARTS
    pairs = [
        (q.at[pl.ds(base, half)], qx.at[pl.ds(HALF_WIN + base, half)]),
        (memory_in, memory),
        (tail_rows.at[pl.ds(0, used)], tail.at[pl.ds(0, used)]),
        (rows_in, frame_row),
        (columns_in.at[seen], frame_column.at[seen]),
    ]
    if r == 0:
        edge, head, source = pl.ds(0, HALF_WIN), pl.ds(HALF_WIN, MEM), pl.ds(0, MEM)
    else:
        edge, head, source = pl.ds(HALF_WIN + ROWS, HALF_WIN), pl.ds(low, HALF_WIN), pl.ds(MEM - HALF_WIN, HALF_WIN)
    pairs += [
        (head_keys.at[source], kx.at[head]),
        (head_values.at[source], vx.at[head]),
        (halo.at[first], kx.at[edge]),
        (halo.at[second], vx.at[edge]),
    ]
    copies = [pltpu.make_async_copy(a, b, sems.at[i]) for i, (a, b) in enumerate(pairs)]
    for copy in copies:
        copy.start()
    blank = jnp.zeros((HALF_WIN, COLS), BF16)
    qx[low : low + HALF_WIN] = blank
    qx[high - HALF_WIN : high] = blank
    start = phase[0] * (ROWS // WIN)
    window = (lax.broadcasted_iota(jnp.int32, (half, HD), 0) + base + HALF_WIN) // WIN
    is_open = jnp.zeros((half, HD), F32)
    for w in range(low // WIN, high // WIN):
        flag = jnp.where(opened[0, start + w] == 1, 1.0, 0.0)
        is_open = jnp.where(window == w, flag, is_open)
    ones = jnp.ones((MEM, HD), BF16)
    copies[0].wait()
    copies[1].wait()
    for h in range(HEADS):
        c = slice(h * HD, (h + 1) * HD)
        keys = memory[:, :PART, c].reshape(MEM, HD)
        values = memory[:, PART:, c].reshape(MEM, HD)
        own = qx[HALF_WIN + base : HALF_WIN + base + half, c]
        score = lax.dot_general(own, keys, (((1,), (1,)), ((), ())), preferred_element_type=F32)
        weight = jnp.exp2(score * SCALE2).astype(BF16)
        result = jnp.dot(weight, jnp.concatenate([values, ones], axis=1), preferred_element_type=F32)
        top[:, c] = is_open * result[:, :HD]
        bottom[:, c] = is_open * result[:, HD:]
    for copy in copies[2:]:
        copy.wait()
    for d in range(used):
        at = HALF_WIN + MEM + d * PART
        kx[at : at + PART] = tail[d, :PART]
        vx[at : at + PART] = tail[d, PART : 2 * PART]
    for begin, size in ((low, half), (low + half, WIN)):
        rows = slice(begin, begin + size)
        window_a = lax.broadcasted_iota(jnp.int32, (size, size), 0) // WIN
        window_b = lax.broadcasted_iota(jnp.int32, (size, size), 1) // WIN
        allowed = (window_a == window_b) & (frame_row[:, rows] <= frame_column[rows, :1])
        begin_own, end_own = max(begin, low + HALF_WIN), min(begin + size, high - HALF_WIN)
        to = slice(begin_own - HALF_WIN - base, end_own - HALF_WIN - base)
        for h in range(HEADS):
            c = slice(h * HD, (h + 1) * HD)
            score = lax.dot_general(qx[rows, c], kx[rows, c], (((1,), (1,)), ((), ())), preferred_element_type=F32)
            weight = jnp.where(allowed, jnp.exp2(score * SCALE2), 0.0).astype(BF16)
            both = jnp.concatenate([vx[rows, c], jnp.ones((size, HD), BF16)], axis=1)
            cut = jnp.dot(weight, both, preferred_element_type=F32)[begin_own - begin : end_own - begin]
            above, below = top[to, c] + cut[:, :HD], bottom[to, c] + cut[:, HD:]
            out[to, c] = (above / below).astype(BF16)


def attention(r, phase, opened, *operands):
    smem = pl.BlockSpec(memory_space=pltpu.SMEM)
    hbm = pl.BlockSpec(memory_space=pl.ANY)
    half = ROWS // 2
    extended = pltpu.VMEM((EXT, COLS), BF16)
    return pl.pallas_call(
        functools.partial(attend_kernel, r),
        out_shape=shape((half, COLS), BF16),
        in_specs=[smem, smem] + [hbm] * len(operands),
        out_specs=pl.BlockSpec(memory_space=pltpu.VMEM),
        scratch_shapes=[
            pltpu.VMEM((half, COLS), F32),
            pltpu.VMEM((half, COLS), F32),
            extended,
            extended,
            extended,
            pltpu.VMEM((PARTS, PAYLOAD, COLS), BF16),
            pltpu.VMEM((1, EXT), jnp.int32),
            pltpu.VMEM((EXT, HD), jnp.int32),
            pltpu.VMEM((PARTS, 2 * PART, COLS), BF16),
            pltpu.SemaphoreType.DMA((9,)),
        ],
        cost_estimate=pl.CostEstimate(
            flops=2 * ROWS * (MEM + half) * COLS * 2, bytes_accessed=1500000, transcendentals=0
        ),
        compiler_params=pltpu.CompilerParams(vmem_limit_bytes=ATTEND_LIMIT),
        name=f"attention_{r}",
    )(phase, opened, *operands)


def joined_rows(core, pair, whole):
    half = pair[0].shape[0]
    for which, part in ((core[0], pair[0]), (1 - core[0], pair[1])):
        whole[pl.ds(pl.multiple_of(which * half, half), half)] = part[...]


def near_kernel(r, core, lat, own, right, left, w_own, w_right, w_right_2, w_left, w_left_2, total, whole, whole_2):
    rows = total.shape[0]
    sums = lat[r * rows : (r + 1) * rows].astype(F32)
    sums = sums + jnp.dot(own[...], w_own[...], preferred_element_type=F32)
    joined_rows(core, (w_right, w_right_2), whole)
    joined_rows(core, (w_left, w_left_2), whole_2)
    for a, w in ((right, whole), (left, whole_2)):
        sums = sums + jnp.dot(a[...], w[...], preferred_element_type=F32)
    total[...] = sums


def far_kernel(core, total, part, w, w_2, *refs):
    out, whole = refs[-2:]
    joined_rows(core, (w, w_2), whole)
    out[...] = (total[...] + jnp.dot(part[...], whole[...], preferred_element_type=F32)).astype(BF16)


def far(r, core, total, part, pair, earlier=None):
    rows, share = total.shape
    vmem = pl.BlockSpec(memory_space=pltpu.VMEM)
    operands = [core, total, part, *pair]
    specs, aliases = [pl.BlockSpec(memory_space=pltpu.SMEM)] + [vmem] * 4, {}
    if earlier is not None:
        operands.append(earlier)
        specs.append(pl.BlockSpec(memory_space=pl.ANY))
        aliases = {5: 0}
    return pl.pallas_call(
        far_kernel,
        grid=(1,),
        in_specs=specs,
        out_specs=pl.BlockSpec((rows, share), lambda i: (r, 0)),
        out_shape=shape((ROWS, share), BF16),
        scratch_shapes=[pltpu.VMEM((COLS, share), BF16)],
        input_output_aliases=aliases,
        cost_estimate=pl.CostEstimate(flops=2 * rows * COLS * share, bytes_accessed=1500000, transcendentals=0),
        compiler_params=pltpu.CompilerParams(vmem_limit_bytes=LIMIT),
        name=f"far_projection_{r}",
    )(*operands)


def moved(x, axis, by):
    size = lax.axis_size(axis)
    return lax.ppermute(x, axis, [(i, (i + by) % size) for i in range(size)])


def swapped(x, axis, bit):
    return lax.ppermute(x, axis, [(i, i ^ bit) for i in range(lax.axis_size(axis))])


def local(latents, w_qkv, w_out, decay, frame_ids, memory_mask):
    phase = lax.axis_index("phase")
    mp = lax.axis_index("mp")
    phase_ref = phase.reshape(1).astype(jnp.int32)
    w3 = jnp.transpose(w_qkv, (1, 0, 2))

    z_ref = lax.axis_index("z").reshape(1).astype(jnp.int32)
    payload = tails(phase_ref, decay[0], latents, w3)
    arrived = lax.all_to_all(payload, PLANE, 0, 0, tiled=True)

    w_out, payload = lax.optimization_barrier((w_out, payload))
    share = w_out.shape[1] // 4
    offsets = (0, 1, -1, 2)
    core = lax.axis_index("core")
    deep = COLS // 2
    own_weight = lax.dynamic_slice_in_dim(w_out, mp * share, share, 1)
    sends = [
        lax.dynamic_slice(w_out, (core * deep, ((mp + by) & 3) * share), (deep, share)) for by in offsets[1:]
    ]
    weights = [moved(piece, "mp", by) for by, piece in zip(offsets[1:], sends)]
    arrived, _ = lax.optimization_barrier((arrived, sends))
    half_keys = shape((MEM, COLS), BF16)

    wide = shape((2 * PART + 8, COLS), F32)
    packed = shape((PAYLOAD, COLS), BF16)
    plain = shape((2 * PART, COLS), BF16)
    plain_all = shape((PARTS, 2 * PART, COLS), BF16)
    own, sent = vmem_call(plane_kernel, (wide, packed), "plane_total", 1000000, (arrived,))
    after, sent = lax.optimization_barrier((z_ref, sent))
    got_1 = swapped(sent, "z", 1)
    head_values = heads(head_values_kernel, half_keys, "head_values", after, latents, w3)
    got_1, head_values = lax.optimization_barrier((got_1, head_values))

    sent = vmem_call(first_kernel, packed, "through_1", 100000, (z_ref, own, got_1), smem=1)
    after, sent = lax.optimization_barrier((phase_ref, sent))
    got_2 = swapped(sent, "z", 2)
    head_keys, edge = heads(
        head_keys_kernel, (half_keys, plain), "head_keys", after, latents, w3, head_values, payload
    )
    got_2, head_keys, edge = lax.optimization_barrier((got_2, head_keys, edge))

    sent = vmem_call(next_kernel, plain, "through_3", 100000, (z_ref, own, got_1, got_2), smem=1)
    latents, sent, edge = lax.optimization_barrier((latents, sent, edge))
    got_4 = swapped(sent, "z", 7)
    halo = swapped(edge, "phase", 1)
    own_columns = lax.dynamic_slice_in_dim(latents, mp * share, share, 1)
    got_4, own_columns, halo, weights = lax.optimization_barrier((got_4, own_columns, halo, weights))
    memory = vmem_call(
        memory_kernel, plain_all, "section_memory", 1000000, (z_ref, got_1, got_2, got_4, arrived), smem=1
    )
    after, memory, frame_ids = lax.optimization_barrier((z_ref, memory, frame_ids))
    memory = lax.all_to_all(memory, PLANE, 0, 0, tiled=True)
    frames_pad = jnp.pad(frame_ids[0], (HALF_WIN, HALF_WIN), constant_values=outside_frame)
    frames = lax.dynamic_slice_in_dim(frames_pad, phase * ROWS, EXT)
    frame_row = frames.reshape(1, EXT)
    frame_column = jnp.broadcast_to(frames[:, None], (EXT, HD))
    queries = query(after, latents, w3)
    weights = [(half, swapped(half, "core", 1)) for half in weights]
    memory, weights = lax.optimization_barrier((memory, weights))
    core_ref = core.reshape(1).astype(jnp.int32)
    halves = [
        attention(
            r, phase_ref, memory_mask, queries, head_keys, head_values, payload, halo, frame_row, frame_column, memory
        )
        for r in range(2)
    ]
    right = [moved(piece, "mp", 1) for piece in halves]
    left = [moved(piece, "mp", -1) for piece in halves]
    right[1], left[1] = lax.optimization_barrier((right[1], left[1]))
    far_parts = moved(right[0], "mp", 1), moved(left[1], "mp", -1)
    refined = None
    for r in (1, 0):
        total = vmem_call(
            functools.partial(near_kernel, r),
            shape((ROWS // 2, share), F32),
            f"near_projection_{r}",
            3 * ROWS * COLS * share,
            (core_ref, own_columns, halves[r], right[r], left[r], own_weight, *weights[0], *weights[1]),
            smem=1,
            scratch=[pltpu.VMEM((COLS, share), BF16)] * 2,
        )
        refined = far(r, core_ref, total, far_parts[r], weights[2], refined)
    return refined


def solution(mesh):
    finer = Mesh(
        mesh.devices.reshape(8, 2, 2, mesh.shape["mp"], mesh.shape["phase"]),
        ("z", "y", "core", "mp", "phase"),
    )
    placed = (
        P((*SPAN, "phase"), None),
        P(None, None, "mp"),
        P("mp", None),
        P(SPAN, None, "mp"),
        P(SPAN, None),
        P(SPAN, None),
    )
    return jax.shard_map(
        local, mesh=finer, in_specs=placed, out_specs=P((*SPAN, "phase"), "mp"), check_vma=False
    )
```

```python
import functools

import jax
import jax.numpy as jnp
from jax import lax
from jax.experimental import pallas as pl
from jax.experimental.pallas import tpu as pltpu
from jax.sharding import Mesh
from jax.sharding import PartitionSpec as P

HD = 128
WIN = 64
HALF_WIN = 32
MEM = 256
ROWS = 512
EXT = ROWS + WIN
HEADS = 3
COLS = HEADS * HD
PARTS = 8
PART = MEM // PARTS
PAYLOAD = 2 * PART + 8
CHUNKS = 5
TAIL_LIMIT = 60 * 1024 * 1024
REST_LIMIT = 60 * 1024 * 1024
ATTEND_LIMIT = 53 * 1024 * 1024
QUERY_LIMIT = 60 * 1024 * 1024
LIMIT = 32 * 1024 * 1024
SPAN = ("z", "y", "core")
PLANE = ("y", "core", "phase")

outside_frame = 1048576
epsilon = 1e-06
F32 = jnp.float32
BF16 = jnp.bfloat16
SCALE2 = HD ** (-0.5) * 1.4426950408889634


def shape(dims, dtype):
    return jax.ShapeDtypeStruct(dims, dtype)


def normed(x):
    heads = []
    for h in range(HEADS):
        part = x[:, h * HD : (h + 1) * HD]
        square = jnp.mean(part * part, axis=-1, keepdims=True)
        heads.append(part * lax.rsqrt(square + epsilon))
    return jnp.concatenate(heads, axis=1).astype(BF16)


def pieces_of(row):
    full = jnp.broadcast_to(row, (8, COLS))
    high = full.astype(BF16).astype(F32)
    middle = (full - high).astype(BF16).astype(F32)
    low = full - high - middle
    at = lax.broadcasted_iota(jnp.int32, (8, COLS), 0)
    return jnp.where(at == 0, high, jnp.where(at == 1, middle, jnp.where(at == 2, low, 0.0))).astype(BF16)


def row_of(pieces):
    wide = pieces.astype(F32)
    return wide[0:1] + wide[1:2] + wide[2:3]


def project_kernel(phase, decay, lat, w, out, head_keys, head_values, edge, rows, wkv, acc, sems):
    depth = lat.shape[1]
    step = depth // CHUNKS
    copies = []
    for k in range(CHUNKS):
        at = pl.ds(k * step, step)
        group = [
            pltpu.make_async_copy(lat.at[:, at], rows.at[:, at], sems.at[3 * k]),
            pltpu.make_async_copy(w.at[1, at], wkv.at[at, pl.ds(0, COLS)], sems.at[3 * k + 1]),
            pltpu.make_async_copy(w.at[2, at], wkv.at[at, pl.ds(COLS, COLS)], sems.at[3 * k + 2]),
        ]
        for copy in group:
            copy.start()
        copies.append(group)
    for k, group in enumerate(copies):
        for copy in group:
            copy.wait()
        at = slice(k * step, (k + 1) * step)
        part = jnp.dot(rows[:, at], wkv[at], preferred_element_type=F32)
        if k == 0:
            acc[...] = part
        else:
            acc[...] += part
    keys = normed(acc[:, :COLS])
    values = acc[:, COLS:].astype(BF16)
    head_keys[...] = keys[:MEM]
    head_values[...] = values[:MEM]
    first = phase[0] == 0
    edge[:PART] = jnp.where(first, keys[ROWS - PART :], keys[:PART])
    edge[PART:] = jnp.where(first, values[ROWS - PART :], values[:PART])
    rates = [jnp.where(first, decay[0, h], decay[1, h]) for h in range(HEADS)]
    lane = lax.broadcasted_iota(jnp.int32, (1, COLS), 1)
    row = jnp.where(lane < HD, rates[0], jnp.where(lane < 2 * HD, rates[1], rates[2]))
    tile = pieces_of(row)
    for d in range(PARTS):
        at = ROWS - MEM + d * PART
        out[d, :PART] = keys[at : at + PART]
        out[d, PART : 2 * PART] = values[at : at + PART]
        out[d, 2 * PART :] = tile


def project(phase, decay, latents, w3):
    depth = latents.shape[1]
    smem = pl.BlockSpec(memory_space=pltpu.SMEM)
    vmem = pl.BlockSpec(memory_space=pltpu.VMEM)
    hbm = pl.BlockSpec(memory_space=pl.ANY)
    return pl.pallas_call(
        project_kernel,
        out_shape=(
            shape((PARTS, PAYLOAD, COLS), BF16),
            shape((MEM, COLS), BF16),
            shape((MEM, COLS), BF16),
            shape((2 * PART, COLS), BF16),
        ),
        in_specs=[smem, smem, hbm, hbm],
        out_specs=(vmem,) * 4,
        scratch_shapes=[
            pltpu.VMEM((ROWS, depth), BF16),
            pltpu.VMEM((depth, 2 * COLS), BF16),
            pltpu.VMEM((ROWS, 2 * COLS), F32),
            pltpu.SemaphoreType.DMA((3 * CHUNKS,)),
        ],
        cost_estimate=pl.CostEstimate(flops=2 * ROWS * depth * 2 * COLS, bytes_accessed=7000000, transcendentals=0),
        compiler_params=pltpu.CompilerParams(vmem_limit_bytes=TAIL_LIMIT),
        name="key_value_projection",
    )(phase, decay, latents, w3)


def call_on_hbm(kernel, outs, name, flops, nbytes, args, scratch, limit=REST_LIMIT):
    vmem = pl.BlockSpec(memory_space=pltpu.VMEM)
    hbm = pl.BlockSpec(memory_space=pl.ANY)
    single = not isinstance(outs, tuple)
    return pl.pallas_call(
        kernel,
        out_shape=outs,
        in_specs=[pl.BlockSpec(memory_space=pltpu.SMEM)] + [hbm] * (len(args) - 1),
        out_specs=vmem if single else tuple(vmem for _ in outs),
        scratch_shapes=scratch,
        cost_estimate=pl.CostEstimate(flops=flops, bytes_accessed=nbytes, transcendentals=0),
        compiler_params=pltpu.CompilerParams(vmem_limit_bytes=limit),
        name=name,
    )(*args)


def query_kernel(after, lat, w, out, rows, part, sems):
    copies = [
        pltpu.make_async_copy(w.at[0], part, sems.at[0]),
        pltpu.make_async_copy(lat.at[pl.ds(0, MEM)], rows.at[pl.ds(0, MEM)], sems.at[1]),
        pltpu.make_async_copy(lat.at[pl.ds(MEM, MEM)], rows.at[pl.ds(MEM, MEM)], sems.at[2]),
    ]
    for copy in copies:
        copy.start()
    copies[0].wait()
    for r in range(2):
        copies[1 + r].wait()
        at = slice(r * MEM, (r + 1) * MEM)
        out[at] = normed(jnp.dot(rows[at], part[...], preferred_element_type=F32))


def query(after, latents, w3):
    depth = latents.shape[1]
    return call_on_hbm(
        query_kernel,
        shape((ROWS, COLS), BF16),
        "query_projection",
        2 * ROWS * depth * COLS,
        4600000,
        (after, latents, w3),
        [pltpu.VMEM((ROWS, depth), BF16), pltpu.VMEM((depth, COLS), BF16), pltpu.SemaphoreType.DMA((3,))],
        QUERY_LIMIT,
    )


def vmem_call(kernel, outs, name, flops, args, smem=0, scratch=()):
    specs = [pl.BlockSpec(memory_space=pltpu.SMEM)] * smem
    specs += [pl.BlockSpec(memory_space=pltpu.VMEM)] * (len(args) - smem)
    single = not isinstance(outs, tuple)
    out_spec = pl.BlockSpec(memory_space=pltpu.VMEM)
    nbytes = sum(a.size * a.dtype.itemsize for a in args)
    return pl.pallas_call(
        kernel,
        out_shape=outs,
        in_specs=specs,
        out_specs=out_spec if single else tuple(out_spec for _ in outs),
        scratch_shapes=list(scratch),
        cost_estimate=pl.CostEstimate(flops=flops, bytes_accessed=nbytes, transcendentals=0),
        compiler_params=pltpu.CompilerParams(vmem_limit_bytes=LIMIT),
        name=name,
    )(*args)


def coefficients(rate):
    return 1.0 - rate, jnp.sqrt(1.0 - rate * rate)


def pack(out, state, row):
    out[: 2 * PART] = state.astype(BF16)
    out[2 * PART :] = pieces_of(row)


def keep(out, state, row):
    out[: 2 * PART] = state
    out[2 * PART :] = jnp.broadcast_to(row, (8, COLS))


def plane_step(keys, values, rate, tail_keys, tail_values):
    for_keys, for_values = coefficients(rate)
    return (
        rate * keys + for_keys * tail_keys.astype(F32),
        rate * values + for_values * tail_values.astype(F32),
    )


def plane_kernel(arrived, state, payload):
    keys = values = jnp.zeros((PART, COLS), F32)
    total = jnp.ones((1, COLS), F32)
    for i in range(PARTS):
        rate = row_of(arrived[i, 2 * PART :])
        keys, values = plane_step(keys, values, rate, arrived[i, :PART], arrived[i, PART : 2 * PART])
        total = total * rate
    both = jnp.concatenate([keys, values], axis=0)
    keep(state, both, total)
    pack(payload, both, total)


def joined(upper, mine, rate, got):
    other, other_rate = got[: 2 * PART].astype(F32), row_of(got[2 * PART :])
    return jnp.where(upper, mine + rate * other, other + other_rate * mine), rate * other_rate


def first_kernel(z, own, got_1, payload):
    total, rate = joined((z[0] & 1) == 1, own[: 2 * PART], own[2 * PART : 2 * PART + 1], got_1)
    pack(payload, total, rate)


def next_kernel(z, own, got_1, got_2, payload):
    total, rate = joined((z[0] & 1) == 1, own[: 2 * PART], own[2 * PART : 2 * PART + 1], got_1)
    total, rate = joined((z[0] & 2) == 2, total, rate, got_2)
    payload[...] = total.astype(BF16)


def memory_kernel(z, got_1, got_2, got_4, arrived, out):
    at_1, at_2, at_4 = (z[0] & 1) == 1, (z[0] & 2) == 2, (z[0] & 4) == 4
    entering = jnp.where(at_1, got_1[: 2 * PART].astype(F32), 0.0)
    rate = jnp.where(at_1, row_of(got_1[2 * PART :]), 1.0)
    entering = jnp.where(at_2, entering + rate * got_2[: 2 * PART].astype(F32), entering)
    rate = jnp.where(at_2, rate * row_of(got_2[2 * PART :]), rate)
    entering = jnp.where(at_4, entering + rate * got_4[...].astype(F32), entering)
    keys, values = entering[:PART], entering[PART:]
    for i in range(PARTS):
        out[i, :PART] = keys.astype(BF16)
        out[i, PART:] = values.astype(BF16)
        if i < PARTS - 1:
            rate = row_of(arrived[i, 2 * PART :])
            keys, values = plane_step(keys, values, rate, arrived[i, :PART], arrived[i, PART : 2 * PART])


def attend_kernel(
    r, phase, opened, q, head_keys, head_values, tail_rows, halo, rows_in, columns_in, memory_in,
    out, top, bottom, qx, kx, vx, tail, frame_row, frame_column, memory, sems,
):
    half = ROWS // 2
    base = r * half
    low, high = base, base + half + WIN
    first, second = pl.ds(0, PART), pl.ds(PART, PART)
    seen = pl.ds(low, high - low)
    used = 1 if r == 0 else PARTS
    pairs = [
        (q.at[pl.ds(base, half)], qx.at[pl.ds(HALF_WIN + base, half)]),
        (memory_in, memory),
        (tail_rows.at[pl.ds(0, used)], tail.at[pl.ds(0, used)]),
        (rows_in, frame_row),
        (columns_in.at[seen], frame_column.at[seen]),
    ]
    if r == 0:
        edge, head, source = pl.ds(0, HALF_WIN), pl.ds(HALF_WIN, MEM), pl.ds(0, MEM)
    else:
        edge, head, source = pl.ds(HALF_WIN + ROWS, HALF_WIN), pl.ds(low, HALF_WIN), pl.ds(MEM - HALF_WIN, HALF_WIN)
    pairs += [
        (head_keys.at[source], kx.at[head]),
        (head_values.at[source], vx.at[head]),
        (halo.at[first], kx.at[edge]),
        (halo.at[second], vx.at[edge]),
    ]
    copies = [pltpu.make_async_copy(a, b, sems.at[i]) for i, (a, b) in enumerate(pairs)]
    for copy in copies:
        copy.start()
    blank = jnp.zeros((HALF_WIN, COLS), BF16)
    qx[low : low + HALF_WIN] = blank
    qx[high - HALF_WIN : high] = blank
    start = phase[0] * (ROWS // WIN)
    window = (lax.broadcasted_iota(jnp.int32, (half, HD), 0) + base + HALF_WIN) // WIN
    is_open = jnp.zeros((half, HD), F32)
    for w in range(low // WIN, high // WIN):
        flag = jnp.where(opened[0, start + w] == 1, 1.0, 0.0)
        is_open = jnp.where(window == w, flag, is_open)
    ones = jnp.ones((MEM, HD), BF16)
    copies[0].wait()
    copies[1].wait()
    for h in range(HEADS):
        c = slice(h * HD, (h + 1) * HD)
        keys = memory[:, :PART, c].reshape(MEM, HD)
        values = memory[:, PART:, c].reshape(MEM, HD)
        own = qx[HALF_WIN + base : HALF_WIN + base + half, c]
        score = lax.dot_general(own, keys, (((1,), (1,)), ((), ())), preferred_element_type=F32)
        weight = jnp.exp2(score * SCALE2).astype(BF16)
        result = jnp.dot(weight, jnp.concatenate([values, ones], axis=1), preferred_element_type=F32)
        top[:, c] = is_open * result[:, :HD]
        bottom[:, c] = is_open * result[:, HD:]
    for copy in copies[2:]:
        copy.wait()
    for d in range(used):
        at = HALF_WIN + MEM + d * PART
        kx[at : at + PART] = tail[d, :PART]
        vx[at : at + PART] = tail[d, PART : 2 * PART]
    for begin, size in ((low, half), (low + half, WIN)):
        rows = slice(begin, begin + size)
        window_a = lax.broadcasted_iota(jnp.int32, (size, size), 0) // WIN
        window_b = lax.broadcasted_iota(jnp.int32, (size, size), 1) // WIN
        allowed = (window_a == window_b) & (frame_row[:, rows] <= frame_column[rows, :1])
        begin_own, end_own = max(begin, low + HALF_WIN), min(begin + size, high - HALF_WIN)
        to = slice(begin_own - HALF_WIN - base, end_own - HALF_WIN - base)
        for h in range(HEADS):
            c = slice(h * HD, (h + 1) * HD)
            score = lax.dot_general(qx[rows, c], kx[rows, c], (((1,), (1,)), ((), ())), preferred_element_type=F32)
            weight = jnp.where(allowed, jnp.exp2(score * SCALE2), 0.0).astype(BF16)
            both = jnp.concatenate([vx[rows, c], jnp.ones((size, HD), BF16)], axis=1)
            cut = jnp.dot(weight, both, preferred_element_type=F32)[begin_own - begin : end_own - begin]
            above, below = top[to, c] + cut[:, :HD], bottom[to, c] + cut[:, HD:]
            out[to, c] = (above / below).astype(BF16)


def attention(r, phase, opened, *operands):
    smem = pl.BlockSpec(memory_space=pltpu.SMEM)
    hbm = pl.BlockSpec(memory_space=pl.ANY)
    half = ROWS // 2
    extended = pltpu.VMEM((EXT, COLS), BF16)
    return pl.pallas_call(
        functools.partial(attend_kernel, r),
        out_shape=shape((half, COLS), BF16),
        in_specs=[smem, smem] + [hbm] * len(operands),
        out_specs=pl.BlockSpec(memory_space=pltpu.VMEM),
        scratch_shapes=[
            pltpu.VMEM((half, COLS), F32),
            pltpu.VMEM((half, COLS), F32),
            extended,
            extended,
            extended,
            pltpu.VMEM((PARTS, PAYLOAD, COLS), BF16),
            pltpu.VMEM((1, EXT), jnp.int32),
            pltpu.VMEM((EXT, HD), jnp.int32),
            pltpu.VMEM((PARTS, 2 * PART, COLS), BF16),
            pltpu.SemaphoreType.DMA((9,)),
        ],
        cost_estimate=pl.CostEstimate(
            flops=2 * ROWS * (MEM + half) * COLS * 2, bytes_accessed=1500000, transcendentals=0
        ),
        compiler_params=pltpu.CompilerParams(vmem_limit_bytes=ATTEND_LIMIT),
        name=f"attention_{r}",
    )(phase, opened, *operands)


def joined_rows(core, pair, whole):
    half = pair[0].shape[0]
    for which, part in ((core[0], pair[0]), (1 - core[0], pair[1])):
        whole[pl.ds(pl.multiple_of(which * half, half), half)] = part[...]


def near_kernel(r, core, lat, own, right, left, w_own, w_right, w_right_2, w_left, w_left_2, total, whole, whole_2):
    rows = total.shape[0]
    sums = lat[r * rows : (r + 1) * rows].astype(F32)
    sums = sums + jnp.dot(own[...], w_own[...], preferred_element_type=F32)
    joined_rows(core, (w_right, w_right_2), whole)
    joined_rows(core, (w_left, w_left_2), whole_2)
    for a, w in ((right, whole), (left, whole_2)):
        sums = sums + jnp.dot(a[...], w[...], preferred_element_type=F32)
    total[...] = sums


def far_kernel(core, total, part, w, w_2, *refs):
    out, whole = refs[-2:]
    joined_rows(core, (w, w_2), whole)
    out[...] = (total[...] + jnp.dot(part[...], whole[...], preferred_element_type=F32)).astype(BF16)


def far(r, core, total, part, pair, earlier=None):
    rows, share = total.shape
    vmem = pl.BlockSpec(memory_space=pltpu.VMEM)
    operands = [core, total, part, *pair]
    specs, aliases = [pl.BlockSpec(memory_space=pltpu.SMEM)] + [vmem] * 4, {}
    if earlier is not None:
        operands.append(earlier)
        specs.append(pl.BlockSpec(memory_space=pl.ANY))
        aliases = {5: 0}
    return pl.pallas_call(
        far_kernel,
        grid=(1,),
        in_specs=specs,
        out_specs=pl.BlockSpec((rows, share), lambda i: (r, 0)),
        out_shape=shape((ROWS, share), BF16),
        scratch_shapes=[pltpu.VMEM((COLS, share), BF16)],
        input_output_aliases=aliases,
        cost_estimate=pl.CostEstimate(flops=2 * rows * COLS * share, bytes_accessed=1500000, transcendentals=0),
        compiler_params=pltpu.CompilerParams(vmem_limit_bytes=LIMIT),
        name=f"far_projection_{r}",
    )(*operands)


def moved(x, axis, by):
    size = lax.axis_size(axis)
    return lax.ppermute(x, axis, [(i, (i + by) % size) for i in range(size)])


def swapped(x, axis, bit):
    return lax.ppermute(x, axis, [(i, i ^ bit) for i in range(lax.axis_size(axis))])


def local(latents, w_qkv, w_out, decay, frame_ids, memory_mask):
    phase = lax.axis_index("phase")
    mp = lax.axis_index("mp")
    phase_ref = phase.reshape(1).astype(jnp.int32)
    w3 = jnp.transpose(w_qkv, (1, 0, 2))

    z_ref = lax.axis_index("z").reshape(1).astype(jnp.int32)
    payload, head_keys, head_values, edge = project(phase_ref, decay[0], latents, w3)
    arrived = lax.all_to_all(payload, PLANE, 0, 0, tiled=True)

    w_out, payload = lax.optimization_barrier((w_out, payload))
    share = w_out.shape[1] // 4
    offsets = (0, 1, -1, 2)
    core = lax.axis_index("core")
    deep = COLS // 2
    sends = [
        lax.dynamic_slice(w_out, (core * deep, ((mp + by) & 3) * share), (deep, share)) for by in offsets[1:]
    ]
    weights = [moved(piece, "mp", by) for by, piece in zip(offsets[1:], sends)]
    halo = swapped(edge, "phase", 1)
    arrived, _, halo = lax.optimization_barrier((arrived, sends, halo))

    wide = shape((2 * PART + 8, COLS), F32)
    packed = shape((PAYLOAD, COLS), BF16)
    plain = shape((2 * PART, COLS), BF16)
    plain_all = shape((PARTS, 2 * PART, COLS), BF16)
    own, sent = vmem_call(plane_kernel, (wide, packed), "plane_total", 1000000, (arrived,))
    latents, sent = lax.optimization_barrier((latents, sent))
    got_1 = swapped(sent, "z", 1)
    own_columns = lax.dynamic_slice_in_dim(latents, mp * share, share, 1)
    got_1, own_columns = lax.optimization_barrier((got_1, own_columns))

    sent = vmem_call(first_kernel, packed, "through_1", 100000, (z_ref, own, got_1), smem=1)
    w_out, sent = lax.optimization_barrier((w_out, sent))
    got_2 = swapped(sent, "z", 2)
    own_weight = lax.dynamic_slice_in_dim(w_out, mp * share, share, 1)
    got_2, own_weight = lax.optimization_barrier((got_2, own_weight))

    sent = vmem_call(next_kernel, plain, "through_3", 100000, (z_ref, own, got_1, got_2), smem=1)
    got_4 = swapped(sent, "z", 7)
    got_4, weights = lax.optimization_barrier((got_4, weights))
    memory = vmem_call(
        memory_kernel, plain_all, "section_memory", 1000000, (z_ref, got_1, got_2, got_4, arrived), smem=1
    )
    after, memory, frame_ids = lax.optimization_barrier((z_ref, memory, frame_ids))
    memory = lax.all_to_all(memory, PLANE, 0, 0, tiled=True)
    frames_pad = jnp.pad(frame_ids[0], (HALF_WIN, HALF_WIN), constant_values=outside_frame)
    frames = lax.dynamic_slice_in_dim(frames_pad, phase * ROWS, EXT)
    frame_row = frames.reshape(1, EXT)
    frame_column = jnp.broadcast_to(frames[:, None], (EXT, HD))
    queries = query(after, latents, w3)
    weights = [(half, swapped(half, "core", 1)) for half in weights]
    memory, weights = lax.optimization_barrier((memory, weights))
    core_ref = core.reshape(1).astype(jnp.int32)
    halves = [
        attention(
            r, phase_ref, memory_mask, queries, head_keys, head_values, payload, halo, frame_row, frame_column, memory
        )
        for r in range(2)
    ]
    right = [moved(piece, "mp", 1) for piece in halves]
    left = [moved(piece, "mp", -1) for piece in halves]
    right[1], left[1] = lax.optimization_barrier((right[1], left[1]))
    far_parts = moved(right[0], "mp", 1), moved(left[1], "mp", -1)
    refined = None
    for r in (1, 0):
        total = vmem_call(
            functools.partial(near_kernel, r),
            shape((ROWS // 2, share), F32),
            f"near_projection_{r}",
            3 * ROWS * COLS * share,
            (core_ref, own_columns, halves[r], right[r], left[r], own_weight, *weights[0], *weights[1]),
            smem=1,
            scratch=[pltpu.VMEM((COLS, share), BF16)] * 2,
        )
        refined = far(r, core_ref, total, far_parts[r], weights[2], refined)
    return refined


def solution(mesh):
    finer = Mesh(
        mesh.devices.reshape(8, 2, 2, mesh.shape["mp"], mesh.shape["phase"]),
        ("z", "y", "core", "mp", "phase"),
    )
    placed = (
        P((*SPAN, "phase"), None),
        P(None, None, "mp"),
        P("mp", None),
        P(SPAN, None, "mp"),
        P(SPAN, None),
        P(SPAN, None),
    )
    return jax.shard_map(
        local, mesh=finer, in_specs=placed, out_specs=P((*SPAN, "phase"), "mp"), check_vma=False
    )
```

```python
import functools

import jax
import jax.numpy as jnp
from jax import lax
from jax.experimental import pallas as pl
from jax.experimental.pallas import tpu as pltpu
from jax.sharding import Mesh
from jax.sharding import PartitionSpec as P

HD = 128
WIN = 64
HALF_WIN = 32
MEM = 256
ROWS = 512
EXT = ROWS + WIN
HEADS = 3
COLS = HEADS * HD
PARTS = 8
PART = MEM // PARTS
PAYLOAD = 2 * PART + 8
CHUNKS = 5
TAIL_LIMIT = 60 * 1024 * 1024
REST_LIMIT = 60 * 1024 * 1024
ATTEND_LIMIT = 53 * 1024 * 1024
QUERY_LIMIT = 60 * 1024 * 1024
LIMIT = 32 * 1024 * 1024
SPAN = ("z", "y", "core")
PLANE = ("y", "core", "phase")

outside_frame = 1048576
epsilon = 1e-06
F32 = jnp.float32
BF16 = jnp.bfloat16
SCALE2 = HD ** (-0.5) * 1.4426950408889634


def shape(dims, dtype):
    return jax.ShapeDtypeStruct(dims, dtype)


def normed(x):
    heads = []
    for h in range(HEADS):
        part = x[:, h * HD : (h + 1) * HD]
        square = jnp.mean(part * part, axis=-1, keepdims=True)
        heads.append(part * lax.rsqrt(square + epsilon))
    return jnp.concatenate(heads, axis=1).astype(BF16)


def pieces_of(row):
    full = jnp.broadcast_to(row, (8, COLS))
    high = full.astype(BF16).astype(F32)
    middle = (full - high).astype(BF16).astype(F32)
    low = full - high - middle
    at = lax.broadcasted_iota(jnp.int32, (8, COLS), 0)
    return jnp.where(at == 0, high, jnp.where(at == 1, middle, jnp.where(at == 2, low, 0.0))).astype(BF16)


def row_of(pieces):
    wide = pieces.astype(F32)
    return wide[0:1] + wide[1:2] + wide[2:3]


def project_kernel(phase, decay, lat, w, out, head_keys, head_values, edge, rows, wkv, acc, sems):
    depth = lat.shape[1]
    step = depth // CHUNKS
    copies = []
    for k in range(CHUNKS):
        at = pl.ds(k * step, step)
        group = [
            pltpu.make_async_copy(lat.at[:, at], rows.at[:, at], sems.at[3 * k]),
            pltpu.make_async_copy(w.at[1, at], wkv.at[at, pl.ds(0, COLS)], sems.at[3 * k + 1]),
            pltpu.make_async_copy(w.at[2, at], wkv.at[at, pl.ds(COLS, COLS)], sems.at[3 * k + 2]),
        ]
        for copy in group:
            copy.start()
        copies.append(group)
    for k, group in enumerate(copies):
        for copy in group:
            copy.wait()
        at = slice(k * step, (k + 1) * step)
        part = jnp.dot(rows[:, at], wkv[at], preferred_element_type=F32)
        if k == 0:
            acc[...] = part
        else:
            acc[...] += part
    keys = normed(acc[:, :COLS])
    values = acc[:, COLS:].astype(BF16)
    head_keys[...] = keys[:MEM]
    head_values[...] = values[:MEM]
    first = phase[0] == 0
    edge[:PART] = jnp.where(first, keys[ROWS - PART :], keys[:PART])
    edge[PART:] = jnp.where(first, values[ROWS - PART :], values[:PART])
    rates = [jnp.where(first, decay[0, h], decay[1, h]) for h in range(HEADS)]
    lane = lax.broadcasted_iota(jnp.int32, (1, COLS), 1)
    row = jnp.where(lane < HD, rates[0], jnp.where(lane < 2 * HD, rates[1], rates[2]))
    tile = pieces_of(row)
    for d in range(PARTS):
        at = ROWS - MEM + d * PART
        out[d, :PART] = keys[at : at + PART]
        out[d, PART : 2 * PART] = values[at : at + PART]
        out[d, 2 * PART :] = tile


def project(phase, decay, latents, w3):
    depth = latents.shape[1]
    smem = pl.BlockSpec(memory_space=pltpu.SMEM)
    vmem = pl.BlockSpec(memory_space=pltpu.VMEM)
    hbm = pl.BlockSpec(memory_space=pl.ANY)
    return pl.pallas_call(
        project_kernel,
        out_shape=(
            shape((PARTS, PAYLOAD, COLS), BF16),
            shape((MEM, COLS), BF16),
            shape((MEM, COLS), BF16),
            shape((2 * PART, COLS), BF16),
        ),
        in_specs=[smem, smem, hbm, hbm],
        out_specs=(vmem,) * 4,
        scratch_shapes=[
            pltpu.VMEM((ROWS, depth), BF16),
            pltpu.VMEM((depth, 2 * COLS), BF16),
            pltpu.VMEM((ROWS, 2 * COLS), F32),
            pltpu.SemaphoreType.DMA((3 * CHUNKS,)),
        ],
        cost_estimate=pl.CostEstimate(flops=2 * ROWS * depth * 2 * COLS, bytes_accessed=7000000, transcendentals=0),
        compiler_params=pltpu.CompilerParams(vmem_limit_bytes=TAIL_LIMIT),
        name="key_value_projection",
    )(phase, decay, latents, w3)


def call_on_hbm(kernel, outs, name, flops, nbytes, args, scratch, limit=REST_LIMIT):
    vmem = pl.BlockSpec(memory_space=pltpu.VMEM)
    hbm = pl.BlockSpec(memory_space=pl.ANY)
    single = not isinstance(outs, tuple)
    return pl.pallas_call(
        kernel,
        out_shape=outs,
        in_specs=[pl.BlockSpec(memory_space=pltpu.SMEM)] + [hbm] * (len(args) - 1),
        out_specs=vmem if single else tuple(vmem for _ in outs),
        scratch_shapes=scratch,
        cost_estimate=pl.CostEstimate(flops=flops, bytes_accessed=nbytes, transcendentals=0),
        compiler_params=pltpu.CompilerParams(vmem_limit_bytes=limit),
        name=name,
    )(*args)


def query_kernel(after, lat, w, out, rows, part, sems):
    copies = [
        pltpu.make_async_copy(w.at[0], part, sems.at[0]),
        pltpu.make_async_copy(lat.at[pl.ds(0, MEM)], rows.at[pl.ds(0, MEM)], sems.at[1]),
        pltpu.make_async_copy(lat.at[pl.ds(MEM, MEM)], rows.at[pl.ds(MEM, MEM)], sems.at[2]),
    ]
    for copy in copies:
        copy.start()
    copies[0].wait()
    for r in range(2):
        copies[1 + r].wait()
        at = slice(r * MEM, (r + 1) * MEM)
        out[at] = normed(jnp.dot(rows[at], part[...], preferred_element_type=F32))


def query(after, latents, w3):
    depth = latents.shape[1]
    return call_on_hbm(
        query_kernel,
        shape((ROWS, COLS), BF16),
        "query_projection",
        2 * ROWS * depth * COLS,
        4600000,
        (after, latents, w3),
        [pltpu.VMEM((ROWS, depth), BF16), pltpu.VMEM((depth, COLS), BF16), pltpu.SemaphoreType.DMA((3,))],
        QUERY_LIMIT,
    )


def vmem_call(kernel, outs, name, flops, args, smem=0, scratch=()):
    specs = [pl.BlockSpec(memory_space=pltpu.SMEM)] * smem
    specs += [pl.BlockSpec(memory_space=pltpu.VMEM)] * (len(args) - smem)
    single = not isinstance(outs, tuple)
    out_spec = pl.BlockSpec(memory_space=pltpu.VMEM)
    nbytes = sum(a.size * a.dtype.itemsize for a in args)
    return pl.pallas_call(
        kernel,
        out_shape=outs,
        in_specs=specs,
        out_specs=out_spec if single else tuple(out_spec for _ in outs),
        scratch_shapes=list(scratch),
        cost_estimate=pl.CostEstimate(flops=flops, bytes_accessed=nbytes, transcendentals=0),
        compiler_params=pltpu.CompilerParams(vmem_limit_bytes=LIMIT),
        name=name,
    )(*args)


def coefficients(rate):
    return 1.0 - rate, jnp.sqrt(1.0 - rate * rate)


def pack(out, state, row):
    out[: 2 * PART] = state.astype(BF16)
    out[2 * PART :] = pieces_of(row)


def keep(out, state, row):
    out[: 2 * PART] = state
    out[2 * PART :] = jnp.broadcast_to(row, (8, COLS))


def plane_step(keys, values, rate, tail_keys, tail_values):
    for_keys, for_values = coefficients(rate)
    return (
        rate * keys + for_keys * tail_keys.astype(F32),
        rate * values + for_values * tail_values.astype(F32),
    )


def plane_kernel(arrived, state, payload):
    keys = values = jnp.zeros((PART, COLS), F32)
    total = jnp.ones((1, COLS), F32)
    for i in range(PARTS):
        rate = row_of(arrived[i, 2 * PART :])
        keys, values = plane_step(keys, values, rate, arrived[i, :PART], arrived[i, PART : 2 * PART])
        total = total * rate
    both = jnp.concatenate([keys, values], axis=0)
    keep(state, both, total)
    pack(payload, both, total)


def joined(upper, mine, rate, got):
    other, other_rate = got[: 2 * PART].astype(F32), row_of(got[2 * PART :])
    return jnp.where(upper, mine + rate * other, other + other_rate * mine), rate * other_rate


def first_kernel(z, own, got_1, payload):
    total, rate = joined((z[0] & 1) == 1, own[: 2 * PART], own[2 * PART : 2 * PART + 1], got_1)
    pack(payload, total, rate)


def next_kernel(z, own, got_1, got_2, payload):
    total, rate = joined((z[0] & 1) == 1, own[: 2 * PART], own[2 * PART : 2 * PART + 1], got_1)
    total, rate = joined((z[0] & 2) == 2, total, rate, got_2)
    payload[...] = total.astype(BF16)


def memory_kernel(z, got_1, got_2, got_4, arrived, out):
    at_1, at_2, at_4 = (z[0] & 1) == 1, (z[0] & 2) == 2, (z[0] & 4) == 4
    entering = jnp.where(at_1, got_1[: 2 * PART].astype(F32), 0.0)
    rate = jnp.where(at_1, row_of(got_1[2 * PART :]), 1.0)
    entering = jnp.where(at_2, entering + rate * got_2[: 2 * PART].astype(F32), entering)
    rate = jnp.where(at_2, rate * row_of(got_2[2 * PART :]), rate)
    entering = jnp.where(at_4, entering + rate * got_4[...].astype(F32), entering)
    keys, values = entering[:PART], entering[PART:]
    for i in range(PARTS):
        out[i, :PART] = keys.astype(BF16)
        out[i, PART:] = values.astype(BF16)
        if i < PARTS - 1:
            rate = row_of(arrived[i, 2 * PART :])
            keys, values = plane_step(keys, values, rate, arrived[i, :PART], arrived[i, PART : 2 * PART])


def attend_kernel(
    r, phase, opened, q, head_keys, head_values, tail_rows, halo, rows_in, columns_in, memory_in,
    out, top, bottom, qx, kx, vx, tail, frame_row, frame_column, memory, sems,
):
    half = ROWS // 2
    base = r * half
    low, high = base, base + half + WIN
    first, second = pl.ds(0, PART), pl.ds(PART, PART)
    seen = pl.ds(low, high - low)
    used = 1 if r == 0 else PARTS
    pairs = [
        (q.at[pl.ds(base, half)], qx.at[pl.ds(HALF_WIN + base, half)]),
        (memory_in, memory),
        (tail_rows.at[pl.ds(0, used)], tail.at[pl.ds(0, used)]),
        (rows_in, frame_row),
        (columns_in.at[seen], frame_column.at[seen]),
    ]
    if r == 0:
        edge, head, source = pl.ds(0, HALF_WIN), pl.ds(HALF_WIN, MEM), pl.ds(0, MEM)
    else:
        edge, head, source = pl.ds(HALF_WIN + ROWS, HALF_WIN), pl.ds(low, HALF_WIN), pl.ds(MEM - HALF_WIN, HALF_WIN)
    pairs += [
        (head_keys.at[source], kx.at[head]),
        (head_values.at[source], vx.at[head]),
        (halo.at[first], kx.at[edge]),
        (halo.at[second], vx.at[edge]),
    ]
    copies = [pltpu.make_async_copy(a, b, sems.at[i]) for i, (a, b) in enumerate(pairs)]
    for copy in copies:
        copy.start()
    blank = jnp.zeros((HALF_WIN, COLS), BF16)
    qx[low : low + HALF_WIN] = blank
    qx[high - HALF_WIN : high] = blank
    start = phase[0] * (ROWS // WIN)
    window = (lax.broadcasted_iota(jnp.int32, (half, HD), 0) + base + HALF_WIN) // WIN
    is_open = jnp.zeros((half, HD), F32)
    for w in range(low // WIN, high // WIN):
        flag = jnp.where(opened[0, start + w] == 1, 1.0, 0.0)
        is_open = jnp.where(window == w, flag, is_open)
    ones = jnp.ones((MEM, HD), BF16)
    copies[0].wait()
    copies[1].wait()
    for h in range(HEADS):
        c = slice(h * HD, (h + 1) * HD)
        keys = memory[:, :PART, c].reshape(MEM, HD)
        values = memory[:, PART:, c].reshape(MEM, HD)
        own = qx[HALF_WIN + base : HALF_WIN + base + half, c]
        score = lax.dot_general(own, keys, (((1,), (1,)), ((), ())), preferred_element_type=F32)
        weight = jnp.exp2(score * SCALE2).astype(BF16)
        result = jnp.dot(weight, jnp.concatenate([values, ones], axis=1), preferred_element_type=F32)
        top[:, c] = is_open * result[:, :HD]
        bottom[:, c] = is_open * result[:, HD:]
    for copy in copies[2:]:
        copy.wait()
    for d in range(used):
        at = HALF_WIN + MEM + d * PART
        kx[at : at + PART] = tail[d, :PART]
        vx[at : at + PART] = tail[d, PART : 2 * PART]
    for begin, size in ((low, half), (low + half, WIN)):
        rows = slice(begin, begin + size)
        window_a = lax.broadcasted_iota(jnp.int32, (size, size), 0) // WIN
        window_b = lax.broadcasted_iota(jnp.int32, (size, size), 1) // WIN
        allowed = (window_a == window_b) & (frame_row[:, rows] <= frame_column[rows, :1])
        begin_own, end_own = max(begin, low + HALF_WIN), min(begin + size, high - HALF_WIN)
        to = slice(begin_own - HALF_WIN - base, end_own - HALF_WIN - base)
        for h in range(HEADS):
            c = slice(h * HD, (h + 1) * HD)
            score = lax.dot_general(qx[rows, c], kx[rows, c], (((1,), (1,)), ((), ())), preferred_element_type=F32)
            weight = jnp.where(allowed, jnp.exp2(score * SCALE2), 0.0).astype(BF16)
            both = jnp.concatenate([vx[rows, c], jnp.ones((size, HD), BF16)], axis=1)
            cut = jnp.dot(weight, both, preferred_element_type=F32)[begin_own - begin : end_own - begin]
            above, below = top[to, c] + cut[:, :HD], bottom[to, c] + cut[:, HD:]
            out[to, c] = (above / below).astype(BF16)


def attention(r, phase, opened, *operands):
    smem = pl.BlockSpec(memory_space=pltpu.SMEM)
    hbm = pl.BlockSpec(memory_space=pl.ANY)
    half = ROWS // 2
    extended = pltpu.VMEM((EXT, COLS), BF16)
    return pl.pallas_call(
        functools.partial(attend_kernel, r),
        out_shape=shape((half, COLS), BF16),
        in_specs=[smem, smem] + [hbm] * len(operands),
        out_specs=pl.BlockSpec(memory_space=pltpu.VMEM),
        scratch_shapes=[
            pltpu.VMEM((half, COLS), F32),
            pltpu.VMEM((half, COLS), F32),
            extended,
            extended,
            extended,
            pltpu.VMEM((PARTS, PAYLOAD, COLS), BF16),
            pltpu.VMEM((1, EXT), jnp.int32),
            pltpu.VMEM((EXT, HD), jnp.int32),
            pltpu.VMEM((PARTS, 2 * PART, COLS), BF16),
            pltpu.SemaphoreType.DMA((9,)),
        ],
        cost_estimate=pl.CostEstimate(
            flops=2 * ROWS * (MEM + half) * COLS * 2, bytes_accessed=1500000, transcendentals=0
        ),
        compiler_params=pltpu.CompilerParams(vmem_limit_bytes=ATTEND_LIMIT),
        name=f"attention_{r}",
    )(phase, opened, *operands)


def joined_rows(core, pair, whole):
    half = pair[0].shape[0]
    for which, part in ((core[0], pair[0]), (1 - core[0], pair[1])):
        whole[pl.ds(pl.multiple_of(which * half, half), half)] = part[...]


def near_kernel(r, core, lat, own, right, left, w_own, w_right, w_right_2, w_left, w_left_2, total, whole, whole_2):
    rows = total.shape[0]
    sums = lat[r * rows : (r + 1) * rows].astype(F32)
    sums = sums + jnp.dot(own[...], w_own[...], preferred_element_type=F32)
    joined_rows(core, (w_right, w_right_2), whole)
    joined_rows(core, (w_left, w_left_2), whole_2)
    for a, w in ((right, whole), (left, whole_2)):
        sums = sums + jnp.dot(a[...], w[...], preferred_element_type=F32)
    total[...] = sums


def far_kernel(core, total, part, w, w_2, *refs):
    out, whole = refs[-2:]
    joined_rows(core, (w, w_2), whole)
    out[...] = (total[...] + jnp.dot(part[...], whole[...], preferred_element_type=F32)).astype(BF16)


def far(r, core, total, part, pair, earlier=None):
    rows, share = total.shape
    vmem = pl.BlockSpec(memory_space=pltpu.VMEM)
    operands = [core, total, part, *pair]
    specs, aliases = [pl.BlockSpec(memory_space=pltpu.SMEM)] + [vmem] * 4, {}
    if earlier is not None:
        operands.append(earlier)
        specs.append(pl.BlockSpec(memory_space=pl.ANY))
        aliases = {5: 0}
    return pl.pallas_call(
        far_kernel,
        grid=(1,),
        in_specs=specs,
        out_specs=pl.BlockSpec((rows, share), lambda i: (r, 0)),
        out_shape=shape((ROWS, share), BF16),
        scratch_shapes=[pltpu.VMEM((COLS, share), BF16)],
        input_output_aliases=aliases,
        cost_estimate=pl.CostEstimate(flops=2 * rows * COLS * share, bytes_accessed=1500000, transcendentals=0),
        compiler_params=pltpu.CompilerParams(vmem_limit_bytes=LIMIT),
        name=f"far_projection_{r}",
    )(*operands)


def moved(x, axis, by):
    size = lax.axis_size(axis)
    return lax.ppermute(x, axis, [(i, (i + by) % size) for i in range(size)])


def swapped(x, axis, bit):
    return lax.ppermute(x, axis, [(i, i ^ bit) for i in range(lax.axis_size(axis))])


def local(latents, w_qkv, w_out, decay, frame_ids, memory_mask):
    phase = lax.axis_index("phase")
    mp = lax.axis_index("mp")
    phase_ref = phase.reshape(1).astype(jnp.int32)
    w3 = jnp.transpose(w_qkv, (1, 0, 2))

    z_ref = lax.axis_index("z").reshape(1).astype(jnp.int32)
    payload, head_keys, head_values, edge = project(phase_ref, decay[0], latents, w3)
    arrived = lax.all_to_all(payload, PLANE, 0, 0, tiled=True)

    w_out, payload = lax.optimization_barrier((w_out, payload))
    share = w_out.shape[1] // 4
    offsets = (0, 1, -1, 2)
    core = lax.axis_index("core")
    deep = COLS // 2
    sends = [
        lax.dynamic_slice(w_out, (core * deep, ((mp + by) & 3) * share), (deep, share)) for by in offsets[1:]
    ]
    weights = [moved(piece, "mp", by) for by, piece in zip(offsets[1:], sends)]
    halo = swapped(edge, "phase", 1)
    arrived, _ = lax.optimization_barrier((arrived, sends))

    wide = shape((2 * PART + 8, COLS), F32)
    packed = shape((PAYLOAD, COLS), BF16)
    plain = shape((2 * PART, COLS), BF16)
    plain_all = shape((PARTS, 2 * PART, COLS), BF16)
    own, sent = vmem_call(plane_kernel, (wide, packed), "plane_total", 1000000, (arrived,))
    latents, sent = lax.optimization_barrier((latents, sent))
    got_1 = swapped(sent, "z", 1)
    own_columns = lax.dynamic_slice_in_dim(latents, mp * share, share, 1)
    got_1, own_columns = lax.optimization_barrier((got_1, own_columns))

    sent = vmem_call(first_kernel, packed, "through_1", 100000, (z_ref, own, got_1), smem=1)
    w_out, sent = lax.optimization_barrier((w_out, sent))
    got_2 = swapped(sent, "z", 2)
    own_weight = lax.dynamic_slice_in_dim(w_out, mp * share, share, 1)
    got_2, own_weight, halo = lax.optimization_barrier((got_2, own_weight, halo))

    sent = vmem_call(next_kernel, plain, "through_3", 100000, (z_ref, own, got_1, got_2), smem=1)
    got_4 = lax.ppermute(sent, "z", [(i, 7 - i) for i in range(4)])
    got_4, weights = lax.optimization_barrier((got_4, weights))
    memory = vmem_call(
        memory_kernel, plain_all, "section_memory", 1000000, (z_ref, got_1, got_2, got_4, arrived), smem=1
    )
    after, memory, frame_ids = lax.optimization_barrier((z_ref, memory, frame_ids))
    memory = lax.all_to_all(memory, PLANE, 0, 0, tiled=True)
    frames_pad = jnp.pad(frame_ids[0], (HALF_WIN, HALF_WIN), constant_values=outside_frame)
    frames = lax.dynamic_slice_in_dim(frames_pad, phase * ROWS, EXT)
    frame_row = frames.reshape(1, EXT)
    frame_column = jnp.broadcast_to(frames[:, None], (EXT, HD))
    queries = query(after, latents, w3)
    weights = [(half, swapped(half, "core", 1)) for half in weights]
    memory, weights = lax.optimization_barrier((memory, weights))
    core_ref = core.reshape(1).astype(jnp.int32)
    halves = [
        attention(
            r, phase_ref, memory_mask, queries, head_keys, head_values, payload, halo, frame_row, frame_column, memory
        )
        for r in range(2)
    ]
    right = [moved(piece, "mp", 1) for piece in halves]
    left = [moved(piece, "mp", -1) for piece in halves]
    right[1], left[1] = lax.optimization_barrier((right[1], left[1]))
    far_parts = moved(right[0], "mp", 1), moved(left[1], "mp", -1)
    refined = None
    for r in (1, 0):
        total = vmem_call(
            functools.partial(near_kernel, r),
            shape((ROWS // 2, share), F32),
            f"near_projection_{r}",
            3 * ROWS * COLS * share,
            (core_ref, own_columns, halves[r], right[r], left[r], own_weight, *weights[0], *weights[1]),
            smem=1,
            scratch=[pltpu.VMEM((COLS, share), BF16)] * 2,
        )
        refined = far(r, core_ref, total, far_parts[r], weights[2], refined)
    return refined


def solution(mesh):
    finer = Mesh(
        mesh.devices.reshape(8, 2, 2, mesh.shape["mp"], mesh.shape["phase"]),
        ("z", "y", "core", "mp", "phase"),
    )
    placed = (
        P((*SPAN, "phase"), None),
        P(None, None, "mp"),
        P("mp", None),
        P(SPAN, None, "mp"),
        P(SPAN, None),
        P(SPAN, None),
    )
    return jax.shard_map(
        local, mesh=finer, in_specs=placed, out_specs=P((*SPAN, "phase"), "mp"), check_vma=False
    )
```

```python
import functools

import jax
import jax.numpy as jnp
from jax import lax
from jax.experimental import pallas as pl
from jax.experimental.pallas import tpu as pltpu
from jax.sharding import Mesh
from jax.sharding import PartitionSpec as P

HD = 128
WIN = 64
HALF_WIN = 32
MEM = 256
ROWS = 512
EXT = ROWS + WIN
HEADS = 3
COLS = HEADS * HD
PARTS = 8
PART = MEM // PARTS
PAYLOAD = 2 * PART + 8
CHUNKS = 5
TAIL_LIMIT = 60 * 1024 * 1024
REST_LIMIT = 60 * 1024 * 1024
ATTEND_LIMIT = 53 * 1024 * 1024
LIMIT = 32 * 1024 * 1024
SPAN = ("z", "y", "core")
PLANE = ("y", "core", "phase")

outside_frame = 1048576
epsilon = 1e-06
F32 = jnp.float32
BF16 = jnp.bfloat16
SCALE2 = HD ** (-0.5) * 1.4426950408889634


def shape(dims, dtype):
    return jax.ShapeDtypeStruct(dims, dtype)


def normed(x):
    heads = []
    for h in range(HEADS):
        part = x[:, h * HD : (h + 1) * HD]
        square = jnp.mean(part * part, axis=-1, keepdims=True)
        heads.append(part * lax.rsqrt(square + epsilon))
    return jnp.concatenate(heads, axis=1).astype(BF16)


def pieces_of(row):
    full = jnp.broadcast_to(row, (8, COLS))
    high = full.astype(BF16).astype(F32)
    middle = (full - high).astype(BF16).astype(F32)
    low = full - high - middle
    at = lax.broadcasted_iota(jnp.int32, (8, COLS), 0)
    return jnp.where(at == 0, high, jnp.where(at == 1, middle, jnp.where(at == 2, low, 0.0))).astype(BF16)


def row_of(pieces):
    wide = pieces.astype(F32)
    return wide[0:1] + wide[1:2] + wide[2:3]


def tail_kernel(phase, decay, lat, w, out, edge, tail, wkv, acc, sems):
    depth = lat.shape[1]
    step = depth // CHUNKS
    copies = []
    for k in range(CHUNKS):
        at = pl.ds(k * step, step)
        group = [
            pltpu.make_async_copy(lat.at[pl.ds(MEM, MEM), at], tail.at[pl.ds(0, MEM), at], sems.at[4 * k]),
            pltpu.make_async_copy(lat.at[pl.ds(0, PART), at], tail.at[pl.ds(MEM, PART), at], sems.at[4 * k + 1]),
            pltpu.make_async_copy(w.at[1, at], wkv.at[at, pl.ds(0, COLS)], sems.at[4 * k + 2]),
            pltpu.make_async_copy(w.at[2, at], wkv.at[at, pl.ds(COLS, COLS)], sems.at[4 * k + 3]),
        ]
        for copy in group:
            copy.start()
        copies.append(group)
    for k, group in enumerate(copies):
        for copy in group:
            copy.wait()
        at = slice(k * step, (k + 1) * step)
        part = jnp.dot(tail[:, at], wkv[at], preferred_element_type=F32)
        if k == 0:
            acc[...] = part
        else:
            acc[...] += part
    keys = normed(acc[:, :COLS])
    values = acc[:, COLS:].astype(BF16)
    first = phase[0] == 0
    last, lead = slice(MEM - PART, MEM), slice(MEM, MEM + PART)
    edge[:PART] = jnp.where(first, keys[last], keys[lead])
    edge[PART:] = jnp.where(first, values[last], values[lead])
    rates = [jnp.where(first, decay[0, h], decay[1, h]) for h in range(HEADS)]
    lane = lax.broadcasted_iota(jnp.int32, (1, COLS), 1)
    row = jnp.where(lane < HD, rates[0], jnp.where(lane < 2 * HD, rates[1], rates[2]))
    tile = pieces_of(row)
    for d in range(PARTS):
        out[d, :PART] = keys[d * PART : (d + 1) * PART]
        out[d, PART : 2 * PART] = values[d * PART : (d + 1) * PART]
        out[d, 2 * PART :] = tile


def tails(phase, decay, latents, w3):
    depth = latents.shape[1]
    smem = pl.BlockSpec(memory_space=pltpu.SMEM)
    vmem = pl.BlockSpec(memory_space=pltpu.VMEM)
    hbm = pl.BlockSpec(memory_space=pl.ANY)
    return pl.pallas_call(
        tail_kernel,
        out_shape=(shape((PARTS, PAYLOAD, COLS), BF16), shape((2 * PART, COLS), BF16)),
        in_specs=[smem, smem, hbm, hbm],
        out_specs=(vmem, vmem),
        scratch_shapes=[
            pltpu.VMEM((MEM + PART, depth), BF16),
            pltpu.VMEM((depth, 2 * COLS), BF16),
            pltpu.VMEM((MEM + PART, 2 * COLS), F32),
            pltpu.SemaphoreType.DMA((4 * CHUNKS,)),
        ],
        cost_estimate=pl.CostEstimate(flops=2 * MEM * depth * 2 * COLS, bytes_accessed=5500000, transcendentals=0),
        compiler_params=pltpu.CompilerParams(vmem_limit_bytes=TAIL_LIMIT),
        name="tail_projection",
    )(phase, decay, latents, w3)


def call_on_hbm(kernel, outs, name, flops, nbytes, args, scratch):
    vmem = pl.BlockSpec(memory_space=pltpu.VMEM)
    hbm = pl.BlockSpec(memory_space=pl.ANY)
    single = not isinstance(outs, tuple)
    return pl.pallas_call(
        kernel,
        out_shape=outs,
        in_specs=[pl.BlockSpec(memory_space=pltpu.SMEM)] + [hbm] * (len(args) - 1),
        out_specs=vmem if single else tuple(vmem for _ in outs),
        scratch_shapes=scratch,
        cost_estimate=pl.CostEstimate(flops=flops, bytes_accessed=nbytes, transcendentals=0),
        compiler_params=pltpu.CompilerParams(vmem_limit_bytes=REST_LIMIT),
        name=name,
    )(*args)


def head_project(which, lat, w, rows, part, sems):
    copies = [
        pltpu.make_async_copy(w.at[which], part, sems.at[0]),
        pltpu.make_async_copy(lat.at[pl.ds(0, MEM)], rows, sems.at[1]),
    ]
    for copy in copies:
        copy.start()
    for copy in copies:
        copy.wait()
    return jnp.dot(rows[...], part[...], preferred_element_type=F32)


def head_values_kernel(after, lat, w, out, rows, part, sems):
    out[...] = head_project(2, lat, w, rows, part, sems).astype(BF16)


def head_keys_kernel(after, lat, w, out, rows, part, sems):
    out[...] = normed(head_project(1, lat, w, rows, part, sems))


def heads(kernel, name, after, latents, w3):
    depth = latents.shape[1]
    return call_on_hbm(
        kernel,
        shape((MEM, COLS), BF16),
        name,
        2 * MEM * depth * COLS,
        3300000,
        (after, latents, w3),
        [pltpu.VMEM((MEM, depth), BF16), pltpu.VMEM((depth, COLS), BF16), pltpu.SemaphoreType.DMA((2,))],
    )


def query_kernel(after, lat, w, out, rows, part, sems):
    copies = [
        pltpu.make_async_copy(w.at[0], part, sems.at[0]),
        pltpu.make_async_copy(lat.at[pl.ds(0, MEM)], rows.at[pl.ds(0, MEM)], sems.at[1]),
        pltpu.make_async_copy(lat.at[pl.ds(MEM, MEM)], rows.at[pl.ds(MEM, MEM)], sems.at[2]),
    ]
    for copy in copies:
        copy.start()
    copies[0].wait()
    for r in range(2):
        copies[1 + r].wait()
        at = slice(r * MEM, (r + 1) * MEM)
        out[at] = normed(jnp.dot(rows[at], part[...], preferred_element_type=F32))


def query(after, latents, w3):
    depth = latents.shape[1]
    return call_on_hbm(
        query_kernel,
        shape((ROWS, COLS), BF16),
        "query_projection",
        2 * ROWS * depth * COLS,
        4600000,
        (after, latents, w3),
        [pltpu.VMEM((ROWS, depth), BF16), pltpu.VMEM((depth, COLS), BF16), pltpu.SemaphoreType.DMA((3,))],
    )


def vmem_call(kernel, outs, name, flops, args, smem=0, scratch=()):
    specs = [pl.BlockSpec(memory_space=pltpu.SMEM)] * smem
    specs += [pl.BlockSpec(memory_space=pltpu.VMEM)] * (len(args) - smem)
    single = not isinstance(outs, tuple)
    out_spec = pl.BlockSpec(memory_space=pltpu.VMEM)
    nbytes = sum(a.size * a.dtype.itemsize for a in args)
    return pl.pallas_call(
        kernel,
        out_shape=outs,
        in_specs=specs,
        out_specs=out_spec if single else tuple(out_spec for _ in outs),
        scratch_shapes=list(scratch),
        cost_estimate=pl.CostEstimate(flops=flops, bytes_accessed=nbytes, transcendentals=0),
        compiler_params=pltpu.CompilerParams(vmem_limit_bytes=LIMIT),
        name=name,
    )(*args)


def coefficients(rate):
    return 1.0 - rate, jnp.sqrt(1.0 - rate * rate)


def pack(out, state, row):
    out[: 2 * PART] = state.astype(BF16)
    out[2 * PART :] = pieces_of(row)


def keep(out, state, row):
    out[: 2 * PART] = state
    out[2 * PART :] = jnp.broadcast_to(row, (8, COLS))


def plane_step(keys, values, rate, tail_keys, tail_values):
    for_keys, for_values = coefficients(rate)
    return (
        rate * keys + for_keys * tail_keys.astype(F32),
        rate * values + for_values * tail_values.astype(F32),
    )


def plane_kernel(arrived, state, payload):
    keys = values = jnp.zeros((PART, COLS), F32)
    total = jnp.ones((1, COLS), F32)
    for i in range(PARTS):
        rate = row_of(arrived[i, 2 * PART :])
        keys, values = plane_step(keys, values, rate, arrived[i, :PART], arrived[i, PART : 2 * PART])
        total = total * rate
    both = jnp.concatenate([keys, values], axis=0)
    keep(state, both, total)
    pack(payload, both, total)


def joined(upper, mine, rate, got):
    other, other_rate = got[: 2 * PART].astype(F32), row_of(got[2 * PART :])
    return jnp.where(upper, mine + rate * other, other + other_rate * mine), rate * other_rate


def first_kernel(z, own, got_1, payload):
    total, rate = joined((z[0] & 1) == 1, own[: 2 * PART], own[2 * PART : 2 * PART + 1], got_1)
    pack(payload, total, rate)


def next_kernel(z, own, got_1, got_2, payload):
    total, rate = joined((z[0] & 1) == 1, own[: 2 * PART], own[2 * PART : 2 * PART + 1], got_1)
    total, rate = joined((z[0] & 2) == 2, total, rate, got_2)
    payload[...] = total.astype(BF16)


def memory_kernel(z, got_1, got_2, got_4, arrived, out):
    at_1, at_2, at_4 = (z[0] & 1) == 1, (z[0] & 2) == 2, (z[0] & 4) == 4
    entering = jnp.where(at_1, got_1[: 2 * PART].astype(F32), 0.0)
    rate = jnp.where(at_1, row_of(got_1[2 * PART :]), 1.0)
    entering = jnp.where(at_2, entering + rate * got_2[: 2 * PART].astype(F32), entering)
    rate = jnp.where(at_2, rate * row_of(got_2[2 * PART :]), rate)
    entering = jnp.where(at_4, entering + rate * got_4[...].astype(F32), entering)
    keys, values = entering[:PART], entering[PART:]
    for i in range(PARTS):
        out[i, :PART] = keys.astype(BF16)
        out[i, PART:] = values.astype(BF16)
        if i < PARTS - 1:
            rate = row_of(arrived[i, 2 * PART :])
            keys, values = plane_step(keys, values, rate, arrived[i, :PART], arrived[i, PART : 2 * PART])


def attend_kernel(
    r, phase, opened, q, head_keys, head_values, tail_rows, halo, rows_in, columns_in, memory_in,
    out, top, bottom, qx, kx, vx, tail, frame_row, frame_column, memory, sems,
):
    half = ROWS // 2
    base = r * half
    low, high = base, base + half + WIN
    first, second = pl.ds(0, PART), pl.ds(PART, PART)
    seen = pl.ds(low, high - low)
    used = 1 if r == 0 else PARTS
    pairs = [
        (q.at[pl.ds(base, half)], qx.at[pl.ds(HALF_WIN + base, half)]),
        (memory_in, memory),
        (tail_rows.at[pl.ds(0, used)], tail.at[pl.ds(0, used)]),
        (rows_in, frame_row),
        (columns_in.at[seen], frame_column.at[seen]),
    ]
    if r == 0:
        edge, head, source = pl.ds(0, HALF_WIN), pl.ds(HALF_WIN, MEM), pl.ds(0, MEM)
    else:
        edge, head, source = pl.ds(HALF_WIN + ROWS, HALF_WIN), pl.ds(low, HALF_WIN), pl.ds(MEM - HALF_WIN, HALF_WIN)
    pairs += [
        (head_keys.at[source], kx.at[head]),
        (head_values.at[source], vx.at[head]),
        (halo.at[first], kx.at[edge]),
        (halo.at[second], vx.at[edge]),
    ]
    copies = [pltpu.make_async_copy(a, b, sems.at[i]) for i, (a, b) in enumerate(pairs)]
    for copy in copies:
        copy.start()
    blank = jnp.zeros((HALF_WIN, COLS), BF16)
    qx[low : low + HALF_WIN] = blank
    qx[high - HALF_WIN : high] = blank
    start = phase[0] * (ROWS // WIN)
    window = (lax.broadcasted_iota(jnp.int32, (half, HD), 0) + base + HALF_WIN) // WIN
    is_open = jnp.zeros((half, HD), F32)
    for w in range(low // WIN, high // WIN):
        flag = jnp.where(opened[0, start + w] == 1, 1.0, 0.0)
        is_open = jnp.where(window == w, flag, is_open)
    ones = jnp.ones((MEM, HD), BF16)
    copies[0].wait()
    copies[1].wait()
    for h in range(HEADS):
        c = slice(h * HD, (h + 1) * HD)
        keys = memory[:, :PART, c].reshape(MEM, HD)
        values = memory[:, PART:, c].reshape(MEM, HD)
        own = qx[HALF_WIN + base : HALF_WIN + base + half, c]
        score = lax.dot_general(own, keys, (((1,), (1,)), ((), ())), preferred_element_type=F32)
        weight = jnp.exp2(score * SCALE2).astype(BF16)
        result = jnp.dot(weight, jnp.concatenate([values, ones], axis=1), preferred_element_type=F32)
        top[:, c] = is_open * result[:, :HD]
        bottom[:, c] = is_open * result[:, HD:]
    for copy in copies[2:]:
        copy.wait()
    for d in range(used):
        at = HALF_WIN + MEM + d * PART
        kx[at : at + PART] = tail[d, :PART]
        vx[at : at + PART] = tail[d, PART : 2 * PART]
    for begin, size in ((low, half), (low + half, WIN)):
        rows = slice(begin, begin + size)
        window_a = lax.broadcasted_iota(jnp.int32, (size, size), 0) // WIN
        window_b = lax.broadcasted_iota(jnp.int32, (size, size), 1) // WIN
        allowed = (window_a == window_b) & (frame_row[:, rows] <= frame_column[rows, :1])
        begin_own, end_own = max(begin, low + HALF_WIN), min(begin + size, high - HALF_WIN)
        to = slice(begin_own - HALF_WIN - base, end_own - HALF_WIN - base)
        for h in range(HEADS):
            c = slice(h * HD, (h + 1) * HD)
            score = lax.dot_general(qx[rows, c], kx[rows, c], (((1,), (1,)), ((), ())), preferred_element_type=F32)
            weight = jnp.where(allowed, jnp.exp2(score * SCALE2), 0.0).astype(BF16)
            both = jnp.concatenate([vx[rows, c], jnp.ones((size, HD), BF16)], axis=1)
            cut = jnp.dot(weight, both, preferred_element_type=F32)[begin_own - begin : end_own - begin]
            above, below = top[to, c] + cut[:, :HD], bottom[to, c] + cut[:, HD:]
            out[to, c] = (above / below).astype(BF16)


def attention(r, phase, opened, *operands):
    smem = pl.BlockSpec(memory_space=pltpu.SMEM)
    hbm = pl.BlockSpec(memory_space=pl.ANY)
    half = ROWS // 2
    extended = pltpu.VMEM((EXT, COLS), BF16)
    return pl.pallas_call(
        functools.partial(attend_kernel, r),
        out_shape=shape((half, COLS), BF16),
        in_specs=[smem, smem] + [hbm] * len(operands),
        out_specs=pl.BlockSpec(memory_space=pltpu.VMEM),
        scratch_shapes=[
            pltpu.VMEM((half, COLS), F32),
            pltpu.VMEM((half, COLS), F32),
            extended,
            extended,
            extended,
            pltpu.VMEM((PARTS, PAYLOAD, COLS), BF16),
            pltpu.VMEM((1, EXT), jnp.int32),
            pltpu.VMEM((EXT, HD), jnp.int32),
            pltpu.VMEM((PARTS, 2 * PART, COLS), BF16),
            pltpu.SemaphoreType.DMA((9,)),
        ],
        cost_estimate=pl.CostEstimate(
            flops=2 * ROWS * (MEM + half) * COLS * 2, bytes_accessed=1500000, transcendentals=0
        ),
        compiler_params=pltpu.CompilerParams(vmem_limit_bytes=ATTEND_LIMIT),
        name=f"attention_{r}",
    )(phase, opened, *operands)


def near_kernel(lat, own_0, own_1, right_0, right_1, left_0, left_1, w_own, w_right, w_left, total):
    half = ROWS // 2
    for r, parts in enumerate(((own_0, right_0, left_0), (own_1, right_1, left_1))):
        at = slice(r * half, (r + 1) * half)
        sums = lat[at].astype(F32)
        for a, w in zip(parts, (w_own, w_right, w_left)):
            sums = sums + jnp.dot(a[...], w[...], preferred_element_type=F32)
        total[at] = sums


def far_kernel(total, first, second, w, out):
    half = ROWS // 2
    for r, part in enumerate((first, second)):
        at = slice(r * half, (r + 1) * half)
        out[at] = (total[at] + jnp.dot(part[...], w[...], preferred_element_type=F32)).astype(BF16)


def moved(x, axis, by):
    size = lax.axis_size(axis)
    return lax.ppermute(x, axis, [(i, (i + by) % size) for i in range(size)])


def swapped(x, axis, bit):
    return lax.ppermute(x, axis, [(i, i ^ bit) for i in range(lax.axis_size(axis))])


def local(latents, w_qkv, w_out, decay, frame_ids, memory_mask):
    phase = lax.axis_index("phase")
    mp = lax.axis_index("mp")
    phase_ref = phase.reshape(1).astype(jnp.int32)
    w3 = jnp.transpose(w_qkv, (1, 0, 2))

    z_ref = lax.axis_index("z").reshape(1).astype(jnp.int32)
    payload, edge = tails(phase_ref, decay[0], latents, w3)
    arrived = lax.all_to_all(payload, PLANE, 0, 0, tiled=True)

    w_out, payload = lax.optimization_barrier((w_out, payload))
    share = w_out.shape[1] // 4
    offsets = (0, 1, -1, 2)
    sends = [lax.dynamic_slice_in_dim(w_out, ((mp + by) & 3) * share, share, 1) for by in offsets]
    weights = [moved(piece, "mp", by) if by else piece for by, piece in zip(offsets, sends)]
    arrived, _ = lax.optimization_barrier((arrived, sends))

    wide = shape((2 * PART + 8, COLS), F32)
    packed = shape((PAYLOAD, COLS), BF16)
    plain = shape((2 * PART, COLS), BF16)
    plain_all = shape((PARTS, 2 * PART, COLS), BF16)
    own, sent = vmem_call(plane_kernel, (wide, packed), "plane_total", 1000000, (arrived,))
    latents, sent = lax.optimization_barrier((latents, sent))
    got_1 = swapped(sent, "z", 1)
    halo = swapped(edge, "phase", 1)
    own_columns = lax.dynamic_slice_in_dim(latents, mp * share, share, 1)
    got_1, own_columns, halo = lax.optimization_barrier((got_1, own_columns, halo))

    sent = vmem_call(first_kernel, packed, "through_1", 100000, (z_ref, own, got_1), smem=1)
    after, sent = lax.optimization_barrier((z_ref, sent))
    got_2 = swapped(sent, "z", 2)
    head_values = heads(head_values_kernel, "head_values", after, latents, w3)
    got_2, head_values = lax.optimization_barrier((got_2, head_values))

    sent = vmem_call(next_kernel, plain, "through_3", 100000, (z_ref, own, got_1, got_2), smem=1)
    after, sent = lax.optimization_barrier((z_ref, sent))
    got_4 = swapped(sent, "z", 7)
    head_keys = heads(head_keys_kernel, "head_keys", after, latents, w3)
    got_4, head_keys = lax.optimization_barrier((got_4, head_keys))
    memory = vmem_call(
        memory_kernel, plain_all, "section_memory", 1000000, (z_ref, got_1, got_2, got_4, arrived), smem=1
    )
    after, memory, frame_ids = lax.optimization_barrier((z_ref, memory, frame_ids))
    memory = lax.all_to_all(memory, PLANE, 0, 0, tiled=True)
    frames_pad = jnp.pad(frame_ids[0], (HALF_WIN, HALF_WIN), constant_values=outside_frame)
    frames = lax.dynamic_slice_in_dim(frames_pad, phase * ROWS, EXT)
    frame_row = frames.reshape(1, EXT)
    frame_column = jnp.broadcast_to(frames[:, None], (EXT, HD))
    queries = query(after, latents, w3)
    memory, weights = lax.optimization_barrier((memory, weights))
    halves = [
        attention(
            r, phase_ref, memory_mask, queries, head_keys, head_values, payload, halo, frame_row, frame_column, memory
        )
        for r in range(2)
    ]
    right = [moved(piece, "mp", 1) for piece in halves]
    left = [moved(piece, "mp", -1) for piece in halves]
    right[1], left[1] = lax.optimization_barrier((right[1], left[1]))
    far_1, far_2 = moved(right[0], "mp", 1), moved(left[1], "mp", -1)
    total = vmem_call(
        near_kernel,
        shape((ROWS, share), F32),
        "near_projection",
        6 * ROWS * COLS * share,
        (own_columns, *halves, *right, *left, *weights[:3]),
    )
    return vmem_call(
        far_kernel,
        shape((ROWS, share), BF16),
        "far_projection",
        2 * ROWS * COLS * share,
        (total, far_1, far_2, weights[3]),
    )


def solution(mesh):
    finer = Mesh(
        mesh.devices.reshape(8, 2, 2, mesh.shape["mp"], mesh.shape["phase"]),
        ("z", "y", "core", "mp", "phase"),
    )
    placed = (
        P((*SPAN, "phase"), None),
        P(None, None, "mp"),
        P("mp", None),
        P(SPAN, None, "mp"),
        P(SPAN, None),
        P(SPAN, None),
    )
    return jax.shard_map(
        local, mesh=finer, in_specs=placed, out_specs=P((*SPAN, "phase"), "mp"), check_vma=False
    )
```

```python
import functools

import jax
import jax.numpy as jnp
from jax import lax
from jax.experimental import pallas as pl
from jax.experimental.pallas import tpu as pltpu
from jax.sharding import Mesh
from jax.sharding import PartitionSpec as P

HD = 128
WIN = 64
HALF_WIN = 32
MEM = 256
ROWS = 512
EXT = ROWS + WIN
HEADS = 3
COLS = HEADS * HD
PARTS = 8
PART = MEM // PARTS
PAYLOAD = 2 * PART + 8
CHUNKS = 5
TAIL_LIMIT = 60 * 1024 * 1024
REST_LIMIT = 60 * 1024 * 1024
ATTEND_LIMIT = 53 * 1024 * 1024
LIMIT = 32 * 1024 * 1024
SPAN = ("z", "y", "core")
PLANE = ("y", "core", "phase")

outside_frame = 1048576
epsilon = 1e-06
F32 = jnp.float32
BF16 = jnp.bfloat16
SCALE2 = HD ** (-0.5) * 1.4426950408889634


def shape(dims, dtype):
    return jax.ShapeDtypeStruct(dims, dtype)


def normed(x):
    heads = []
    for h in range(HEADS):
        part = x[:, h * HD : (h + 1) * HD]
        square = jnp.mean(part * part, axis=-1, keepdims=True)
        heads.append(part * lax.rsqrt(square + epsilon))
    return jnp.concatenate(heads, axis=1).astype(BF16)


def pieces_of(row):
    full = jnp.broadcast_to(row, (8, COLS))
    high = full.astype(BF16).astype(F32)
    middle = (full - high).astype(BF16).astype(F32)
    low = full - high - middle
    at = lax.broadcasted_iota(jnp.int32, (8, COLS), 0)
    return jnp.where(at == 0, high, jnp.where(at == 1, middle, jnp.where(at == 2, low, 0.0))).astype(BF16)


def row_of(pieces):
    wide = pieces.astype(F32)
    return wide[0:1] + wide[1:2] + wide[2:3]


def tail_kernel(phase, decay, lat, w, out, edge, tail, wkv, acc, sems):
    depth = lat.shape[1]
    step = depth // CHUNKS
    copies = []
    for k in range(CHUNKS):
        at = pl.ds(k * step, step)
        group = [
            pltpu.make_async_copy(lat.at[pl.ds(MEM, MEM), at], tail.at[pl.ds(0, MEM), at], sems.at[4 * k]),
            pltpu.make_async_copy(lat.at[pl.ds(0, PART), at], tail.at[pl.ds(MEM, PART), at], sems.at[4 * k + 1]),
            pltpu.make_async_copy(w.at[1, at], wkv.at[at, pl.ds(0, COLS)], sems.at[4 * k + 2]),
            pltpu.make_async_copy(w.at[2, at], wkv.at[at, pl.ds(COLS, COLS)], sems.at[4 * k + 3]),
        ]
        for copy in group:
            copy.start()
        copies.append(group)
    for k, group in enumerate(copies):
        for copy in group:
            copy.wait()
        at = slice(k * step, (k + 1) * step)
        part = jnp.dot(tail[:, at], wkv[at], preferred_element_type=F32)
        if k == 0:
            acc[...] = part
        else:
            acc[...] += part
    keys = normed(acc[:, :COLS])
    values = acc[:, COLS:].astype(BF16)
    first = phase[0] == 0
    last, lead = slice(MEM - PART, MEM), slice(MEM, MEM + PART)
    edge[:PART] = jnp.where(first, keys[last], keys[lead])
    edge[PART:] = jnp.where(first, values[last], values[lead])
    rates = [jnp.where(first, decay[0, h], decay[1, h]) for h in range(HEADS)]
    lane = lax.broadcasted_iota(jnp.int32, (1, COLS), 1)
    row = jnp.where(lane < HD, rates[0], jnp.where(lane < 2 * HD, rates[1], rates[2]))
    tile = pieces_of(row)
    for d in range(PARTS):
        out[d, :PART] = keys[d * PART : (d + 1) * PART]
        out[d, PART : 2 * PART] = values[d * PART : (d + 1) * PART]
        out[d, 2 * PART :] = tile


def tails(phase, decay, latents, w3):
    depth = latents.shape[1]
    smem = pl.BlockSpec(memory_space=pltpu.SMEM)
    vmem = pl.BlockSpec(memory_space=pltpu.VMEM)
    hbm = pl.BlockSpec(memory_space=pl.ANY)
    return pl.pallas_call(
        tail_kernel,
        out_shape=(shape((PARTS, PAYLOAD, COLS), BF16), shape((2 * PART, COLS), BF16)),
        in_specs=[smem, smem, hbm, hbm],
        out_specs=(vmem, vmem),
        scratch_shapes=[
            pltpu.VMEM((MEM + PART, depth), BF16),
            pltpu.VMEM((depth, 2 * COLS), BF16),
            pltpu.VMEM((MEM + PART, 2 * COLS), F32),
            pltpu.SemaphoreType.DMA((4 * CHUNKS,)),
        ],
        cost_estimate=pl.CostEstimate(flops=2 * MEM * depth * 2 * COLS, bytes_accessed=5500000, transcendentals=0),
        compiler_params=pltpu.CompilerParams(vmem_limit_bytes=TAIL_LIMIT),
        name="tail_projection",
    )(phase, decay, latents, w3)


def call_on_hbm(kernel, outs, name, flops, nbytes, args, scratch):
    vmem = pl.BlockSpec(memory_space=pltpu.VMEM)
    hbm = pl.BlockSpec(memory_space=pl.ANY)
    single = not isinstance(outs, tuple)
    return pl.pallas_call(
        kernel,
        out_shape=outs,
        in_specs=[pl.BlockSpec(memory_space=pltpu.SMEM)] + [hbm] * (len(args) - 1),
        out_specs=vmem if single else tuple(vmem for _ in outs),
        scratch_shapes=scratch,
        cost_estimate=pl.CostEstimate(flops=flops, bytes_accessed=nbytes, transcendentals=0),
        compiler_params=pltpu.CompilerParams(vmem_limit_bytes=REST_LIMIT),
        name=name,
    )(*args)


def head_project(which, lat, w, rows, part, sems):
    copies = [
        pltpu.make_async_copy(w.at[which], part, sems.at[0]),
        pltpu.make_async_copy(lat.at[pl.ds(0, MEM)], rows, sems.at[1]),
    ]
    for copy in copies:
        copy.start()
    for copy in copies:
        copy.wait()
    return jnp.dot(rows[...], part[...], preferred_element_type=F32)


def head_values_kernel(after, lat, w, out, rows, part, sems):
    out[...] = head_project(2, lat, w, rows, part, sems).astype(BF16)


def head_keys_kernel(after, lat, w, out, rows, part, sems):
    out[...] = normed(head_project(1, lat, w, rows, part, sems))


def heads(kernel, name, after, latents, w3):
    depth = latents.shape[1]
    return call_on_hbm(
        kernel,
        shape((MEM, COLS), BF16),
        name,
        2 * MEM * depth * COLS,
        3300000,
        (after, latents, w3),
        [pltpu.VMEM((MEM, depth), BF16), pltpu.VMEM((depth, COLS), BF16), pltpu.SemaphoreType.DMA((2,))],
    )


def query_kernel(after, lat, w, out, rows, part, sems):
    copies = [
        pltpu.make_async_copy(w.at[0], part, sems.at[0]),
        pltpu.make_async_copy(lat.at[pl.ds(0, MEM)], rows.at[pl.ds(0, MEM)], sems.at[1]),
        pltpu.make_async_copy(lat.at[pl.ds(MEM, MEM)], rows.at[pl.ds(MEM, MEM)], sems.at[2]),
    ]
    for copy in copies:
        copy.start()
    copies[0].wait()
    for r in range(2):
        copies[1 + r].wait()
        at = slice(r * MEM, (r + 1) * MEM)
        out[at] = normed(jnp.dot(rows[at], part[...], preferred_element_type=F32))


def query(after, latents, w3):
    depth = latents.shape[1]
    return call_on_hbm(
        query_kernel,
        shape((ROWS, COLS), BF16),
        "query_projection",
        2 * ROWS * depth * COLS,
        4600000,
        (after, latents, w3),
        [pltpu.VMEM((ROWS, depth), BF16), pltpu.VMEM((depth, COLS), BF16), pltpu.SemaphoreType.DMA((3,))],
    )


def vmem_call(kernel, outs, name, flops, args, smem=0, scratch=()):
    specs = [pl.BlockSpec(memory_space=pltpu.SMEM)] * smem
    specs += [pl.BlockSpec(memory_space=pltpu.VMEM)] * (len(args) - smem)
    single = not isinstance(outs, tuple)
    out_spec = pl.BlockSpec(memory_space=pltpu.VMEM)
    nbytes = sum(a.size * a.dtype.itemsize for a in args)
    return pl.pallas_call(
        kernel,
        out_shape=outs,
        in_specs=specs,
        out_specs=out_spec if single else tuple(out_spec for _ in outs),
        scratch_shapes=list(scratch),
        cost_estimate=pl.CostEstimate(flops=flops, bytes_accessed=nbytes, transcendentals=0),
        compiler_params=pltpu.CompilerParams(vmem_limit_bytes=LIMIT),
        name=name,
    )(*args)


def coefficients(rate):
    return 1.0 - rate, jnp.sqrt(1.0 - rate * rate)


def pack(out, state, row):
    out[: 2 * PART] = state.astype(BF16)
    out[2 * PART :] = pieces_of(row)


def keep(out, state, row):
    out[: 2 * PART] = state
    out[2 * PART :] = jnp.broadcast_to(row, (8, COLS))


def plane_step(keys, values, rate, tail_keys, tail_values):
    for_keys, for_values = coefficients(rate)
    return (
        rate * keys + for_keys * tail_keys.astype(F32),
        rate * values + for_values * tail_values.astype(F32),
    )


def plane_kernel(arrived, state, payload):
    keys = values = jnp.zeros((PART, COLS), F32)
    total = jnp.ones((1, COLS), F32)
    for i in range(PARTS):
        rate = row_of(arrived[i, 2 * PART :])
        keys, values = plane_step(keys, values, rate, arrived[i, :PART], arrived[i, PART : 2 * PART])
        total = total * rate
    both = jnp.concatenate([keys, values], axis=0)
    keep(state, both, total)
    pack(payload, both, total)


def joined(upper, mine, rate, got):
    other, other_rate = got[: 2 * PART].astype(F32), row_of(got[2 * PART :])
    return jnp.where(upper, mine + rate * other, other + other_rate * mine), rate * other_rate


def first_kernel(z, own, got_1, payload):
    total, rate = joined((z[0] & 1) == 1, own[: 2 * PART], own[2 * PART : 2 * PART + 1], got_1)
    pack(payload, total, rate)


def next_kernel(z, own, got_1, got_2, payload):
    total, rate = joined((z[0] & 1) == 1, own[: 2 * PART], own[2 * PART : 2 * PART + 1], got_1)
    total, rate = joined((z[0] & 2) == 2, total, rate, got_2)
    payload[...] = total.astype(BF16)


def memory_kernel(z, got_1, got_2, got_4, arrived, out):
    at_1, at_2, at_4 = (z[0] & 1) == 1, (z[0] & 2) == 2, (z[0] & 4) == 4
    entering = jnp.where(at_1, got_1[: 2 * PART].astype(F32), 0.0)
    rate = jnp.where(at_1, row_of(got_1[2 * PART :]), 1.0)
    entering = jnp.where(at_2, entering + rate * got_2[: 2 * PART].astype(F32), entering)
    rate = jnp.where(at_2, rate * row_of(got_2[2 * PART :]), rate)
    entering = jnp.where(at_4, entering + rate * got_4[...].astype(F32), entering)
    keys, values = entering[:PART], entering[PART:]
    for i in range(PARTS):
        out[i, :PART] = keys.astype(BF16)
        out[i, PART:] = values.astype(BF16)
        if i < PARTS - 1:
            rate = row_of(arrived[i, 2 * PART :])
            keys, values = plane_step(keys, values, rate, arrived[i, :PART], arrived[i, PART : 2 * PART])


def attend_kernel(
    r, phase, opened, q, head_keys, head_values, tail_rows, halo, rows_in, columns_in, memory_in,
    out, top, bottom, qx, kx, vx, tail, frame_row, frame_column, memory, sems,
):
    half = ROWS // 2
    base = r * half
    low, high = base, base + half + WIN
    first, second = pl.ds(0, PART), pl.ds(PART, PART)
    seen = pl.ds(low, high - low)
    used = 1 if r == 0 else PARTS
    pairs = [
        (q.at[pl.ds(base, half)], qx.at[pl.ds(HALF_WIN + base, half)]),
        (memory_in, memory),
        (tail_rows.at[pl.ds(0, used)], tail.at[pl.ds(0, used)]),
        (rows_in, frame_row),
        (columns_in.at[seen], frame_column.at[seen]),
    ]
    if r == 0:
        edge, head, source = pl.ds(0, HALF_WIN), pl.ds(HALF_WIN, MEM), pl.ds(0, MEM)
    else:
        edge, head, source = pl.ds(HALF_WIN + ROWS, HALF_WIN), pl.ds(low, HALF_WIN), pl.ds(MEM - HALF_WIN, HALF_WIN)
    pairs += [
        (head_keys.at[source], kx.at[head]),
        (head_values.at[source], vx.at[head]),
        (halo.at[first], kx.at[edge]),
        (halo.at[second], vx.at[edge]),
    ]
    copies = [pltpu.make_async_copy(a, b, sems.at[i]) for i, (a, b) in enumerate(pairs)]
    for copy in copies:
        copy.start()
    blank = jnp.zeros((HALF_WIN, COLS), BF16)
    qx[low : low + HALF_WIN] = blank
    qx[high - HALF_WIN : high] = blank
    start = phase[0] * (ROWS // WIN)
    window = (lax.broadcasted_iota(jnp.int32, (half, HD), 0) + base + HALF_WIN) // WIN
    is_open = jnp.zeros((half, HD), F32)
    for w in range(low // WIN, high // WIN):
        flag = jnp.where(opened[0, start + w] == 1, 1.0, 0.0)
        is_open = jnp.where(window == w, flag, is_open)
    ones = jnp.ones((MEM, HD), BF16)
    copies[0].wait()
    copies[1].wait()
    for h in range(HEADS):
        c = slice(h * HD, (h + 1) * HD)
        keys = memory[:, :PART, c].reshape(MEM, HD)
        values = memory[:, PART:, c].reshape(MEM, HD)
        own = qx[HALF_WIN + base : HALF_WIN + base + half, c]
        score = lax.dot_general(own, keys, (((1,), (1,)), ((), ())), preferred_element_type=F32)
        weight = jnp.exp2(score * SCALE2).astype(BF16)
        result = jnp.dot(weight, jnp.concatenate([values, ones], axis=1), preferred_element_type=F32)
        top[:, c] = is_open * result[:, :HD]
        bottom[:, c] = is_open * result[:, HD:]
    for copy in copies[2:]:
        copy.wait()
    for d in range(used):
        at = HALF_WIN + MEM + d * PART
        kx[at : at + PART] = tail[d, :PART]
        vx[at : at + PART] = tail[d, PART : 2 * PART]
    for begin, size in ((low, half), (low + half, WIN)):
        rows = slice(begin, begin + size)
        window_a = lax.broadcasted_iota(jnp.int32, (size, size), 0) // WIN
        window_b = lax.broadcasted_iota(jnp.int32, (size, size), 1) // WIN
        allowed = (window_a == window_b) & (frame_row[:, rows] <= frame_column[rows, :1])
        begin_own, end_own = max(begin, low + HALF_WIN), min(begin + size, high - HALF_WIN)
        to = slice(begin_own - HALF_WIN - base, end_own - HALF_WIN - base)
        for h in range(HEADS):
            c = slice(h * HD, (h + 1) * HD)
            score = lax.dot_general(qx[rows, c], kx[rows, c], (((1,), (1,)), ((), ())), preferred_element_type=F32)
            weight = jnp.where(allowed, jnp.exp2(score * SCALE2), 0.0).astype(BF16)
            both = jnp.concatenate([vx[rows, c], jnp.ones((size, HD), BF16)], axis=1)
            cut = jnp.dot(weight, both, preferred_element_type=F32)[begin_own - begin : end_own - begin]
            above, below = top[to, c] + cut[:, :HD], bottom[to, c] + cut[:, HD:]
            out[to, c] = (above / below).astype(BF16)


def attention(r, phase, opened, *operands):
    smem = pl.BlockSpec(memory_space=pltpu.SMEM)
    hbm = pl.BlockSpec(memory_space=pl.ANY)
    half = ROWS // 2
    extended = pltpu.VMEM((EXT, COLS), BF16)
    return pl.pallas_call(
        functools.partial(attend_kernel, r),
        out_shape=shape((half, COLS), BF16),
        in_specs=[smem, smem] + [hbm] * len(operands),
        out_specs=pl.BlockSpec(memory_space=pltpu.VMEM),
        scratch_shapes=[
            pltpu.VMEM((half, COLS), F32),
            pltpu.VMEM((half, COLS), F32),
            extended,
            extended,
            extended,
            pltpu.VMEM((PARTS, PAYLOAD, COLS), BF16),
            pltpu.VMEM((1, EXT), jnp.int32),
            pltpu.VMEM((EXT, HD), jnp.int32),
            pltpu.VMEM((PARTS, 2 * PART, COLS), BF16),
            pltpu.SemaphoreType.DMA((9,)),
        ],
        cost_estimate=pl.CostEstimate(
            flops=2 * ROWS * (MEM + half) * COLS * 2, bytes_accessed=1500000, transcendentals=0
        ),
        compiler_params=pltpu.CompilerParams(vmem_limit_bytes=ATTEND_LIMIT),
        name=f"attention_{r}",
    )(phase, opened, *operands)


def near_kernel(r, lat, own, right, left, w_own, w_right, w_left, total):
    rows = total.shape[0]
    sums = lat[r * rows : (r + 1) * rows].astype(F32)
    for a, w in ((own, w_own), (right, w_right), (left, w_left)):
        sums = sums + jnp.dot(a[...], w[...], preferred_element_type=F32)
    total[...] = sums


def far_kernel(total_0, total_1, first, second, w, out):
    half = ROWS // 2
    for r, (total, part) in enumerate(((total_0, first), (total_1, second))):
        at = slice(r * half, (r + 1) * half)
        out[at] = (total[...] + jnp.dot(part[...], w[...], preferred_element_type=F32)).astype(BF16)


def moved(x, axis, by):
    size = lax.axis_size(axis)
    return lax.ppermute(x, axis, [(i, (i + by) % size) for i in range(size)])


def swapped(x, axis, bit):
    return lax.ppermute(x, axis, [(i, i ^ bit) for i in range(lax.axis_size(axis))])


def local(latents, w_qkv, w_out, decay, frame_ids, memory_mask):
    phase = lax.axis_index("phase")
    mp = lax.axis_index("mp")
    phase_ref = phase.reshape(1).astype(jnp.int32)
    w3 = jnp.transpose(w_qkv, (1, 0, 2))

    z_ref = lax.axis_index("z").reshape(1).astype(jnp.int32)
    payload, edge = tails(phase_ref, decay[0], latents, w3)
    arrived = lax.all_to_all(payload, PLANE, 0, 0, tiled=True)

    w_out, payload = lax.optimization_barrier((w_out, payload))
    share = w_out.shape[1] // 4
    offsets = (0, 1, -1, 2)
    sends = [lax.dynamic_slice_in_dim(w_out, ((mp + by) & 3) * share, share, 1) for by in offsets]
    weights = [moved(piece, "mp", by) if by else piece for by, piece in zip(offsets, sends)]
    arrived, _ = lax.optimization_barrier((arrived, sends))

    wide = shape((2 * PART + 8, COLS), F32)
    packed = shape((PAYLOAD, COLS), BF16)
    plain = shape((2 * PART, COLS), BF16)
    plain_all = shape((PARTS, 2 * PART, COLS), BF16)
    own, sent = vmem_call(plane_kernel, (wide, packed), "plane_total", 1000000, (arrived,))
    latents, sent = lax.optimization_barrier((latents, sent))
    got_1 = swapped(sent, "z", 1)
    halo = swapped(edge, "phase", 1)
    own_columns = lax.dynamic_slice_in_dim(latents, mp * share, share, 1)
    got_1, own_columns, halo = lax.optimization_barrier((got_1, own_columns, halo))

    sent = vmem_call(first_kernel, packed, "through_1", 100000, (z_ref, own, got_1), smem=1)
    after, sent = lax.optimization_barrier((z_ref, sent))
    got_2 = swapped(sent, "z", 2)
    head_values = heads(head_values_kernel, "head_values", after, latents, w3)
    got_2, head_values = lax.optimization_barrier((got_2, head_values))

    sent = vmem_call(next_kernel, plain, "through_3", 100000, (z_ref, own, got_1, got_2), smem=1)
    after, sent = lax.optimization_barrier((z_ref, sent))
    got_4 = swapped(sent, "z", 7)
    head_keys = heads(head_keys_kernel, "head_keys", after, latents, w3)
    got_4, head_keys = lax.optimization_barrier((got_4, head_keys))
    memory = vmem_call(
        memory_kernel, plain_all, "section_memory", 1000000, (z_ref, got_1, got_2, got_4, arrived), smem=1
    )
    after, memory, frame_ids = lax.optimization_barrier((z_ref, memory, frame_ids))
    memory = lax.all_to_all(memory, PLANE, 0, 0, tiled=True)
    frames_pad = jnp.pad(frame_ids[0], (HALF_WIN, HALF_WIN), constant_values=outside_frame)
    frames = lax.dynamic_slice_in_dim(frames_pad, phase * ROWS, EXT)
    frame_row = frames.reshape(1, EXT)
    frame_column = jnp.broadcast_to(frames[:, None], (EXT, HD))
    queries = query(after, latents, w3)
    memory, weights = lax.optimization_barrier((memory, weights))
    halves = [
        attention(
            r, phase_ref, memory_mask, queries, head_keys, head_values, payload, halo, frame_row, frame_column, memory
        )
        for r in range(2)
    ]
    right = [moved(piece, "mp", 1) for piece in halves]
    left = [moved(piece, "mp", -1) for piece in halves]
    right[1], left[1] = lax.optimization_barrier((right[1], left[1]))
    far_2 = moved(left[1], "mp", -1)
    totals = [None, None]
    for r in (1, 0):
        totals[r] = vmem_call(
            functools.partial(near_kernel, r),
            shape((ROWS // 2, share), F32),
            f"near_projection_{r}",
            3 * ROWS * COLS * share,
            (own_columns, halves[r], right[r], left[r], *weights[:3]),
        )
        if r == 1:
            right[0], totals[1] = lax.optimization_barrier((right[0], totals[1]))
            far_1 = moved(right[0], "mp", 1)
    return vmem_call(
        far_kernel,
        shape((ROWS, share), BF16),
        "far_projection",
        2 * ROWS * COLS * share,
        (*totals, far_1, far_2, weights[3]),
    )


def solution(mesh):
    finer = Mesh(
        mesh.devices.reshape(8, 2, 2, mesh.shape["mp"], mesh.shape["phase"]),
        ("z", "y", "core", "mp", "phase"),
    )
    placed = (
        P((*SPAN, "phase"), None),
        P(None, None, "mp"),
        P("mp", None),
        P(SPAN, None, "mp"),
        P(SPAN, None),
        P(SPAN, None),
    )
    return jax.shard_map(
        local, mesh=finer, in_specs=placed, out_specs=P((*SPAN, "phase"), "mp"), check_vma=False
    )
```

```python
import functools

import jax
import jax.numpy as jnp
from jax import lax
from jax.experimental import pallas as pl
from jax.experimental.pallas import tpu as pltpu
from jax.sharding import Mesh
from jax.sharding import PartitionSpec as P

HD = 128
WIN = 64
HALF_WIN = 32
MEM = 256
ROWS = 512
EXT = ROWS + WIN
HEADS = 3
COLS = HEADS * HD
PARTS = 8
PART = MEM // PARTS
PAYLOAD = 2 * PART + 8
CHUNKS = 5
TAIL_LIMIT = 60 * 1024 * 1024
REST_LIMIT = 60 * 1024 * 1024
ATTEND_LIMIT = 53 * 1024 * 1024
LIMIT = 32 * 1024 * 1024
SPAN = ("z", "y", "core")
PLANE = ("y", "core", "phase")

outside_frame = 1048576
epsilon = 1e-06
F32 = jnp.float32
BF16 = jnp.bfloat16
SCALE2 = HD ** (-0.5) * 1.4426950408889634


def shape(dims, dtype):
    return jax.ShapeDtypeStruct(dims, dtype)


def normed(x):
    heads = []
    for h in range(HEADS):
        part = x[:, h * HD : (h + 1) * HD]
        square = jnp.mean(part * part, axis=-1, keepdims=True)
        heads.append(part * lax.rsqrt(square + epsilon))
    return jnp.concatenate(heads, axis=1).astype(BF16)


def pieces_of(row):
    full = jnp.broadcast_to(row, (8, COLS))
    high = full.astype(BF16).astype(F32)
    middle = (full - high).astype(BF16).astype(F32)
    low = full - high - middle
    at = lax.broadcasted_iota(jnp.int32, (8, COLS), 0)
    return jnp.where(at == 0, high, jnp.where(at == 1, middle, jnp.where(at == 2, low, 0.0))).astype(BF16)


def row_of(pieces):
    wide = pieces.astype(F32)
    return wide[0:1] + wide[1:2] + wide[2:3]


def tail_kernel(phase, decay, lat, w, out, tail, wkv, acc, sems):
    depth = lat.shape[1]
    step = depth // CHUNKS
    copies = []
    for k in range(CHUNKS):
        at = pl.ds(k * step, step)
        group = [
            pltpu.make_async_copy(lat.at[pl.ds(MEM, MEM), at], tail.at[:, at], sems.at[3 * k]),
            pltpu.make_async_copy(w.at[1, at], wkv.at[at, pl.ds(0, COLS)], sems.at[3 * k + 1]),
            pltpu.make_async_copy(w.at[2, at], wkv.at[at, pl.ds(COLS, COLS)], sems.at[3 * k + 2]),
        ]
        for copy in group:
            copy.start()
        copies.append(group)
    for k, group in enumerate(copies):
        for copy in group:
            copy.wait()
        at = slice(k * step, (k + 1) * step)
        part = jnp.dot(tail[:, at], wkv[at], preferred_element_type=F32)
        if k == 0:
            acc[...] = part
        else:
            acc[...] += part
    keys = normed(acc[:, :COLS])
    values = acc[:, COLS:].astype(BF16)
    first = phase[0] == 0
    rates = [jnp.where(first, decay[0, h], decay[1, h]) for h in range(HEADS)]
    lane = lax.broadcasted_iota(jnp.int32, (1, COLS), 1)
    row = jnp.where(lane < HD, rates[0], jnp.where(lane < 2 * HD, rates[1], rates[2]))
    tile = pieces_of(row)
    for d in range(PARTS):
        out[d, :PART] = keys[d * PART : (d + 1) * PART]
        out[d, PART : 2 * PART] = values[d * PART : (d + 1) * PART]
        out[d, 2 * PART :] = tile


def tails(phase, decay, latents, w3):
    depth = latents.shape[1]
    smem = pl.BlockSpec(memory_space=pltpu.SMEM)
    vmem = pl.BlockSpec(memory_space=pltpu.VMEM)
    hbm = pl.BlockSpec(memory_space=pl.ANY)
    return pl.pallas_call(
        tail_kernel,
        out_shape=shape((PARTS, PAYLOAD, COLS), BF16),
        in_specs=[smem, smem, hbm, hbm],
        out_specs=vmem,
        scratch_shapes=[
            pltpu.VMEM((MEM, depth), BF16),
            pltpu.VMEM((depth, 2 * COLS), BF16),
            pltpu.VMEM((MEM, 2 * COLS), F32),
            pltpu.SemaphoreType.DMA((3 * CHUNKS,)),
        ],
        cost_estimate=pl.CostEstimate(flops=2 * MEM * depth * 2 * COLS, bytes_accessed=5500000, transcendentals=0),
        compiler_params=pltpu.CompilerParams(vmem_limit_bytes=TAIL_LIMIT),
        name="tail_projection",
    )(phase, decay, latents, w3)


def call_on_hbm(kernel, outs, name, flops, nbytes, args, scratch):
    vmem = pl.BlockSpec(memory_space=pltpu.VMEM)
    hbm = pl.BlockSpec(memory_space=pl.ANY)
    single = not isinstance(outs, tuple)
    return pl.pallas_call(
        kernel,
        out_shape=outs,
        in_specs=[pl.BlockSpec(memory_space=pltpu.SMEM)] + [hbm] * (len(args) - 1),
        out_specs=vmem if single else tuple(vmem for _ in outs),
        scratch_shapes=scratch,
        cost_estimate=pl.CostEstimate(flops=flops, bytes_accessed=nbytes, transcendentals=0),
        compiler_params=pltpu.CompilerParams(vmem_limit_bytes=REST_LIMIT),
        name=name,
    )(*args)


def head_project(which, lat, w, rows, part, sems):
    copies = [
        pltpu.make_async_copy(w.at[which], part, sems.at[0]),
        pltpu.make_async_copy(lat.at[pl.ds(0, MEM)], rows, sems.at[1]),
    ]
    for copy in copies:
        copy.start()
    for copy in copies:
        copy.wait()
    return jnp.dot(rows[...], part[...], preferred_element_type=F32)


def head_values_kernel(after, lat, w, out, rows, part, sems):
    out[...] = head_project(2, lat, w, rows, part, sems).astype(BF16)


def head_keys_kernel(phase, lat, w, values, payload, out, edge, rows, part, first_values, last, sems):
    copies = [
        pltpu.make_async_copy(values.at[pl.ds(0, PART)], first_values, sems.at[2]),
        pltpu.make_async_copy(payload.at[PARTS - 1, pl.ds(0, 2 * PART)], last, sems.at[3]),
    ]
    for copy in copies:
        copy.start()
    keys = normed(head_project(1, lat, w, rows, part, sems))
    out[...] = keys
    for copy in copies:
        copy.wait()
    first = phase[0] == 0
    edge[:PART] = jnp.where(first, last[:PART], keys[:PART])
    edge[PART:] = jnp.where(first, last[PART:], first_values[...])


def heads(kernel, outs, name, after, latents, w3, *more):
    depth = latents.shape[1]
    scratch = [pltpu.VMEM((MEM, depth), BF16), pltpu.VMEM((depth, COLS), BF16)]
    if more:
        scratch += [pltpu.VMEM((PART, COLS), BF16), pltpu.VMEM((2 * PART, COLS), BF16)]
    return call_on_hbm(
        kernel,
        outs,
        name,
        2 * MEM * depth * COLS,
        3300000,
        (after, latents, w3, *more),
        scratch + [pltpu.SemaphoreType.DMA((4,))],
    )


def query_kernel(after, lat, w, out, rows, part, sems):
    copies = [
        pltpu.make_async_copy(w.at[0], part, sems.at[0]),
        pltpu.make_async_copy(lat.at[pl.ds(0, MEM)], rows.at[pl.ds(0, MEM)], sems.at[1]),
        pltpu.make_async_copy(lat.at[pl.ds(MEM, MEM)], rows.at[pl.ds(MEM, MEM)], sems.at[2]),
    ]
    for copy in copies:
        copy.start()
    copies[0].wait()
    for r in range(2):
        copies[1 + r].wait()
        at = slice(r * MEM, (r + 1) * MEM)
        out[at] = normed(jnp.dot(rows[at], part[...], preferred_element_type=F32))


def query(after, latents, w3):
    depth = latents.shape[1]
    return call_on_hbm(
        query_kernel,
        shape((ROWS, COLS), BF16),
        "query_projection",
        2 * ROWS * depth * COLS,
        4600000,
        (after, latents, w3),
        [pltpu.VMEM((ROWS, depth), BF16), pltpu.VMEM((depth, COLS), BF16), pltpu.SemaphoreType.DMA((3,))],
    )


def vmem_call(kernel, outs, name, flops, args, smem=0, scratch=()):
    specs = [pl.BlockSpec(memory_space=pltpu.SMEM)] * smem
    specs += [pl.BlockSpec(memory_space=pltpu.VMEM)] * (len(args) - smem)
    single = not isinstance(outs, tuple)
    out_spec = pl.BlockSpec(memory_space=pltpu.VMEM)
    nbytes = sum(a.size * a.dtype.itemsize for a in args)
    return pl.pallas_call(
        kernel,
        out_shape=outs,
        in_specs=specs,
        out_specs=out_spec if single else tuple(out_spec for _ in outs),
        scratch_shapes=list(scratch),
        cost_estimate=pl.CostEstimate(flops=flops, bytes_accessed=nbytes, transcendentals=0),
        compiler_params=pltpu.CompilerParams(vmem_limit_bytes=LIMIT),
        name=name,
    )(*args)


def coefficients(rate):
    return 1.0 - rate, jnp.sqrt(1.0 - rate * rate)


def pack(out, state, row):
    out[: 2 * PART] = state.astype(BF16)
    out[2 * PART :] = pieces_of(row)


def keep(out, state, row):
    out[: 2 * PART] = state
    out[2 * PART :] = jnp.broadcast_to(row, (8, COLS))


def plane_step(keys, values, rate, tail_keys, tail_values):
    for_keys, for_values = coefficients(rate)
    return (
        rate * keys + for_keys * tail_keys.astype(F32),
        rate * values + for_values * tail_values.astype(F32),
    )


def plane_kernel(arrived, state, payload):
    keys = values = jnp.zeros((PART, COLS), F32)
    total = jnp.ones((1, COLS), F32)
    for i in range(PARTS):
        rate = row_of(arrived[i, 2 * PART :])
        keys, values = plane_step(keys, values, rate, arrived[i, :PART], arrived[i, PART : 2 * PART])
        total = total * rate
    both = jnp.concatenate([keys, values], axis=0)
    keep(state, both, total)
    pack(payload, both, total)


def joined(upper, mine, rate, got):
    other, other_rate = got[: 2 * PART].astype(F32), row_of(got[2 * PART :])
    return jnp.where(upper, mine + rate * other, other + other_rate * mine), rate * other_rate


def first_kernel(z, own, got_1, payload):
    total, rate = joined((z[0] & 1) == 1, own[: 2 * PART], own[2 * PART : 2 * PART + 1], got_1)
    pack(payload, total, rate)


def next_kernel(z, own, got_1, got_2, payload):
    total, rate = joined((z[0] & 1) == 1, own[: 2 * PART], own[2 * PART : 2 * PART + 1], got_1)
    total, rate = joined((z[0] & 2) == 2, total, rate, got_2)
    payload[...] = total.astype(BF16)


def memory_kernel(z, got_1, got_2, got_4, arrived, out):
    at_1, at_2, at_4 = (z[0] & 1) == 1, (z[0] & 2) == 2, (z[0] & 4) == 4
    entering = jnp.where(at_1, got_1[: 2 * PART].astype(F32), 0.0)
    rate = jnp.where(at_1, row_of(got_1[2 * PART :]), 1.0)
    entering = jnp.where(at_2, entering + rate * got_2[: 2 * PART].astype(F32), entering)
    rate = jnp.where(at_2, rate * row_of(got_2[2 * PART :]), rate)
    entering = jnp.where(at_4, entering + rate * got_4[...].astype(F32), entering)
    keys, values = entering[:PART], entering[PART:]
    for i in range(PARTS):
        out[i, :PART] = keys.astype(BF16)
        out[i, PART:] = values.astype(BF16)
        if i < PARTS - 1:
            rate = row_of(arrived[i, 2 * PART :])
            keys, values = plane_step(keys, values, rate, arrived[i, :PART], arrived[i, PART : 2 * PART])


def attend_kernel(
    r, phase, opened, q, head_keys, head_values, tail_rows, halo, rows_in, columns_in, memory_in,
    out, top, bottom, qx, kx, vx, tail, frame_row, frame_column, memory, sems,
):
    half = ROWS // 2
    base = r * half
    low, high = base, base + half + WIN
    first, second = pl.ds(0, PART), pl.ds(PART, PART)
    seen = pl.ds(low, high - low)
    used = 1 if r == 0 else PARTS
    pairs = [
        (q.at[pl.ds(base, half)], qx.at[pl.ds(HALF_WIN + base, half)]),
        (memory_in, memory),
        (tail_rows.at[pl.ds(0, used)], tail.at[pl.ds(0, used)]),
        (rows_in, frame_row),
        (columns_in.at[seen], frame_column.at[seen]),
    ]
    if r == 0:
        edge, head, source = pl.ds(0, HALF_WIN), pl.ds(HALF_WIN, MEM), pl.ds(0, MEM)
    else:
        edge, head, source = pl.ds(HALF_WIN + ROWS, HALF_WIN), pl.ds(low, HALF_WIN), pl.ds(MEM - HALF_WIN, HALF_WIN)
    pairs += [
        (head_keys.at[source], kx.at[head]),
        (head_values.at[source], vx.at[head]),
        (halo.at[first], kx.at[edge]),
        (halo.at[second], vx.at[edge]),
    ]
    copies = [pltpu.make_async_copy(a, b, sems.at[i]) for i, (a, b) in enumerate(pairs)]
    for copy in copies:
        copy.start()
    blank = jnp.zeros((HALF_WIN, COLS), BF16)
    qx[low : low + HALF_WIN] = blank
    qx[high - HALF_WIN : high] = blank
    start = phase[0] * (ROWS // WIN)
    window = (lax.broadcasted_iota(jnp.int32, (half, HD), 0) + base + HALF_WIN) // WIN
    is_open = jnp.zeros((half, HD), F32)
    for w in range(low // WIN, high // WIN):
        flag = jnp.where(opened[0, start + w] == 1, 1.0, 0.0)
        is_open = jnp.where(window == w, flag, is_open)
    ones = jnp.ones((MEM, HD), BF16)
    copies[0].wait()
    copies[1].wait()
    for h in range(HEADS):
        c = slice(h * HD, (h + 1) * HD)
        keys = memory[:, :PART, c].reshape(MEM, HD)
        values = memory[:, PART:, c].reshape(MEM, HD)
        own = qx[HALF_WIN + base : HALF_WIN + base + half, c]
        score = lax.dot_general(own, keys, (((1,), (1,)), ((), ())), preferred_element_type=F32)
        weight = jnp.exp2(score * SCALE2).astype(BF16)
        result = jnp.dot(weight, jnp.concatenate([values, ones], axis=1), preferred_element_type=F32)
        top[:, c] = is_open * result[:, :HD]
        bottom[:, c] = is_open * result[:, HD:]
    for copy in copies[2:]:
        copy.wait()
    for d in range(used):
        at = HALF_WIN + MEM + d * PART
        kx[at : at + PART] = tail[d, :PART]
        vx[at : at + PART] = tail[d, PART : 2 * PART]
    for begin, size in ((low, half), (low + half, WIN)):
        rows = slice(begin, begin + size)
        window_a = lax.broadcasted_iota(jnp.int32, (size, size), 0) // WIN
        window_b = lax.broadcasted_iota(jnp.int32, (size, size), 1) // WIN
        allowed = (window_a == window_b) & (frame_row[:, rows] <= frame_column[rows, :1])
        begin_own, end_own = max(begin, low + HALF_WIN), min(begin + size, high - HALF_WIN)
        to = slice(begin_own - HALF_WIN - base, end_own - HALF_WIN - base)
        for h in range(HEADS):
            c = slice(h * HD, (h + 1) * HD)
            score = lax.dot_general(qx[rows, c], kx[rows, c], (((1,), (1,)), ((), ())), preferred_element_type=F32)
            weight = jnp.where(allowed, jnp.exp2(score * SCALE2), 0.0).astype(BF16)
            both = jnp.concatenate([vx[rows, c], jnp.ones((size, HD), BF16)], axis=1)
            cut = jnp.dot(weight, both, preferred_element_type=F32)[begin_own - begin : end_own - begin]
            above, below = top[to, c] + cut[:, :HD], bottom[to, c] + cut[:, HD:]
            out[to, c] = (above / below).astype(BF16)


def attention(r, phase, opened, *operands):
    smem = pl.BlockSpec(memory_space=pltpu.SMEM)
    hbm = pl.BlockSpec(memory_space=pl.ANY)
    half = ROWS // 2
    extended = pltpu.VMEM((EXT, COLS), BF16)
    return pl.pallas_call(
        functools.partial(attend_kernel, r),
        out_shape=shape((half, COLS), BF16),
        in_specs=[smem, smem] + [hbm] * len(operands),
        out_specs=pl.BlockSpec(memory_space=pltpu.VMEM),
        scratch_shapes=[
            pltpu.VMEM((half, COLS), F32),
            pltpu.VMEM((half, COLS), F32),
            extended,
            extended,
            extended,
            pltpu.VMEM((PARTS, PAYLOAD, COLS), BF16),
            pltpu.VMEM((1, EXT), jnp.int32),
            pltpu.VMEM((EXT, HD), jnp.int32),
            pltpu.VMEM((PARTS, 2 * PART, COLS), BF16),
            pltpu.SemaphoreType.DMA((9,)),
        ],
        cost_estimate=pl.CostEstimate(
            flops=2 * ROWS * (MEM + half) * COLS * 2, bytes_accessed=1500000, transcendentals=0
        ),
        compiler_params=pltpu.CompilerParams(vmem_limit_bytes=ATTEND_LIMIT),
        name=f"attention_{r}",
    )(phase, opened, *operands)


def near_kernel(r, lat, own, right, left, w_own, w_right, w_left, total):
    rows = total.shape[0]
    sums = lat[r * rows : (r + 1) * rows].astype(F32)
    for a, w in ((own, w_own), (right, w_right), (left, w_left)):
        sums = sums + jnp.dot(a[...], w[...], preferred_element_type=F32)
    total[...] = sums


def far_kernel(total_0, total_1, first, second, w, out):
    half = ROWS // 2
    for r, (total, part) in enumerate(((total_0, first), (total_1, second))):
        at = slice(r * half, (r + 1) * half)
        out[at] = (total[...] + jnp.dot(part[...], w[...], preferred_element_type=F32)).astype(BF16)


def moved(x, axis, by):
    size = lax.axis_size(axis)
    return lax.ppermute(x, axis, [(i, (i + by) % size) for i in range(size)])


def swapped(x, axis, bit):
    return lax.ppermute(x, axis, [(i, i ^ bit) for i in range(lax.axis_size(axis))])


def local(latents, w_qkv, w_out, decay, frame_ids, memory_mask):
    phase = lax.axis_index("phase")
    mp = lax.axis_index("mp")
    phase_ref = phase.reshape(1).astype(jnp.int32)
    w3 = jnp.transpose(w_qkv, (1, 0, 2))

    z_ref = lax.axis_index("z").reshape(1).astype(jnp.int32)
    payload = tails(phase_ref, decay[0], latents, w3)
    arrived = lax.all_to_all(payload, PLANE, 0, 0, tiled=True)

    w_out, payload = lax.optimization_barrier((w_out, payload))
    share = w_out.shape[1] // 4
    offsets = (0, 1, -1, 2)
    sends = [lax.dynamic_slice_in_dim(w_out, ((mp + by) & 3) * share, share, 1) for by in offsets]
    weights = [moved(piece, "mp", by) if by else piece for by, piece in zip(offsets, sends)]
    arrived, _ = lax.optimization_barrier((arrived, sends))
    half_keys = shape((MEM, COLS), BF16)

    wide = shape((2 * PART + 8, COLS), F32)
    packed = shape((PAYLOAD, COLS), BF16)
    plain = shape((2 * PART, COLS), BF16)
    plain_all = shape((PARTS, 2 * PART, COLS), BF16)
    own, sent = vmem_call(plane_kernel, (wide, packed), "plane_total", 1000000, (arrived,))
    latents, sent = lax.optimization_barrier((latents, sent))
    got_1 = swapped(sent, "z", 1)
    own_columns = lax.dynamic_slice_in_dim(latents, mp * share, share, 1)
    got_1, own_columns = lax.optimization_barrier((got_1, own_columns))
    sent = vmem_call(first_kernel, packed, "through_1", 100000, (z_ref, own, got_1), smem=1)
    after, sent = lax.optimization_barrier((z_ref, sent))
    got_2 = swapped(sent, "z", 2)
    head_values = heads(head_values_kernel, half_keys, "head_values", after, latents, w3)
    got_2, head_values = lax.optimization_barrier((got_2, head_values))

    sent = vmem_call(next_kernel, plain, "through_3", 100000, (z_ref, own, got_1, got_2), smem=1)
    after, sent = lax.optimization_barrier((phase_ref, sent))
    got_4 = swapped(sent, "z", 7)
    head_keys, edge = heads(
        head_keys_kernel, (half_keys, plain), "head_keys", after, latents, w3, head_values, payload
    )
    got_4, head_keys = lax.optimization_barrier((got_4, head_keys))
    memory = vmem_call(
        memory_kernel, plain_all, "section_memory", 1000000, (z_ref, got_1, got_2, got_4, arrived), smem=1
    )
    after, memory, edge, frame_ids = lax.optimization_barrier((z_ref, memory, edge, frame_ids))
    memory = lax.all_to_all(memory, PLANE, 0, 0, tiled=True)
    halo = swapped(edge, "phase", 1)
    frames_pad = jnp.pad(frame_ids[0], (HALF_WIN, HALF_WIN), constant_values=outside_frame)
    frames = lax.dynamic_slice_in_dim(frames_pad, phase * ROWS, EXT)
    frame_row = frames.reshape(1, EXT)
    frame_column = jnp.broadcast_to(frames[:, None], (EXT, HD))
    queries = query(after, latents, w3)
    memory, weights = lax.optimization_barrier((memory, weights))
    halves = [
        attention(
            r, phase_ref, memory_mask, queries, head_keys, head_values, payload, halo, frame_row, frame_column, memory
        )
        for r in range(2)
    ]
    right = [moved(piece, "mp", 1) for piece in halves]
    left = [moved(piece, "mp", -1) for piece in halves]
    right[1], left[1] = lax.optimization_barrier((right[1], left[1]))
    far_2 = moved(left[1], "mp", -1)
    totals = [None, None]
    for r in (1, 0):
        totals[r] = vmem_call(
            functools.partial(near_kernel, r),
            shape((ROWS // 2, share), F32),
            f"near_projection_{r}",
            3 * ROWS * COLS * share,
            (own_columns, halves[r], right[r], left[r], *weights[:3]),
        )
        if r == 1:
            right[0], totals[1] = lax.optimization_barrier((right[0], totals[1]))
            far_1 = moved(right[0], "mp", 1)
    return vmem_call(
        far_kernel,
        shape((ROWS, share), BF16),
        "far_projection",
        2 * ROWS * COLS * share,
        (*totals, far_1, far_2, weights[3]),
    )


def solution(mesh):
    finer = Mesh(
        mesh.devices.reshape(8, 2, 2, mesh.shape["mp"], mesh.shape["phase"]),
        ("z", "y", "core", "mp", "phase"),
    )
    placed = (
        P((*SPAN, "phase"), None),
        P(None, None, "mp"),
        P("mp", None),
        P(SPAN, None, "mp"),
        P(SPAN, None),
        P(SPAN, None),
    )
    return jax.shard_map(
        local, mesh=finer, in_specs=placed, out_specs=P((*SPAN, "phase"), "mp"), check_vma=False
    )
```
